256 devices in a mesh: rows: 128 (over y, z, x), sub: 2 (over core).
Axes of the slice: x: 4, y: 4, z: 8, core: 2. Of those that a mesh axis runs over, the one named last changes fastest.
Arguments:
- embeddings: bfloat16 [262144, 768], P(('rows', 'sub')), may hold values from -0.21875 to 0.21875
- candidates: int32 [2048, 128], P(('rows', 'sub')), may hold values from 0 to 262143, as said below
- fresh_flags: int32 [2048, 128], P(('rows', 'sub')), may hold values 0 or 1
- current: float32 [262144, 32], P(('rows', 'sub')), may hold values from 1.6 to 2.2
Outputs:
- refined: float32 [262144, 32], P(('rows', 'sub'))
The draws below stay inside these ranges and needn't reach their ends.
Inputs may be any that keep to these rules, and one draw needn't show every extreme that they name: `candidates`: the 8 lists of one device's blocks together name 1024 distinct rows, none owned by that device. Of the 2048 rows of one index of rows, one device's lists name at most 16, and exactly 16 for some such ranges in every device's lists.
All inputs are finite; a program needn't handle non-finite values. No bound on the sum of `fresh_flags` on one device may be relied on, other than what follows from the above.
Results may differ from the reference program's by a relative error of at most 0.0003.
Values may be sent and summed in bfloat16 or wider, within the bound.
A program may use at most 128 MiB of HBM per device.

```python
import jax
import jax.numpy as jnp
from jax import lax

D = 768
K = 32
BLOCK = 128
CAP = 16
ROWS_DEV = 1024
CANDS = 1024
BLOCKS_DEV = 8
CAND = 128
NROWS = 262144
NBLOCKS = 2048
N_ROWS = 128
N_SUB = 2


def draw_candidates(key, part):
    key = jax.random.fold_in(key, 7)
    chip_span = N_SUB * ROWS_DEV
    chip_ids = jnp.arange(N_ROWS, dtype=jnp.int32)
    rank_load = jnp.where(chip_ids < N_ROWS // 4, CAP, jnp.where(chip_ids < N_ROWS // 2, CAP // 2, CAP // 4)).astype(jnp.int32)

    def one_device(device):
        device_key = jax.random.fold_in(key, device)
        key_order, key_rows, key_own, key_shuffle = jax.random.split(device_key, 4)
        my_chip = device // N_SUB
        my_side = device % N_SUB
        order = jax.random.permutation(key_order, N_ROWS)
        load = jnp.zeros((N_ROWS,), jnp.int32).at[order].set(rank_load)
        chip_keys = jax.random.split(key_rows, N_ROWS)
        picks = jax.vmap(lambda each_key: jax.random.permutation(each_key, chip_span)[:CAP])(chip_keys)
        own_pick = (1 - my_side) * ROWS_DEV + jax.random.permutation(key_own, ROWS_DEV)[:CAP]
        picks = jnp.where((chip_ids == my_chip)[:, None], own_pick[None, :], picks)
        row_ids = chip_ids[:, None] * chip_span + picks
        is_live = jnp.arange(CAP, dtype=jnp.int32)[None, :] < load[:, None]
        flat_ids = row_ids.reshape(-1)
        flat_live = is_live.reshape(-1).astype(jnp.int32)
        chosen_pos = jnp.argsort(1 - flat_live, stable=True)[:CANDS]
        chosen = jax.random.permutation(key_shuffle, flat_ids[chosen_pos])
        return chosen.reshape(BLOCKS_DEV, CAND)
    devices = jnp.arange(N_ROWS * N_SUB, dtype=jnp.int32)
    return jax.vmap(one_device)(devices).reshape(NBLOCKS, CAND).astype(jnp.int32)


def with_ends(drawn, rng, low, top_value):
    extent = drawn.shape
    place = [jax.random.randint(jax.random.fold_in(rng, axis), (), 0, extent[axis]) for axis in range(len(extent))]
    drawn = drawn.at[tuple(place)].set(low)
    longest = extent.index(max(extent))
    place[longest] = (place[longest] + 1) % extent[longest]
    return drawn.at[tuple(place)].set(top_value)


def steps_of(rng, dims, cuts, low, largest):
    level, own = 1.0, jax.random.fold_in(rng, 6)
    for dim, parts in cuts:
        draws = jnp.exp(jax.random.uniform(jax.random.fold_in(own, dim), (parts,), jnp.float32, low / len(cuts), largest / len(cuts)))
        level = level * jnp.repeat(draws, dims[dim] // parts).reshape([-1 if axis == dim else 1 for axis in range(len(dims))])
    return level


def gaussian(own_key, dims, deviation, reach, cuts=(), held_as=jnp.bfloat16):
    array = jax.random.normal(own_key, dims, jnp.float32) * deviation
    if len(cuts) > 0:
        array = steps_of(own_key, dims, cuts, -0.22, 0.18) * array
    return jnp.clip(array, min=-reach, max=reach).astype(held_as)


def setup_inputs(seed: int = 0) -> dict:
    key_list = jax.random.split(jax.random.key(seed), 5)
    embeddings = gaussian(key_list[0], (NROWS, D), D ** -0.5, 0.21875, ((0, 256),))
    candidates = draw_candidates(jax.random.fold_in(key_list[4], 71), 0)
    fresh_flags = with_ends((jax.random.randint(key_list[2], (NBLOCKS, CAND), 0, 2) < 1).astype(jnp.int32), jax.random.fold_in(key_list[2], 1), 0, 1)
    current = jnp.clip(1.6 + 0.6 * jax.random.uniform(key_list[3], (NROWS, K), jnp.float32) ** steps_of(key_list[3], (NROWS, K), ((0, 256),), -0.2, 0.2), 1.6, 2.2)
    return dict(embeddings=embeddings, candidates=candidates, fresh_flags=fresh_flags, current=current)


FAR_VALUE = 1.0e9


def smallest(values, count):
    return -lax.top_k(-values, count)[0]


def reference(embeddings, candidates, fresh_flags, current):
    block_count, cand_count = candidates.shape
    row_count, row_width = embeddings.shape
    norms = jnp.sum(jnp.square(embeddings.astype(jnp.float32)), axis=1)
    own_all = embeddings.reshape(block_count, BLOCK, row_width)
    own_norms = norms.reshape(block_count, BLOCK)
    diagonal_mask = jnp.eye(cand_count, dtype=jnp.bool_)

    def join_block(packed):
        own_rows, own_norm, cand_ids, flags = packed
        cand_rows = jnp.take(embeddings, cand_ids, axis=0)
        cand_norm = jnp.take(norms, cand_ids, axis=0)
        cross_dot = jnp.dot(own_rows, cand_rows.T, preferred_element_type=jnp.float32)
        forward = own_norm[:, None] + cand_norm[None, :] - 2.0 * cross_dot
        inner_dot = jnp.dot(cand_rows, cand_rows.T, preferred_element_type=jnp.float32)
        among_dist = cand_norm[:, None] + cand_norm[None, :] - 2.0 * inner_dot
        fresh_bool = flags > 0
        keep_pair = (fresh_bool[:, None] | fresh_bool[None, :]) & (~diagonal_mask)
        among_dist = jnp.where(keep_pair, among_dist, FAR_VALUE)
        backward = jnp.concatenate([forward.T, among_dist], axis=1)
        return forward, smallest(backward, K)

    forward, rev_best = lax.map(join_block, (own_all, own_norms, candidates, fresh_flags))
    forward = forward.reshape(row_count, cand_count)
    flat_ids = candidates.reshape(-1).astype(jnp.int32)
    row_keys = jnp.broadcast_to(flat_ids[:, None], (flat_ids.shape[0], K)).reshape(-1)
    sorted_keys, sorted_vals = lax.sort((row_keys, rev_best.reshape(-1)), num_keys=2)
    counts = jax.ops.segment_sum(jnp.ones(flat_ids.shape, jnp.int32), flat_ids, num_segments=row_count) * K
    starts = jnp.cumsum(counts) - counts
    offsets = jnp.arange(K, dtype=jnp.int32)
    take_index = jnp.minimum(starts[:, None] + offsets[None, :], sorted_vals.shape[0] - 1).astype(jnp.int32)
    reverse = jnp.where(offsets[None, :] < counts[:, None], sorted_vals[take_index], FAR_VALUE)
    pool_dist = jnp.concatenate([current, forward, reverse], axis=1)
    return smallest(pool_dist, K)
```

```python
import functools

import jax
import jax.numpy as jnp
from jax import lax
from jax.experimental import pallas as pl
from jax.experimental.pallas import tpu as pltpu
from jax.sharding import PartitionSpec as P

BLOCK = 128
CAP = 16
K = 32
FAR = 1.0e9
F32, BF16, I32 = jnp.float32, jnp.bfloat16, jnp.int32
NT = (((1,), (1,)), ((), ()))
NN = (((1,), (0,)), ((), ()))
PITCH = 40


def dot(a, b, dims):
    return lax.dot_general(a, b, dims, preferred_element_type=F32)


def sort_pairs(n):
    pairs = []
    p = 1
    while p < n:
        k = p
        while k >= 1:
            for j in range(k % p, n - k, 2 * k):
                for i in range(min(k, n - j - k)):
                    if (i + j) // (2 * p) == (i + j + k) // (2 * p):
                        pairs.append((i + j, i + j + k))
            k //= 2
        p *= 2
    return pairs


SORT = sort_pairs(K)


def exchange(v, i, j):
    v[i], v[j] = jnp.minimum(v[i], v[j]), jnp.maximum(v[i], v[j])


def sort_list(values):
    v = list(values)
    for i, j in SORT:
        exchange(v, i, j)
    return v


def merge_low(mins):
    v = list(mins)
    d = K // 2
    while d >= 1:
        for i in range(K):
            if i & d == 0:
                exchange(v, i, i + d)
        d //= 2
    return v


def merge_lists(a, b):
    return merge_low([jnp.minimum(a[i], b[K - 1 - i]) for i in range(K)])


def split2(x):
    hi = x.astype(BF16)
    mid = (x - hi.astype(F32)).astype(BF16)
    return hi, mid


def iota(shape, dim):
    return lax.broadcasted_iota(I32, shape, dim)


def onehot(mask):
    return jnp.where(mask, 1.0, 0.0).astype(BF16)


def layout_kernel(span_bits, c_ref, w_ref, s_ref):
    blocks, n = c_ref.shape
    chips = w_ref.shape[0]
    owners = iota((chips, n), 0)
    before = onehot(iota((n, n), 0) < iota((n, n), 1))
    ranks = iota((CAP, n), 0)
    run = jnp.zeros((chips, 1), F32)
    acc = jnp.zeros((chips, 2 * CAP), F32)
    for b in range(blocks):
        c = c_ref[b : b + 1, :]
        owner = lax.shift_right_logical(c, span_bits)
        row1 = (c & ((1 << span_bits) - 1)) + 1
        mine = owner == owners
        mine_b = onehot(mine)
        pre = dot(mine_b, before, NN) + run
        rank = jnp.sum(jnp.where(mine, pre, 0.0), axis=0, keepdims=True).astype(I32)
        run = run + jnp.sum(jnp.where(mine, 1.0, 0.0), axis=1, keepdims=True)
        s_ref[b : b + 1, :] = owner * CAP + rank
        sel = ranks == rank
        hi = jnp.where(sel, lax.shift_right_logical(row1, 4).astype(F32), 0.0).astype(BF16)
        lo = jnp.where(sel, (row1 & 15).astype(F32), 0.0).astype(BF16)
        acc = acc + dot(mine_b, jnp.concatenate([hi, lo], axis=0), NT)
    w_ref[...] = (acc[:, :CAP] * 16.0 + acc[:, CAP:]).astype(I32) - 1


def layout(candidates, chips, span):
    return pl.pallas_call(
        functools.partial(layout_kernel, span.bit_length() - 1),
        out_shape=(
            jax.ShapeDtypeStruct((chips, CAP), I32),
            jax.ShapeDtypeStruct(candidates.shape, I32),
        ),
        name="layout",
    )(candidates)


def serve_kernel(a_ref, rows_ref, out_ref):
    span = rows_ref.shape[0]
    step = out_ref.shape[0]
    asked = a_ref[0].T
    for c in range(step // 128):
        hit = asked[:, c : c + 1] == iota((128, span), 1)
        out_ref[c * 128 : (c + 1) * 128, :] = dot(onehot(hit), rows_ref[...], NN).astype(BF16)


def serve(asked, rows):
    span, width = rows.shape
    slots = asked.size
    per = 8
    steps = slots // (128 * per)
    return pl.pallas_call(
        serve_kernel,
        grid=(steps,),
        in_specs=[
            pl.BlockSpec((1, per, 128), lambda i: (i, 0, 0)),
            pl.BlockSpec((span, width), lambda i: (0, 0)),
        ],
        out_specs=pl.BlockSpec((128 * per, width), lambda i: (i, 0)),
        out_shape=jax.ShapeDtypeStruct((slots, width), BF16),
        compiler_params=pltpu.CompilerParams(vmem_limit_bytes=40 << 20),
        name="serve",
    )(asked.reshape(steps, per, 128), rows)


def plan_kernel(a_ref, pos_ref, row_ref, start_ref, info_ref, key_ref, lv_ref, col_ref, acc_ref, end_ref):
    rows_dev = start_ref.shape[0]
    nrow = a_ref.shape[0]
    slots = nrow * 128
    a = a_ref[...]
    live = (a >= 0) & (a < rows_dev)
    sid = iota((nrow, 128), 0) * 128 + iota((nrow, 128), 1)
    key = jnp.where(live, a * slots + sid, (1 << 30) + sid)
    key_ref[...] = key
    lv_ref[...] = jnp.where(live, a, rows_dev)
    for h in range(nrow // 8):
        col_ref[:, h * 8 : (h + 1) * 8] = key[h * 8 : (h + 1) * 8, :].T
    acc_ref[...] = jnp.zeros_like(acc_ref)
    lane = iota((128, nrow), 1)

    def outer(c, carry):
        col = jnp.sum(jnp.where(lane == c, col_ref[...], 0), axis=1, keepdims=True)
        colb = jnp.broadcast_to(col, (128, 128))

        def inner(e, carry):
            less = jnp.where(colb < key_ref[pl.ds(e, 1), :], 1.0, 0.0)
            part = jnp.sum(less.reshape(16, 8, 128), axis=0)
            at = pl.ds(pl.multiple_of(e * 8, 8), 8)
            acc_ref[at, :] = acc_ref[at, :] + part
            return carry

        return lax.fori_loop(0, nrow, inner, carry)

    lax.fori_loop(0, nrow, outer, 0)
    for e in range(nrow):
        pos_ref[e : e + 1, :] = jnp.sum(acc_ref[e * 8 : (e + 1) * 8, :], axis=0, keepdims=True).astype(I32)

    def start_of(g, most):
        v = g * 128 + iota((128, 128), 0)
        low = jnp.zeros((128, 128), F32)
        own = jnp.zeros((128, 128), F32)
        for e in range(nrow):
            lv = lv_ref[e : e + 1, :]
            low = low + jnp.where(lv < v, 1.0, 0.0)
            own = own + jnp.where(lv == v, 1.0, 0.0)
        start = jnp.sum(low, axis=1, keepdims=True)
        count = jnp.sum(own, axis=1, keepdims=True)
        at = pl.ds(pl.multiple_of(g * 128, 128), 128)
        end_ref[at, :] = jnp.broadcast_to((start + count).astype(I32), (128, 128))
        start_ref[at, :] = jnp.broadcast_to(jnp.where(count > 0, start, -1.0).astype(I32), (128, 128))
        return jnp.maximum(most, jnp.max(count))

    most = lax.fori_loop(0, rows_dev // 128, start_of, jnp.float32(0))
    total = jnp.sum(jnp.where(live, 1.0, 0.0)).astype(I32)
    info_ref[0] = total
    info_ref[1] = most.astype(I32)
    row_ref[...] = jnp.full(row_ref.shape, rows_dev, I32)

    def row_of(c, carry):
        p = c * 128 + iota((8, 128), 1)
        acc = jnp.zeros((8, 128), F32)
        for g in range(rows_dev // 8):
            acc = acc + jnp.where(end_ref[g * 8 : (g + 1) * 8, :] <= p, 1.0, 0.0)
        row = jnp.sum(acc, axis=0, keepdims=True).astype(I32)
        row_ref[pl.ds(c, 1), :] = jnp.where(p[0:1, :] < total, row, rows_dev)
        return carry

    lax.fori_loop(0, nrow, row_of, 0)


def plan(asked_rows, rows_dev):
    nrow = asked_rows.shape[0]
    return pl.pallas_call(
        plan_kernel,
        out_shape=(
            jax.ShapeDtypeStruct((nrow, 128), I32),
            jax.ShapeDtypeStruct((PITCH, 128), I32),
            jax.ShapeDtypeStruct((rows_dev, 128), I32),
            jax.ShapeDtypeStruct((2,), I32),
        ),
        out_specs=(
            pl.BlockSpec(memory_space=pltpu.VMEM),
            pl.BlockSpec(memory_space=pltpu.VMEM),
            pl.BlockSpec(memory_space=pltpu.VMEM),
            pl.BlockSpec(memory_space=pltpu.SMEM),
        ),
        scratch_shapes=[
            pltpu.VMEM((nrow, 128), I32),
            pltpu.VMEM((nrow, 128), I32),
            pltpu.VMEM((128, nrow), I32),
            pltpu.VMEM((nrow * 8, 128), F32),
            pltpu.VMEM((rows_dev, 128), I32),
        ],
        cost_estimate=pl.CostEstimate(flops=20_000_000_000, bytes_accessed=1_000_000, transcendentals=0),
        name="plan",
    )(asked_rows)


def join_kernel(pulled_ref, own_ref, slot_ref, flag_ref, out_ref, fwd_ref, z_ref, f_ref, a_ref, t_ref, hot_ref, pay_ref):
    blocks = slot_ref.shape[0]
    slots = pulled_ref.shape[0]
    slot_cols = slot_ref[...].T
    flags = flag_ref[...]
    flag_cols = flags.T
    ids = iota((128, slots), 1)
    r2, c2 = iota((256, 256), 0), iota((256, 256), 1)
    eye = r2 == c2
    off_diag = iota((128, 128), 0) != iota((128, 128), 1)
    for b in range(blocks):
        at = slice(b * 128, (b + 1) * 128)
        pick = onehot(slot_cols[:, b : b + 1] == ids)
        z_ref[0:128, :] = own_ref[at, :]
        z_ref[128:256, :] = dot(pick, pulled_ref[...], NN).astype(BF16)
        z = z_ref[...]
        gram = dot(z, z, NT)
        diag = jnp.where(eye, gram, 0.0)
        n_col = jnp.sum(diag, axis=1, keepdims=True)
        n_row = jnp.sum(diag, axis=0, keepdims=True)
        dist = n_col + n_row - 2.0 * gram
        f_ref[at, :] = dist[0:128, 128:256]
        fwd_ref[at, :] = dist[128:256, 0:128]
        fresh = (flag_cols[:, b : b + 1] + flags[b : b + 1, :]) > 0
        a_ref[at, :] = jnp.where(fresh & off_diag, dist[128:256, 128:256], FAR)

    def take(ref, g):
        return [ref[pl.ds(g * K + t, 8, stride=128), :] for t in range(K)]

    best = sort_list(take(f_ref, 0))

    def more(ref, lo, best):
        def body(g, best):
            return tuple(merge_lists(list(best), sort_list(take(ref, g))))

        return lax.fori_loop(lo, 128 // K, body, tuple(best))

    best = more(f_ref, 1, best)
    best = more(a_ref, 0, best)
    for k in range(K):
        t_ref[k * 8 : (k + 1) * 8, :] = best[k]
    quad = lax.shift_right_logical(iota((128, 128), 0), 5)
    groups = iota((slots // 4, 128), 0)
    for b in range(blocks):
        at = slice(b * 128, (b + 1) * 128)
        slot = slot_ref[b : b + 1, :]
        mine = t_ref[pl.ds(b, K, stride=8), :]
        tiled = jnp.concatenate([mine] * 4, axis=0)
        hi, mid = split2(jnp.where((slot & 3) == quad, tiled, 0.0))
        pay_ref[0:128, at] = hi
        pay_ref[128:256, at] = mid
        hot_ref[:, at] = onehot(lax.shift_right_logical(slot, 2) == groups)
    both = dot(hot_ref[...], pay_ref[...], NT)
    out_ref[...] = both[:, 0:128] + both[:, 128:256]


def join(pulled, own, slots, flags):
    n = pulled.shape[0]
    rows, width = own.shape
    return pl.pallas_call(
        join_kernel,
        out_shape=(
            jax.ShapeDtypeStruct((n // 4, 128), F32),
            jax.ShapeDtypeStruct((rows, 128), F32),
        ),
        scratch_shapes=[
            pltpu.VMEM((256, width), BF16),
            pltpu.VMEM((rows, 128), F32),
            pltpu.VMEM((rows, 128), F32),
            pltpu.VMEM((K * 8, 128), F32),
            pltpu.VMEM((n // 4, rows), BF16),
            pltpu.VMEM((256, rows), BF16),
        ],
        compiler_params=pltpu.CompilerParams(vmem_limit_bytes=40 << 20),
        name="join",
    )(pulled, own, slots, flags)


def near_kernel(fwd_ref, cur_ref, out_ref, s_ref):
    blocks = cur_ref.shape[0] // 128
    for b in range(blocks):
        s_ref[b * K : (b + 1) * K, :] = cur_ref[b * 128 : (b + 1) * 128, :].T
    best = sort_list([s_ref[pl.ds(k, 8, stride=K), :] for k in range(K)])

    def body(g, best):
        more = [fwd_ref[pl.ds(g * K + t, 8, stride=128), :] for t in range(K)]
        return tuple(merge_lists(list(best), sort_list(more)))

    best = lax.fori_loop(0, 128 // K, body, tuple(best))
    for k in range(K):
        out_ref[k * 8 : (k + 1) * 8, :] = best[k]


def near(fwd, current):
    return pl.pallas_call(
        near_kernel,
        out_shape=jax.ShapeDtypeStruct((K * 8, 128), F32),
        scratch_shapes=[pltpu.VMEM((current.shape[0] // 128 * K, 128), F32)],
        cost_estimate=pl.CostEstimate(flops=8_000_000_000, bytes_accessed=1_000_000, transcendentals=0),
        name="near",
    )(fwd, current)


def merge_kernel(mine_ref, his_ref, pos_ref, row_ref, start_ref, info_ref, near_ref, out_ref, pay_ref, s_ref, x_ref, acc_ref):
    half = mine_ref.shape[0]
    rows_dev = out_ref.shape[0]
    lanes = iota((half, 128), 1)
    total = info_ref[0]
    most = info_ref[1]
    for h, ref in enumerate((mine_ref, his_ref)):
        vals = ref[...]
        for q in range(4):
            at = slice((q * 2 + h) * half, (q * 2 + h + 1) * half)
            hi, mid = split2(jnp.where(lax.shift_right_logical(lanes, 5) == q, vals, 0.0))
            pay_ref[at, 0:128] = hi
            pay_ref[at, 128:256] = mid
    s_ref[...] = jnp.full(s_ref.shape, FAR, F32)
    chunks = (total + 127) // 128
    width = pay_ref.shape[0]

    def gather(c, carry):
        p = c * 128 + iota((128, width), 0)
        got = dot(onehot(pos_ref[...] == p), pay_ref[...], NN)
        turned = (got[:, 0:128] + got[:, 128:256]).T
        vals = turned[0:32] + turned[32:64] + turned[64:96] + turned[96:128]
        s_ref[pl.ds(c, K, stride=PITCH), :] = vals
        return carry

    lax.fori_loop(0, chunks, gather, 0)
    lane = iota((8, 128), 1)
    groups = (total + 1023) // 1024

    def ahead(ref, at, s):
        here = ref[pl.ds(at, 8), :]
        after = ref[pl.ds(at + 1, 8), :]
        return after if s == 128 else pltpu.roll(jnp.where(lane >= s, here, after), 128 - s, 1)

    for e in range(8):

        @pl.when(most > 1 << e)
        def _():
            def step(g, carry):
                at = pl.multiple_of(g * 8, 8)
                same = row_ref[pl.ds(at, 8), :] == ahead(row_ref, at, 1 << e)
                mins = []
                for k in range(K):
                    later = ahead(s_ref, (K - 1 - k) * PITCH + at, 1 << e)
                    mins.append(jnp.minimum(s_ref[pl.ds(k * PITCH + at, 8), :], jnp.where(same, later, FAR)))
                best = merge_low(mins)
                for k in range(K):
                    s_ref[pl.ds(k * PITCH + at, 8), :] = best[k]
                return carry

            lax.fori_loop(0, groups, step, 0)

    acc_ref[...] = jnp.zeros_like(acc_ref)

    def expand(c, carry):
        vals = s_ref[pl.ds(c, K, stride=PITCH), :]
        live = c * 128 + iota((K, 128), 1) < total
        hi, mid = split2(jnp.where(live, vals, 0.0))
        p = c * 128 + iota((rows_dev, 128), 1)
        hot = onehot(start_ref[...] == p)
        ones = jnp.ones((K // 2, 128), BF16)
        acc_ref[...] = acc_ref[...] + dot(jnp.concatenate([hi, mid, ones], axis=0), hot, NT)
        return carry

    lax.fori_loop(0, chunks, expand, 0)
    for b in range(rows_dev // 128):
        at = slice(b * 128, (b + 1) * 128)
        named = acc_ref[2 * K : 2 * K + 1, at] > 0.5
        x_ref[b * K : (b + 1) * K, :] = jnp.where(named, acc_ref[0:K, at] + acc_ref[K : 2 * K, at], FAR)
    have = near_ref[...]
    got = [x_ref[pl.ds(k, 8, stride=K), :] for k in range(K)]
    mins = [
        jnp.minimum(have[k * 8 : (k + 1) * 8, :], got[K - 1 - k])
        for k in range(K)
    ]
    best = merge_low(mins)
    for k in range(K):
        x_ref[k * 8 : (k + 1) * 8, :] = best[k]
    for b in range(rows_dev // 128):
        out_ref[b * 128 : (b + 1) * 128, :] = x_ref[pl.ds(b, K, stride=8), :].T


def merge(mine, his, pos, row, start, info, best):
    rows_dev = start.shape[0]
    vmem = pl.BlockSpec(memory_space=pltpu.VMEM)
    return pl.pallas_call(
        merge_kernel,
        in_specs=[vmem] * 5 + [pl.BlockSpec(memory_space=pltpu.SMEM), vmem],
        out_specs=vmem,
        out_shape=jax.ShapeDtypeStruct((rows_dev, K), F32),
        scratch_shapes=[
            pltpu.VMEM((pos.shape[1], 256), BF16),
            pltpu.VMEM((K * PITCH, 128), F32),
            pltpu.VMEM((rows_dev // 128 * K, 128), F32),
            pltpu.VMEM((2 * K + K // 2, rows_dev), F32),
        ],
        compiler_params=pltpu.CompilerParams(vmem_limit_bytes=40 << 20),
        name="merge",
    )(mine, his, pos, row, start, info, best)


def per_device(embeddings, candidates, fresh_flags, current):
    rows_dev = embeddings.shape[0]
    chips = lax.axis_size("rows")
    sides = lax.axis_size("sub")
    swap = [(i, i ^ 1) for i in range(sides)]
    span = sides * rows_dev
    total = chips * CAP
    wanted, slots = layout(candidates, chips, span)
    chip_rows = lax.all_gather(embeddings, "sub", axis=0, tiled=True)
    asked = lax.all_to_all(wanted, "rows", split_axis=0, concat_axis=0, tiled=True)
    served = serve(asked.reshape(total // 128, 128), chip_rows)
    pulled = lax.all_to_all(
        served.reshape(chips, CAP, -1), "rows", split_axis=0, concat_axis=0, tiled=True
    ).reshape(total, -1)
    his_asked = lax.ppermute(asked, "sub", swap)
    here = jnp.stack([asked, his_asked]) - lax.axis_index("sub") * rows_dev
    here = here.reshape(2, chips, CAP // 4, 4).transpose(3, 0, 1, 2).reshape(-1, 128)
    pos, row, start, info = plan(here, rows_dev)
    outgoing, fwd = join(pulled, embeddings, slots, fresh_flags)
    returned = lax.all_to_all(
        outgoing.reshape(chips, CAP // 4, 128), "rows", split_axis=0, concat_axis=0, tiled=True
    ).reshape(total // 4, 128)
    best = near(fwd, current)
    his = lax.ppermute(returned, "sub", swap)
    return merge(returned, his, pos.reshape(1, -1), row, start, info, best)


def solution(mesh):
    spec = P(("rows", "sub"), None)
    return jax.shard_map(
        per_device, mesh=mesh, in_specs=(spec,) * 4, out_specs=spec, check_vma=False
    )
```

```python
import functools

import jax
import jax.numpy as jnp
from jax import lax
from jax.experimental import pallas as pl
from jax.experimental.pallas import tpu as pltpu
from jax.sharding import PartitionSpec as P

BLOCK = 128
CAP = 16
K = 32
FAR = 1.0e9
F32, BF16, I32 = jnp.float32, jnp.bfloat16, jnp.int32
NT = (((1,), (1,)), ((), ()))
NN = (((1,), (0,)), ((), ()))
PITCH = 40
NY, NZ, NX = 4, 8, 4
PLANE = NY * NX
FAR_FIRST = (4, 3, 5, 2, 6, 1, 7, 0)
MESH = pl.DeviceIdType.MESH


def dot(a, b, dims):
    return lax.dot_general(a, b, dims, preferred_element_type=F32)


def sort_pairs(n):
    pairs = []
    p = 1
    while p < n:
        k = p
        while k >= 1:
            for j in range(k % p, n - k, 2 * k):
                for i in range(min(k, n - j - k)):
                    if (i + j) // (2 * p) == (i + j + k) // (2 * p):
                        pairs.append((i + j, i + j + k))
            k //= 2
        p *= 2
    return pairs


SORT = sort_pairs(K)


def exchange(v, i, j):
    v[i], v[j] = jnp.minimum(v[i], v[j]), jnp.maximum(v[i], v[j])


def sort_list(values):
    v = list(values)
    for i, j in SORT:
        exchange(v, i, j)
    return v


def merge_low(mins):
    v = list(mins)
    d = K // 2
    while d >= 1:
        for i in range(K):
            if i & d == 0:
                exchange(v, i, i + d)
        d //= 2
    return v


def merge_lists(a, b):
    return merge_low([jnp.minimum(a[i], b[K - 1 - i]) for i in range(K)])


def split2(x):
    hi = x.astype(BF16)
    mid = (x - hi.astype(F32)).astype(BF16)
    return hi, mid


def iota(shape, dim):
    return lax.broadcasted_iota(I32, shape, dim)


def onehot(mask):
    return jnp.where(mask, 1.0, 0.0).astype(BF16)


def place():
    chip = lax.axis_index("rows")
    return lax.div(chip, NZ * NX), lax.rem(lax.div(chip, NX), NZ), lax.rem(chip, NX), lax.axis_index("sub")


def chip_at(y, z, x):
    return (lax.rem(y, NY) * NZ + lax.rem(z, NZ)) * NX + lax.rem(x, NX)


def column_peers(here):
    y, z, x, side = here
    return [(dz, {"rows": chip_at(y, z + dz, x), "sub": side}) for dz in FAR_FIRST[:-1]]


def plane_peers(here):
    y, z, x, side = here
    return [
        (dy, dx, h, {"rows": chip_at(y + dy, z, x + dx), "sub": lax.rem(side + h, 2)})
        for dy in range(NY)
        for dx in range(NX)
        for h in range(2)
        if dy + dx + h > 0
    ]


def greet(here):
    sem = pltpu.get_barrier_semaphore()
    peers = [p[-1] for p in column_peers(here)] + [p[-1] for p in plane_peers(here)]
    for device in peers:
        pl.semaphore_signal(sem, inc=1, device_id=device, device_id_type=MESH)
    return lambda: pl.semaphore_wait(sem, len(peers))


def remote(src, dst, send, recv, device):
    return pltpu.make_async_remote_copy(
        src_ref=src, dst_ref=dst, send_sem=send, recv_sem=recv, device_id=device, device_id_type=MESH
    )


def far_rank(dz):
    return FAR_FIRST.index(dz % NZ)


def plane_rank(dy, dx):
    return (dy % NY) * NX + dx % NX


def slots_of(c_ref, w_ref, s_ref, span_bits):
    blocks, n = c_ref.shape
    chips = w_ref.shape[0]
    owners = iota((chips, n), 0)
    before = onehot(iota((n, n), 0) < iota((n, n), 1))
    ranks = iota((CAP, n), 0)
    run = jnp.zeros((chips, 1), F32)
    acc = jnp.zeros((chips, 2 * CAP), F32)
    for b in range(blocks):
        c = c_ref[b : b + 1, :]
        chip = lax.shift_right_logical(c, span_bits)
        owner = (chip & 28) * 4 + lax.shift_right_logical(chip, 5) * 4 + (chip & 3)
        row1 = (c & ((1 << span_bits) - 1)) + 1
        mine = owner == owners
        mine_b = onehot(mine)
        pre = dot(mine_b, before, NN) + run
        rank = jnp.sum(jnp.where(mine, pre, 0.0), axis=0, keepdims=True).astype(I32)
        run = run + jnp.sum(jnp.where(mine, 1.0, 0.0), axis=1, keepdims=True)
        s_ref[b : b + 1, :] = owner * CAP + rank
        sel = ranks == rank
        hi = jnp.where(sel, lax.shift_right_logical(row1, 4).astype(F32), 0.0).astype(BF16)
        lo = jnp.where(sel, (row1 & 15).astype(F32), 0.0).astype(BF16)
        acc = acc + dot(mine_b, jnp.concatenate([hi, lo], axis=0), NT)
    wanted = (acc[:, :CAP] * 16.0 + acc[:, CAP:]).astype(I32) - 1
    w_ref[...] = jnp.concatenate([wanted] + [jnp.full((chips, CAP), -1, I32)] * (128 // CAP - 1), axis=1)


def plan_way_back(a, pos_ref, row_ref, start_ref, info_ref, key_ref, lv_ref, col_ref, acc_ref, end_ref):
    rows_dev = start_ref.shape[0]
    nrow = a.shape[0]
    slots = nrow * 128
    live = (a >= 0) & (a < rows_dev)
    sid = iota((nrow, 128), 0) * 128 + iota((nrow, 128), 1)
    key = jnp.where(live, a * slots + sid, (1 << 30) + sid)
    key_ref[...] = key
    lv_ref[...] = jnp.where(live, a, rows_dev)
    for h in range(nrow // 8):
        col_ref[:, h * 8 : (h + 1) * 8] = key[h * 8 : (h + 1) * 8, :].T
    acc_ref[...] = jnp.zeros_like(acc_ref)
    lane = iota((128, nrow), 1)

    def outer(c, carry):
        col = jnp.sum(jnp.where(lane == c, col_ref[...], 0), axis=1, keepdims=True)
        colb = jnp.broadcast_to(col, (128, 128))

        def inner(e, carry):
            less = jnp.where(colb < key_ref[pl.ds(e, 1), :], 1.0, 0.0)
            part = jnp.sum(less.reshape(16, 8, 128), axis=0)
            at = pl.ds(pl.multiple_of(e * 8, 8), 8)
            acc_ref[at, :] = acc_ref[at, :] + part
            return carry

        return lax.fori_loop(0, nrow, inner, carry)

    lax.fori_loop(0, nrow, outer, 0)
    for e in range(nrow):
        pos_ref[e : e + 1, :] = jnp.sum(acc_ref[e * 8 : (e + 1) * 8, :], axis=0, keepdims=True).astype(I32)

    def start_of(g, most):
        v = g * 128 + iota((128, 128), 0)
        low = jnp.zeros((128, 128), F32)
        own = jnp.zeros((128, 128), F32)
        for e in range(nrow):
            lv = lv_ref[e : e + 1, :]
            low = low + jnp.where(lv < v, 1.0, 0.0)
            own = own + jnp.where(lv == v, 1.0, 0.0)
        start = jnp.sum(low, axis=1, keepdims=True)
        count = jnp.sum(own, axis=1, keepdims=True)
        at = pl.ds(pl.multiple_of(g * 128, 128), 128)
        end_ref[at, :] = jnp.broadcast_to((start + count).astype(I32), (128, 128))
        start_ref[at, :] = jnp.broadcast_to(jnp.where(count > 0, start, -1.0).astype(I32), (128, 128))
        return jnp.maximum(most, count)

    most = lax.fori_loop(0, rows_dev // 128, start_of, jnp.zeros((128, 1), F32))
    total = jnp.sum(jnp.where(live, 1.0, 0.0), axis=(0, 1), keepdims=True).astype(I32)
    most = jnp.max(most, axis=0, keepdims=True).astype(I32)
    info_ref[...] = jnp.where(iota((8, 128), 1) == 0, total, most)
    row_ref[...] = jnp.full(row_ref.shape, rows_dev, I32)

    def row_of(c, carry):
        p = c * 128 + iota((8, 128), 1)
        acc = jnp.zeros((8, 128), F32)
        for g in range(rows_dev // 8):
            acc = acc + jnp.where(end_ref[g * 8 : (g + 1) * 8, :] <= p, 1.0, 0.0)
        row = jnp.sum(acc, axis=0, keepdims=True).astype(I32)
        row_ref[pl.ds(c, 1), :] = jnp.where(p[0:1, :] < total, row, rows_dev)
        return carry

    lax.fori_loop(0, nrow, row_of, 0)


def pull_kernel(
    c_ref, emb_ref,
    pulled_ref, slot_ref, pos_ref, row_ref, start_ref, info_ref,
    rows_ref, served_ref, w_ref, d_ref, e_ref, fin_ref,
    key_ref, lv_ref, col_ref, acc_ref, end_ref,
    keep_sem, half_send, half_recv, col_send, col_recv, plane_send, plane_recv, out_send, out_recv, own_sem,
):
    here = place()
    y, z, x, side = here
    rows_dev = emb_ref.shape[0]
    span = rows_ref.shape[0]
    chips = pulled_ref.shape[0]
    wait_for_peers = greet(here)
    my_half = rows_ref.at[pl.ds(pl.multiple_of(side * rows_dev, rows_dev), rows_dev)]
    keep = pltpu.make_async_copy(emb_ref, my_half, keep_sem)
    keep.start()
    slots_of(c_ref, w_ref, slot_ref, span.bit_length() - 1)
    wait_for_peers()
    half = remote(emb_ref, my_half, half_send, half_recv, {"rows": chip_at(y, z, x), "sub": 1 - side})
    half.start()

    copies = []
    for dz, device in column_peers(here):
        src = w_ref.at[pl.ds(pl.multiple_of(lax.rem(z + dz, NZ) * PLANE, PLANE), PLANE)]
        dst = d_ref.at[pl.ds(far_rank(-dz) * PLANE, PLANE)]
        copies.append(remote(src, dst, col_send.at[dz], col_recv.at[dz], device))
        copies[-1].start()
    own = pl.ds(pl.multiple_of(z * PLANE, PLANE), PLANE)
    d_ref[far_rank(0) * PLANE : (far_rank(0) + 1) * PLANE, :] = w_ref[own, :]
    for copy in copies:
        copy.wait()
    copies = []
    for dy, dx, h, device in plane_peers(here):
        i = plane_rank(dy, dx)
        if h == 0 or i == 0:
            cell = lax.rem(y + dy, NY) * NX + lax.rem(x + dx, NX)
            e_ref[i * NZ : (i + 1) * NZ, :] = d_ref[pl.ds(cell, NZ, stride=PLANE), :]
        at = h * chips + plane_rank(-dy, -dx) * NZ
        copies.append(
            remote(
                e_ref.at[pl.ds(i * NZ, NZ)], fin_ref.at[pl.ds(at, NZ)],
                plane_send.at[2 * i + h], plane_recv.at[2 * i + h], device,
            )
        )
        copies[-1].start()
    fin_ref[0:NZ, :] = e_ref[0:NZ, :]
    for copy in copies:
        copy.wait()
    keep.wait()
    half.wait()

    spread = iota((128, 128), 1) == (iota((128, 128), 0) & (CAP - 1))
    ids = iota((128, span), 1)
    me = z * PLANE + y * NX + x

    def serve(t, carry):
        c = lax.rem(t + 1, PLANE)
        asked = fin_ref[pl.ds(pl.multiple_of(c * NZ, NZ), NZ), :]
        wide = jnp.concatenate([jnp.broadcast_to(asked[j : j + 1, :], (CAP, 128)) for j in range(NZ)], axis=0)
        col = jnp.sum(jnp.where(spread, wide, 0), axis=1, keepdims=True)
        got = dot(onehot(col == ids), rows_ref[...], NN).astype(BF16)
        for j in range(NZ):
            served_ref[c * NZ + j] = got[j * CAP : (j + 1) * CAP, :]
        dy, dx = lax.div(c, NX), lax.rem(c, NX)

        def send(j):
            device = {"rows": chip_at(y + dy, z + FAR_FIRST[j], x + dx), "sub": side}
            remote(served_ref.at[c * NZ + j], pulled_ref.at[me], out_send, out_recv, device).start()

        for j in range(NZ - 1):
            send(j)

        @pl.when(c > 0)
        def _():
            send(NZ - 1)

        return carry

    lax.fori_loop(0, PLANE, serve, 0)
    stay = pltpu.make_async_copy(served_ref.at[NZ - 1], pulled_ref.at[me], own_sem)
    stay.start()

    rows = [fin_ref[h * chips : (h + 1) * chips, :].T[0:CAP, :] for h in range(2)]
    plan_way_back(
        jnp.concatenate(rows, axis=0) - side * rows_dev,
        pos_ref, row_ref, start_ref, info_ref, key_ref, lv_ref, col_ref, acc_ref, end_ref,
    )
    stay.wait()
    rest = pl.ds(0, chips - 1)
    pltpu.make_async_copy(served_ref.at[rest], served_ref.at[rest], out_send).wait()
    pltpu.make_async_copy(pulled_ref.at[rest], pulled_ref.at[rest], out_recv).wait()


def pull(candidates, embeddings, chips):
    rows_dev, width = embeddings.shape
    nrow = 2 * CAP
    vmem = pl.BlockSpec(memory_space=pltpu.VMEM)
    anywhere = pl.BlockSpec(memory_space=pl.ANY)
    grid = pltpu.VMEM((chips, 128), I32)
    dma = pltpu.SemaphoreType.DMA
    return pl.pallas_call(
        pull_kernel,
        in_specs=[vmem, anywhere],
        out_specs=[vmem] * 6,
        out_shape=(
            jax.ShapeDtypeStruct((chips, CAP, width), BF16),
            jax.ShapeDtypeStruct(candidates.shape, I32),
            jax.ShapeDtypeStruct((nrow, 128), I32),
            jax.ShapeDtypeStruct((PITCH, 128), I32),
            jax.ShapeDtypeStruct((rows_dev, 128), I32),
            jax.ShapeDtypeStruct((8, 128), I32),
        ),
        scratch_shapes=[
            pltpu.VMEM((2 * rows_dev, width), BF16),
            pltpu.VMEM((chips, CAP, width), BF16),
            grid, grid, grid,
            pltpu.VMEM((2 * chips, 128), I32),
            pltpu.VMEM((nrow, 128), I32),
            pltpu.VMEM((nrow, 128), I32),
            pltpu.VMEM((128, nrow), I32),
            pltpu.VMEM((nrow * 8, 128), F32),
            pltpu.VMEM((rows_dev, 128), I32),
            dma, dma, dma, dma((NZ,)), dma((NZ,)), dma((2 * PLANE,)), dma((2 * PLANE,)), dma, dma, dma,
        ],
        compiler_params=pltpu.CompilerParams(
            collective_id=0, has_side_effects=True, vmem_limit_bytes=40 << 20
        ),
        name="pull",
    )(candidates, embeddings)


def near(fwd_ref, cur_ref, out_ref, s_ref):
    blocks = cur_ref.shape[0] // 128
    for b in range(blocks):
        s_ref[b * K : (b + 1) * K, :] = cur_ref[b * 128 : (b + 1) * 128, :].T
    best = sort_list([s_ref[pl.ds(k, 8, stride=K), :] for k in range(K)])

    def body(g, best):
        more = [fwd_ref[pl.ds(g * K + t, 8, stride=128), :] for t in range(K)]
        return tuple(merge_lists(list(best), sort_list(more)))

    best = lax.fori_loop(0, 128 // K, body, tuple(best))
    for k in range(K):
        out_ref[k * 8 : (k + 1) * 8, :] = best[k]


def join_kernel(
    pulled_ref, own_ref, slot_ref, flag_ref, cur_ref,
    back_ref, near_ref,
    z_ref, f_ref, a_ref, t_ref, hot_ref, pay_ref, fwd_ref, w_ref, d_ref, s_ref,
    col_send, col_recv, plane_send, plane_recv, own_sem,
):
    here = place()
    y, z, x, side = here
    wait_for_peers = greet(here)
    blocks = slot_ref.shape[0]
    slots = pulled_ref.shape[0]
    slot_cols = slot_ref[...].T
    flags = flag_ref[...]
    flag_cols = flags.T
    ids = iota((128, slots), 1)
    r2, c2 = iota((256, 256), 0), iota((256, 256), 1)
    eye = r2 == c2
    off_diag = iota((128, 128), 0) != iota((128, 128), 1)
    for b in range(blocks):
        at = slice(b * 128, (b + 1) * 128)
        pick = onehot(slot_cols[:, b : b + 1] == ids)
        z_ref[0:128, :] = own_ref[at, :]
        z_ref[128:256, :] = dot(pick, pulled_ref[...], NN).astype(BF16)
        both = z_ref[...]
        gram = dot(both, both, NT)
        diag = jnp.where(eye, gram, 0.0)
        n_col = jnp.sum(diag, axis=1, keepdims=True)
        n_row = jnp.sum(diag, axis=0, keepdims=True)
        dist = n_col + n_row - 2.0 * gram
        f_ref[at, :] = dist[0:128, 128:256]
        fwd_ref[at, :] = dist[128:256, 0:128]
        fresh = (flag_cols[:, b : b + 1] + flags[b : b + 1, :]) > 0
        a_ref[at, :] = jnp.where(fresh & off_diag, dist[128:256, 128:256], FAR)

    def take(ref, g):
        return [ref[pl.ds(g * K + t, 8, stride=128), :] for t in range(K)]

    best = sort_list(take(f_ref, 0))

    def more(ref, lo, best):
        def body(g, best):
            return tuple(merge_lists(list(best), sort_list(take(ref, g))))

        return lax.fori_loop(lo, 128 // K, body, tuple(best))

    best = more(f_ref, 1, best)
    best = more(a_ref, 0, best)
    for k in range(K):
        t_ref[k * 8 : (k + 1) * 8, :] = best[k]
    quad = lax.shift_right_logical(iota((128, 128), 0), 5)
    groups = iota((slots // 4, 128), 0)
    for b in range(blocks):
        at = slice(b * 128, (b + 1) * 128)
        slot = slot_ref[b : b + 1, :]
        mine = t_ref[pl.ds(b, K, stride=8), :]
        tiled = jnp.concatenate([mine] * 4, axis=0)
        hi, mid = split2(jnp.where((slot & 3) == quad, tiled, 0.0))
        pay_ref[0:128, at] = hi
        pay_ref[128:256, at] = mid
        hot_ref[:, at] = onehot(lax.shift_right_logical(slot, 2) == groups)
    both = dot(hot_ref[...], pay_ref[...], NT)
    offers = both[:, 0:128] + both[:, 128:256]
    per = CAP // 4
    for n in range(slots // CAP):
        w_ref[n] = offers[n * per : (n + 1) * per, :]
    wait_for_peers()
    copies = []
    for dz, device in column_peers(here):
        src = w_ref.at[pl.ds(lax.rem(z + dz, NZ) * PLANE, PLANE)]
        copies.append(remote(src, d_ref.at[far_rank(-dz)], col_send.at[dz], col_recv.at[dz], device))
        copies[-1].start()
    stay = pltpu.make_async_copy(w_ref.at[pl.ds(z * PLANE, PLANE)], d_ref.at[far_rank(0)], own_sem)
    stay.start()
    near(fwd_ref, cur_ref, near_ref, s_ref)
    stay.wait()
    for copy in copies:
        copy.wait()
    copies = []
    for dy, dx, h, device in plane_peers(here):
        i = plane_rank(dy, dx)
        cell = lax.rem(y + dy, NY) * NX + lax.rem(x + dx, NX)
        dst = back_ref.at[h, plane_rank(-dy, -dx)]
        copies.append(remote(d_ref.at[:, cell], dst, plane_send.at[2 * i + h], plane_recv.at[2 * i + h], device))
        copies[-1].start()
    stay = pltpu.make_async_copy(d_ref.at[:, y * NX + x], back_ref.at[0, 0], own_sem)
    stay.start()
    stay.wait()
    for copy in copies:
        copy.wait()


def join(pulled, own, slots, flags, current):
    n = pulled.shape[0]
    rows, width = own.shape
    vmem = pl.BlockSpec(memory_space=pltpu.VMEM)
    dma = pltpu.SemaphoreType.DMA
    per = CAP // 4
    return pl.pallas_call(
        join_kernel,
        in_specs=[vmem] * 5,
        out_specs=[vmem] * 2,
        out_shape=(
            jax.ShapeDtypeStruct((2, PLANE, NZ, per, 128), F32),
            jax.ShapeDtypeStruct((K * 8, 128), F32),
        ),
        scratch_shapes=[
            pltpu.VMEM((256, width), BF16),
            pltpu.VMEM((rows, 128), F32),
            pltpu.VMEM((rows, 128), F32),
            pltpu.VMEM((K * 8, 128), F32),
            pltpu.VMEM((n // 4, rows), BF16),
            pltpu.VMEM((256, rows), BF16),
            pltpu.VMEM((rows, 128), F32),
            pltpu.VMEM((n // CAP, per, 128), F32),
            pltpu.VMEM((NZ, PLANE, per, 128), F32),
            pltpu.VMEM((rows // 128 * K, 128), F32),
            dma((NZ,)), dma((NZ,)), dma((2 * PLANE,)), dma((2 * PLANE,)), dma,
        ],
        compiler_params=pltpu.CompilerParams(
            collective_id=1, has_side_effects=True, vmem_limit_bytes=40 << 20
        ),
        name="join",
    )(pulled, own, slots, flags, current)


def merge_kernel(back_ref, pos_ref, row_ref, start_ref, info_ref, near_ref, out_ref, pay_ref, s_ref, x_ref, acc_ref):
    rows_dev = out_ref.shape[0]
    group = lax.shift_right_logical(iota((128, 128), 1), 5)
    total = info_ref[0]
    most = info_ref[1]
    for h in range(2):
        for rr in range(CAP // 4):
            vals = back_ref[h, :, rr, :]
            for q in range(4):
                n = (h * CAP + rr * 4 + q) * 128
                hi, mid = split2(jnp.where(group == q, vals, 0.0))
                pay_ref[n : n + 128, 0:128] = hi
                pay_ref[n : n + 128, 128:256] = mid
    s_ref[...] = jnp.full(s_ref.shape, FAR, F32)
    chunks = (total + 127) // 128
    width = pay_ref.shape[0]

    def gather(c, carry):
        p = c * 128 + iota((128, width), 0)
        got = dot(onehot(pos_ref[...] == p), pay_ref[...], NN)
        turned = (got[:, 0:128] + got[:, 128:256]).T
        vals = turned[0:32] + turned[32:64] + turned[64:96] + turned[96:128]
        s_ref[pl.ds(c, K, stride=PITCH), :] = vals
        return carry

    lax.fori_loop(0, chunks, gather, 0)
    lane = iota((8, 128), 1)
    groups = (total + 1023) // 1024

    def ahead(ref, at, s):
        here = ref[pl.ds(at, 8), :]
        after = ref[pl.ds(at + 1, 8), :]
        return after if s == 128 else pltpu.roll(jnp.where(lane >= s, here, after), 128 - s, 1)

    for e in range(8):

        @pl.when(most > 1 << e)
        def _():
            def step(g, carry):
                at = pl.multiple_of(g * 8, 8)
                same = row_ref[pl.ds(at, 8), :] == ahead(row_ref, at, 1 << e)
                mins = []
                for k in range(K):
                    later = ahead(s_ref, (K - 1 - k) * PITCH + at, 1 << e)
                    mins.append(jnp.minimum(s_ref[pl.ds(k * PITCH + at, 8), :], jnp.where(same, later, FAR)))
                best = merge_low(mins)
                for k in range(K):
                    s_ref[pl.ds(k * PITCH + at, 8), :] = best[k]
                return carry

            lax.fori_loop(0, groups, step, 0)

    acc_ref[...] = jnp.zeros_like(acc_ref)

    def expand(c, carry):
        vals = s_ref[pl.ds(c, K, stride=PITCH), :]
        live = c * 128 + iota((K, 128), 1) < total
        hi, mid = split2(jnp.where(live, vals, 0.0))
        p = c * 128 + iota((rows_dev, 128), 1)
        hot = onehot(start_ref[...] == p)
        ones = jnp.ones((K // 2, 128), BF16)
        acc_ref[...] = acc_ref[...] + dot(jnp.concatenate([hi, mid, ones], axis=0), hot, NT)
        return carry

    lax.fori_loop(0, chunks, expand, 0)
    for b in range(rows_dev // 128):
        at = slice(b * 128, (b + 1) * 128)
        named = acc_ref[2 * K : 2 * K + 1, at] > 0.5
        x_ref[b * K : (b + 1) * K, :] = jnp.where(named, acc_ref[0:K, at] + acc_ref[K : 2 * K, at], FAR)
    have = near_ref[...]
    got = [x_ref[pl.ds(k, 8, stride=K), :] for k in range(K)]
    mins = [
        jnp.minimum(have[k * 8 : (k + 1) * 8, :], got[K - 1 - k])
        for k in range(K)
    ]
    best = merge_low(mins)
    for k in range(K):
        x_ref[k * 8 : (k + 1) * 8, :] = best[k]
    for b in range(rows_dev // 128):
        out_ref[b * 128 : (b + 1) * 128, :] = x_ref[pl.ds(b, K, stride=8), :].T


def merge(back, pos, row, start, info, best):
    rows_dev = start.shape[0]
    vmem = pl.BlockSpec(memory_space=pltpu.VMEM)
    return pl.pallas_call(
        merge_kernel,
        in_specs=[vmem] * 4 + [pl.BlockSpec(memory_space=pltpu.SMEM), vmem],
        out_specs=vmem,
        out_shape=jax.ShapeDtypeStruct((rows_dev, K), F32),
        scratch_shapes=[
            pltpu.VMEM((pos.shape[1], 256), BF16),
            pltpu.VMEM((K * PITCH, 128), F32),
            pltpu.VMEM((rows_dev // 128 * K, 128), F32),
            pltpu.VMEM((2 * K + K // 2, rows_dev), F32),
        ],
        compiler_params=pltpu.CompilerParams(vmem_limit_bytes=40 << 20),
        name="merge",
    )(back, pos, row, start, info, best)


def per_device(embeddings, candidates, fresh_flags, current):
    chips = lax.axis_size("rows")
    pulled, slots, pos, row, start, info = pull(candidates, embeddings, chips)
    pulled = pulled.reshape(chips * CAP, -1)
    back, best = join(pulled, embeddings, slots, fresh_flags, current)
    back = back.reshape(2, chips, CAP // 4, 128)
    return merge(back, pos.reshape(1, -1), row, start, info[0, 0:2], best)


def solution(mesh):
    spec = P(("rows", "sub"), None)
    return jax.shard_map(
        per_device, mesh=mesh, in_specs=(spec,) * 4, out_specs=spec, check_vma=False
    )
```

```python
import functools

import jax
import jax.numpy as jnp
from jax import lax
from jax.experimental import pallas as pl
from jax.experimental.pallas import tpu as pltpu
from jax.sharding import PartitionSpec as P

BLOCK = 128
CAP = 16
K = 32
FAR = 1.0e9
F32, BF16, I32 = jnp.float32, jnp.bfloat16, jnp.int32
NT = (((1,), (1,)), ((), ()))
NN = (((1,), (0,)), ((), ()))
PITCH = 40
NY, NZ, NX = 4, 8, 4
PLANE = NY * NX
AWAY = (0, 4, 3, 5, 2, 6, 1, 7)
STEP = 384
READY = 3
SCALE = 28672.0
TOP = 65535.0
MESH = pl.DeviceIdType.MESH


def dot(a, b, dims):
    return lax.dot_general(a, b, dims, preferred_element_type=F32)


def sort_pairs(n):
    pairs = []
    p = 1
    while p < n:
        k = p
        while k >= 1:
            for j in range(k % p, n - k, 2 * k):
                for i in range(min(k, n - j - k)):
                    if (i + j) // (2 * p) == (i + j + k) // (2 * p):
                        pairs.append((i + j, i + j + k))
            k //= 2
        p *= 2
    return pairs


SORT = sort_pairs(K)


def exchange(v, i, j):
    v[i], v[j] = jnp.minimum(v[i], v[j]), jnp.maximum(v[i], v[j])


def sort_list(values):
    v = list(values)
    for i, j in SORT:
        exchange(v, i, j)
    return v


def merge_low(mins):
    v = list(mins)
    d = K // 2
    while d >= 1:
        for i in range(K):
            if i & d == 0:
                exchange(v, i, i + d)
        d //= 2
    return v


def merge_lists(a, b):
    return merge_low([jnp.minimum(a[i], b[K - 1 - i]) for i in range(K)])


def split2(x):
    hi = x.astype(BF16)
    mid = (x - hi.astype(F32)).astype(BF16)
    return hi, mid


def iota(shape, dim):
    return lax.broadcasted_iota(I32, shape, dim)


def onehot(mask):
    return jnp.where(mask, 1.0, 0.0).astype(BF16)


def place():
    chip = lax.axis_index("rows")
    return lax.div(chip, NZ * NX), lax.rem(lax.div(chip, NX), NZ), lax.rem(chip, NX), lax.axis_index("sub")


def chip_at(y, z, x):
    return (lax.rem(y, NY) * NZ + lax.rem(z, NZ)) * NX + lax.rem(x, NX)


def column_peers(here):
    y, z, x, side = here
    return [(dz, {"rows": chip_at(y, z + dz, x), "sub": side}) for dz in AWAY[1:]]


def plane_peers(here):
    y, z, x, side = here
    return [
        (dy, dx, h, {"rows": chip_at(y + dy, z, x + dx), "sub": lax.rem(side + h, 2)})
        for dy in range(NY)
        for dx in range(NX)
        for h in range(2)
        if dy + dx + h > 0
    ]


def greet(here):
    sem = pltpu.get_barrier_semaphore()
    peers = [p[-1] for p in column_peers(here)] + [p[-1] for p in plane_peers(here)]
    for device in peers:
        pl.semaphore_signal(sem, inc=1, device_id=device, device_id_type=MESH)
    return lambda: pl.semaphore_wait(sem, len(peers))


def remote(src, dst, send, recv, device):
    return pltpu.make_async_remote_copy(
        src_ref=src, dst_ref=dst, send_sem=send, recv_sem=recv, device_id=device, device_id_type=MESH
    )


def away(k):
    m = k - 1
    dz = jnp.where(lax.rem(m, 2) == 1, 4 - lax.div(m + 1, 2), 4 + lax.div(m, 2))
    return jnp.where(k == 0, 0, dz)


def far_rank(dz):
    return AWAY.index(dz % NZ)


def plane_rank(dy, dx):
    return (dy % NY) * NX + dx % NX


def slots_of(c_ref, w_ref, s_ref, span_bits):
    blocks, n = c_ref.shape
    chips = w_ref.shape[0]
    owners = iota((chips, n), 0)
    before = onehot(iota((n, n), 0) < iota((n, n), 1))
    ranks = iota((CAP, n), 0)
    run = jnp.zeros((chips, 1), F32)
    acc = jnp.zeros((chips, 2 * CAP), F32)
    for b in range(blocks):
        c = c_ref[b : b + 1, :]
        chip = lax.shift_right_logical(c, span_bits)
        owner = (chip & 28) * 4 + lax.shift_right_logical(chip, 5) * 4 + (chip & 3)
        row1 = (c & ((1 << span_bits) - 1)) + 1
        mine = owner == owners
        mine_b = onehot(mine)
        pre = dot(mine_b, before, NN) + run
        rank = jnp.sum(jnp.where(mine, pre, 0.0), axis=0, keepdims=True).astype(I32)
        run = run + jnp.sum(jnp.where(mine, 1.0, 0.0), axis=1, keepdims=True)
        s_ref[b : b + 1, :] = owner * CAP + rank
        sel = ranks == rank
        hi = jnp.where(sel, lax.shift_right_logical(row1, 4).astype(F32), 0.0).astype(BF16)
        lo = jnp.where(sel, (row1 & 15).astype(F32), 0.0).astype(BF16)
        acc = acc + dot(mine_b, jnp.concatenate([hi, lo], axis=0), NT)
    wanted = (acc[:, :CAP] * 16.0 + acc[:, CAP:]).astype(I32) - 1
    w_ref[...] = jnp.concatenate([wanted] + [jnp.full((chips, CAP), -1, I32)] * (128 // CAP - 1), axis=1)


def plan_way_back(a, pos_ref, row_ref, start_ref, info_ref, key_ref, lv_ref, col_ref, acc_ref, end_ref):
    rows_dev = start_ref.shape[0]
    nrow = a.shape[0]
    slots = nrow * 128
    live = (a >= 0) & (a < rows_dev)
    sid = iota((nrow, 128), 0) * 128 + iota((nrow, 128), 1)
    key = jnp.where(live, a * slots + sid, (1 << 30) + sid)
    key_ref[...] = key
    lv_ref[...] = jnp.where(live, a, rows_dev)
    for h in range(nrow // 8):
        col_ref[:, h * 8 : (h + 1) * 8] = key[h * 8 : (h + 1) * 8, :].T
    acc_ref[...] = jnp.zeros_like(acc_ref)
    lane = iota((128, nrow), 1)

    def outer(c, carry):
        col = jnp.sum(jnp.where(lane == c, col_ref[...], 0), axis=1, keepdims=True)
        colb = jnp.broadcast_to(col, (128, 128))

        def inner(e, carry):
            less = jnp.where(colb < key_ref[pl.ds(e, 1), :], 1.0, 0.0)
            part = jnp.sum(less.reshape(16, 8, 128), axis=0)
            at = pl.ds(pl.multiple_of(e * 8, 8), 8)
            acc_ref[at, :] = acc_ref[at, :] + part
            return carry

        return lax.fori_loop(0, nrow, inner, carry)

    lax.fori_loop(0, nrow, outer, 0)
    for e in range(nrow):
        pos_ref[e : e + 1, :] = jnp.sum(acc_ref[e * 8 : (e + 1) * 8, :], axis=0, keepdims=True).astype(I32)

    def start_of(g, most):
        v = g * 128 + iota((128, 128), 0)
        low = jnp.zeros((128, 128), F32)
        own = jnp.zeros((128, 128), F32)
        for e in range(nrow):
            lv = lv_ref[e : e + 1, :]
            low = low + jnp.where(lv < v, 1.0, 0.0)
            own = own + jnp.where(lv == v, 1.0, 0.0)
        start = jnp.sum(low, axis=1, keepdims=True)
        count = jnp.sum(own, axis=1, keepdims=True)
        at = pl.ds(pl.multiple_of(g * 128, 128), 128)
        end_ref[at, :] = jnp.broadcast_to((start + count).astype(I32), (128, 128))
        start_ref[at, :] = jnp.broadcast_to(jnp.where(count > 0, start, -1.0).astype(I32), (128, 128))
        return jnp.maximum(most, count)

    most = lax.fori_loop(0, rows_dev // 128, start_of, jnp.zeros((128, 1), F32))
    total = jnp.sum(jnp.where(live, 1.0, 0.0), axis=(0, 1), keepdims=True).astype(I32)
    most = jnp.max(most, axis=0, keepdims=True).astype(I32)
    info_ref[...] = jnp.where(iota((8, 128), 0) == 0, total, most).astype(F32)
    row_ref[...] = jnp.full(row_ref.shape, rows_dev, I32)

    def row_of(c, carry):
        p = c * 128 + iota((8, 128), 1)
        acc = jnp.zeros((8, 128), F32)
        for g in range(rows_dev // 8):
            acc = acc + jnp.where(end_ref[g * 8 : (g + 1) * 8, :] <= p, 1.0, 0.0)
        row = jnp.sum(acc, axis=0, keepdims=True).astype(I32)
        row_ref[pl.ds(c, 1), :] = jnp.where(p[0:1, :] < total, row, rows_dev)
        return carry

    lax.fori_loop(0, nrow, row_of, 0)


def near(fwd_ref, cur_ref, out_ref, s_ref):
    for b in range(cur_ref.shape[1] // 128):
        s_ref[b * K : (b + 1) * K, :] = cur_ref[:, b * 128 : (b + 1) * 128]
    best = sort_list([s_ref[pl.ds(k, 8, stride=K), :] for k in range(K)])

    def body(g, best):
        more = [fwd_ref[pl.ds(g * K + t, 8, stride=128), :] for t in range(K)]
        return tuple(merge_lists(list(best), sort_list(more)))

    best = lax.fori_loop(0, 128 // K, body, tuple(best))
    for k in range(K):
        out_ref[k * 8 : (k + 1) * 8, :] = best[k]


def round_kernel(
    cand_hbm, flag_hbm, emb_hbm, cur_hbm,
    back_ref, near_ref, pos_ref, row_ref, info_ref, q_ref, start_ref, hit_ref,
    c_ref, flag_ref, cur_ref, slot_ref,
    rows_ref, served_ref, pulled_ref, w_ref, d_ref, e_ref, fin_ref, ask_ref,
    key_ref, lv_ref, col_ref, acc_ref, end_ref,
    cand_ref, z_ref, f_ref, a_ref, fwd_ref, t_ref, hot_ref, pay_ref, w2_ref, d2_ref, s_ref,
    in_sem, half_send, half_recv, col_send, col_recv, plane_send, plane_recv,
    out_send, out_recv, own_sem, col_send2, col_recv2, plane_send2, plane_recv2,
):
    here = place()
    y, z, x, side = here
    rows_dev = emb_hbm.shape[0]
    span = rows_ref.shape[0]
    chips = pulled_ref.shape[0]
    half_at = pl.multiple_of(side * rows_dev, rows_dev)
    my_half = rows_ref.at[pl.ds(half_at, rows_dev)]
    brought = [
        pltpu.make_async_copy(src, dst, in_sem.at[i])
        for i, (src, dst) in enumerate(
            [(cand_hbm, c_ref), (emb_hbm, my_half), (flag_hbm, flag_ref), (cur_hbm, cur_ref)]
        )
    ]
    for copy in brought:
        copy.start()
    wait_for_peers = greet(here)
    brought[0].wait()
    slots_of(c_ref, w_ref, slot_ref, span.bit_length() - 1)
    wait_for_peers()

    copies = []
    for dz, device in column_peers(here):
        src = w_ref.at[pl.ds(pl.multiple_of(lax.rem(z + dz, NZ) * PLANE, PLANE), PLANE)]
        dst = d_ref.at[pl.ds(far_rank(-dz) * PLANE, PLANE)]
        copies.append(remote(src, dst, col_send.at[dz], col_recv.at[dz], device))
        copies[-1].start()
    half = remote(emb_hbm, my_half, half_send, half_recv, {"rows": chip_at(y, z, x), "sub": 1 - side})
    half.start()
    own = pl.ds(pl.multiple_of(z * PLANE, PLANE), PLANE)
    d_ref[far_rank(0) * PLANE : (far_rank(0) + 1) * PLANE, :] = w_ref[own, :]
    for copy in copies:
        copy.wait()
    copies = []
    for dy, dx, h, device in plane_peers(here):
        i = plane_rank(dy, dx)
        if h == 0 or i == 0:
            cell = lax.rem(y + dy, NY) * NX + lax.rem(x + dx, NX)
            e_ref[i * NZ : (i + 1) * NZ, :] = d_ref[pl.ds(cell, NZ, stride=PLANE), :]
        at = h * chips + plane_rank(-dy, -dx) * NZ
        copies.append(
            remote(
                e_ref.at[pl.ds(i * NZ, NZ)], fin_ref.at[pl.ds(at, NZ)],
                plane_send.at[2 * i + h], plane_recv.at[2 * i + h], device,
            )
        )
        copies[-1].start()
    fin_ref[0:NZ, :] = e_ref[0:NZ, :]
    for copy in copies:
        copy.wait()
    for k in range(NZ):
        ask_ref[k * PLANE : (k + 1) * PLANE, :] = fin_ref[pl.ds(k, PLANE, stride=NZ), :]
    for copy in brought[1:]:
        copy.wait()
    half.wait()

    spread = iota((128, 128), 1) == (iota((128, 128), 0) & (CAP - 1))
    ids = iota((128, span), 1)
    me = z * PLANE + y * NX + x
    part = PLANE // 2

    def serve(t, carry):
        asked = ask_ref[pl.ds(pl.multiple_of(t * part, part), part), :]
        wide = jnp.concatenate([jnp.broadcast_to(asked[j : j + 1, :], (CAP, 128)) for j in range(part)], axis=0)
        col = jnp.sum(jnp.where(spread, wide, 0), axis=1, keepdims=True)
        got = dot(onehot(col == ids), rows_ref[...], NN).astype(BF16)
        for j in range(part):
            served_ref[t * part + j] = got[j * CAP : (j + 1) * CAP, :]
        k = lax.div(t, 2)
        dz = away(k)

        def send(j):
            i = lax.rem(t, 2) * part + j
            device = {"rows": chip_at(y + lax.div(i, NX), z + dz, x + lax.rem(i, NX)), "sub": side}
            remote(served_ref.at[t * part + j], pulled_ref.at[me], out_send, out_recv.at[k], device).start()

        @pl.when(t > 0)
        def _():
            send(0)

        for j in range(1, part):
            send(j)
        return carry

    lax.fori_loop(0, 2 * NZ, serve, 0)
    stay = pltpu.make_async_copy(served_ref.at[0], pulled_ref.at[me], own_sem)
    stay.start()

    turned = [fin_ref[h * chips : (h + 1) * chips, :].T[0:CAP, :] for h in range(2)]
    plan_way_back(
        jnp.concatenate(turned, axis=0) - side * rows_dev,
        pos_ref, row_ref, start_ref, info_ref, key_ref, lv_ref, col_ref, acc_ref, end_ref,
    )

    def ready(t, carry):
        p = iota((128, 128), 0) + t * 128
        for e in range(pos_ref.shape[0]):
            q_ref[pl.ds(pl.multiple_of(t * 128, 128), 128), e * 128 : (e + 1) * 128] = onehot(pos_ref[e : e + 1, :] == p)
        return carry

    lax.fori_loop(0, READY * STEP // 128, ready, 0)
    for t in range(READY):
        for i in range(STEP // 128):
            p = iota((rows_dev, 128), 1) + (t * STEP + i * 128)
            hit_ref[t, :, i * 128 : (i + 1) * 128] = onehot(start_ref[...] == p)

    slot_cols = slot_ref[...].T
    blocks = slot_ref.shape[0]
    size = PLANE * CAP

    def arrived(k, count):
        got = pulled_ref.at[pl.ds(0, count)]
        pltpu.make_async_copy(got, got, out_recv.at[k]).wait()
        return lax.rem(z - away(k) + NZ, NZ)

    def picked(b, plane, rows):
        pick = onehot(slot_cols[:, b : b + 1] - plane * size == iota((128, size), 1))
        return dot(pick, rows, NN)

    def plane_rows(plane):
        return pulled_ref[pl.ds(plane * PLANE, PLANE)].reshape(size, -1)

    stay.wait()
    plane = arrived(0, PLANE - 1)
    rows = plane_rows(plane)
    for b in range(blocks):
        cand_ref[b * 128 : (b + 1) * 128, :] = picked(b, plane, rows)

    def more_rows(k, carry):
        plane = arrived(k, PLANE)
        rows = plane_rows(plane)
        for b in range(blocks):
            at = slice(b * 128, (b + 1) * 128)
            cand_ref[at, :] = cand_ref[at, :] + picked(b, plane, rows)
        return carry

    lax.fori_loop(1, NZ - 1, more_rows, 0)
    plane = arrived(NZ - 1, PLANE)
    rows = plane_rows(plane)

    flags = flag_ref[...]
    flag_cols = flags.T
    eye = iota((256, 256), 0) == iota((256, 256), 1)
    off_diag = iota((128, 128), 0) != iota((128, 128), 1)
    for b in range(blocks):
        at = slice(b * 128, (b + 1) * 128)
        z_ref[0:128, :] = rows_ref[pl.ds(half_at + b * 128, 128), :]
        z_ref[128:256, :] = (cand_ref[at, :] + picked(b, plane, rows)).astype(BF16)
        both = z_ref[...]
        gram = dot(both, both, NT)
        diag = jnp.where(eye, gram, 0.0)
        n_col = jnp.sum(diag, axis=1, keepdims=True)
        n_row = jnp.sum(diag, axis=0, keepdims=True)
        dist = n_col + n_row - 2.0 * gram
        f_ref[at, :] = dist[0:128, 128:256]
        fwd_ref[at, :] = dist[128:256, 0:128]
        fresh = (flag_cols[:, b : b + 1] + flags[b : b + 1, :]) > 0
        a_ref[at, :] = jnp.where(fresh & off_diag, dist[128:256, 128:256], FAR)

    def take(ref, g):
        return [ref[pl.ds(g * K + t, 8, stride=128), :] for t in range(K)]

    best = sort_list(take(f_ref, 0))

    def more(ref, lo, best):
        def body(g, best):
            return tuple(merge_lists(list(best), sort_list(take(ref, g))))

        return lax.fori_loop(lo, 128 // K, body, tuple(best))

    best = more(f_ref, 1, best)
    best = more(a_ref, 0, best)

    for k in range(K):
        t_ref[k * 8 : (k + 1) * 8, :] = jnp.floor(jnp.clip(best[k] * SCALE + 0.5, 0.0, TOP))
    octet = lax.shift_right_logical(iota((128, 128), 0), 4)
    groups = iota((chips * 2, 128), 0)
    for b in range(blocks):
        at = slice(b * 128, (b + 1) * 128)
        slot = slot_ref[b : b + 1, :]
        code = t_ref[pl.ds(b, K, stride=8), :]
        hi = jnp.floor(code * (1.0 / 256.0))
        lo = code - hi * 256.0
        mine = (slot & 7) == octet
        for i, piece in enumerate((hi[:16], lo[:16], hi[16:], lo[16:])):
            pay_ref[i * 128 : (i + 1) * 128, at] = jnp.where(mine, jnp.concatenate([piece] * 8, axis=0), 0.0).astype(BF16)
        hot_ref[:, at] = onehot(lax.shift_right_logical(slot, 3) == groups)
    sums = dot(hot_ref[...], pay_ref[...], NT)
    low = (sums[:, 0:128] * 256.0 + sums[:, 128:256]).astype(I32)
    high = (sums[:, 256:384] * 256.0 + sums[:, 384:512]).astype(I32)
    words = low + lax.shift_left(high, 16)
    for n in range(chips):
        w2_ref[n] = words[2 * n : 2 * n + 2, :]
    copies = []
    for dz, device in column_peers(here):
        src = w2_ref.at[pl.ds(lax.rem(z + dz, NZ) * PLANE, PLANE)]
        copies.append(remote(src, d2_ref.at[far_rank(-dz)], col_send2.at[dz], col_recv2.at[dz], device))
        copies[-1].start()
    stay = pltpu.make_async_copy(w2_ref.at[pl.ds(z * PLANE, PLANE)], d2_ref.at[far_rank(0)], own_sem)
    stay.start()
    near(fwd_ref, cur_ref, near_ref, s_ref)
    stay.wait()
    for copy in copies:
        copy.wait()
    copies = []
    for dy, dx, h, device in plane_peers(here):
        i = plane_rank(dy, dx)
        cell = lax.rem(y + dy, NY) * NX + lax.rem(x + dx, NX)
        dst = back_ref.at[h, plane_rank(-dy, -dx)]
        copies.append(remote(d2_ref.at[:, cell], dst, plane_send2.at[2 * i + h], plane_recv2.at[2 * i + h], device))
        copies[-1].start()
    stay = pltpu.make_async_copy(d2_ref.at[:, y * NX + x], back_ref.at[0, 0], own_sem)
    stay.start()
    stay.wait()
    for copy in copies:
        copy.wait()
    sent = served_ref.at[pl.ds(0, chips - 1)]
    pltpu.make_async_copy(sent, sent, out_send).wait()


def one_round(candidates, flags, embeddings, current, chips):
    rows_dev, width = embeddings.shape
    nrow = 2 * CAP
    vmem = pl.BlockSpec(memory_space=pltpu.VMEM)
    hbm = pl.BlockSpec(memory_space=pltpu.HBM)
    grid = pltpu.VMEM((chips, 128), I32)
    block = pltpu.VMEM((rows_dev, 128), F32)
    dma = pltpu.SemaphoreType.DMA
    return pl.pallas_call(
        round_kernel,
        in_specs=[hbm] * 4,
        out_specs=[vmem] * 8,
        out_shape=(
            jax.ShapeDtypeStruct((2, PLANE, NZ, 2, 128), I32),
            jax.ShapeDtypeStruct((K * 8, 128), F32),
            jax.ShapeDtypeStruct((nrow, 128), I32),
            jax.ShapeDtypeStruct((PITCH, 128), I32),
            jax.ShapeDtypeStruct((8, 128), F32),
            jax.ShapeDtypeStruct((READY * STEP, nrow * 128), BF16),
            jax.ShapeDtypeStruct((rows_dev, 128), I32),
            jax.ShapeDtypeStruct((READY, rows_dev, STEP), BF16),
        ),
        scratch_shapes=[
            pltpu.VMEM(candidates.shape, I32),
            pltpu.VMEM(candidates.shape, I32),
            pltpu.VMEM(current.shape, F32),
            pltpu.VMEM(candidates.shape, I32),
            pltpu.VMEM((2 * rows_dev, width), BF16),
            pltpu.VMEM((chips, CAP, width), BF16),
            pltpu.VMEM((chips, CAP, width), BF16),
            grid, grid, grid,
            pltpu.VMEM((2 * chips, 128), I32),
            grid,
            pltpu.VMEM((nrow, 128), I32),
            pltpu.VMEM((nrow, 128), I32),
            pltpu.VMEM((128, nrow), I32),
            pltpu.VMEM((nrow * 8, 128), F32),
            pltpu.VMEM((rows_dev, 128), I32),
            pltpu.VMEM((rows_dev, width), F32),
            pltpu.VMEM((256, width), BF16),
            block, block, block,
            pltpu.VMEM((K * 8, 128), F32),
            pltpu.VMEM((chips * 2, rows_dev), BF16),
            pltpu.VMEM((512, rows_dev), BF16),
            pltpu.VMEM((chips, 2, 128), I32),
            pltpu.VMEM((NZ, PLANE, 2, 128), I32),
            pltpu.VMEM((rows_dev // 128 * K, 128), F32),
            dma((4,)), dma, dma, dma((NZ,)), dma((NZ,)), dma((2 * PLANE,)), dma((2 * PLANE,)),
            dma, dma((NZ,)), dma, dma((NZ,)), dma((NZ,)), dma((2 * PLANE,)), dma((2 * PLANE,)),
        ],
        compiler_params=pltpu.CompilerParams(
            collective_id=0, has_side_effects=True, vmem_limit_bytes=34 << 20
        ),
        name="one_round",
    )(*[pltpu.with_memory_space_constraint(v, pltpu.HBM) for v in (candidates, flags, embeddings, current)])


def merge_kernel(
    back_ref, near_ref, pos_ref, row_ref, info_ref, q_ref, start_ref, hit_ref,
    out_ref, pay_ref, s_ref, x_ref, acc_ref, hot_ref,
):
    rows_dev = out_ref.shape[1]
    chips = back_ref.shape[1]
    lanes = iota((chips, 128), 1)
    group = lax.shift_right_logical(lanes, 5)
    first = (lanes & 16) == 0
    total = jnp.max(info_ref[0:1, :]).astype(I32)
    most = jnp.max(info_ref[1:2, :]).astype(I32)
    for h in range(2):
        for rr in range(2):
            words = back_ref[h, :, rr, :]
            low = (words & 65535).astype(F32)
            high = lax.shift_right_logical(words, 16).astype(F32)
            even = jnp.where(first, low, pltpu.roll(high, 16, 1))
            odd = jnp.where(first, pltpu.roll(low, 112, 1), high)
            for q in range(8):
                n = (h * CAP + rr * 8 + q) * chips
                hi, mid = split2(jnp.where(group == q // 2, odd if q & 1 else even, 0.0))
                pay_ref[n : n + chips, 0:128] = hi
                pay_ref[n : n + chips, 128:256] = mid
    steps = (total + STEP - 1) // STEP
    width = pay_ref.shape[0]

    def place_rows(t, hot):
        got = dot(hot, pay_ref[...], NN)
        for i in range(STEP // 128):
            at = slice(i * 128, (i + 1) * 128)
            turned = (got[at, 0:128] + got[at, 128:256]).T
            vals = turned[0:32] + turned[32:64] + turned[64:96] + turned[96:128]
            s_ref[pl.ds(t * (STEP // 128) + i, K, stride=PITCH), :] = vals

    def gather(t, carry):
        place_rows(t, q_ref[pl.ds(pl.multiple_of(t * STEP, STEP), STEP), :])
        return carry

    def gather_more(t, carry):
        place_rows(t, onehot(pos_ref[...] == t * STEP + iota((STEP, width), 0)))
        return carry

    lax.fori_loop(0, jnp.minimum(steps, READY), gather, 0)
    lax.fori_loop(READY, steps, gather_more, 0)
    lane = iota((8, 128), 1)
    groups = (total + 1023) // 1024

    def ahead(ref, at, s):
        here = ref[pl.ds(at, 8), :]
        after = ref[pl.ds(at + 1, 8), :]
        return after if s == 128 else pltpu.roll(jnp.where(lane >= s, here, after), 128 - s, 1)

    for e in range(8):

        @pl.when(most > 1 << e)
        def _():
            def step(g, carry):
                at = pl.multiple_of(g * 8, 8)
                same = row_ref[pl.ds(at, 8), :] == ahead(row_ref, at, 1 << e)
                mins = []
                for k in range(K):
                    later = ahead(s_ref, (K - 1 - k) * PITCH + at, 1 << e)
                    mins.append(jnp.minimum(s_ref[pl.ds(k * PITCH + at, 8), :], jnp.where(same, later, FAR)))
                best = merge_low(mins)
                for k in range(K):
                    s_ref[pl.ds(k * PITCH + at, 8), :] = best[k]
                return carry

            lax.fori_loop(0, groups, step, 0)

    acc_ref[...] = jnp.zeros_like(acc_ref)

    def expand_by(t, hot):
        cells = [s_ref[pl.ds(t * (STEP // 128) + i, K, stride=PITCH), :] for i in range(STEP // 128)]
        vals = jnp.concatenate(cells, axis=1)
        live = t * STEP + iota((K, STEP), 1) < total
        hi, mid = split2(jnp.where(live, vals, 0.0))
        ones = jnp.ones((K // 2, STEP), BF16)
        acc_ref[...] = acc_ref[...] + dot(jnp.concatenate([hi, mid, ones], axis=0), hot, NT)

    def expand(t, carry):
        expand_by(t, hit_ref[t])
        return carry

    def expand_more(t, carry):
        for i in range(STEP // 128):
            at = slice(i * 128, (i + 1) * 128)
            p = t * STEP + i * 128 + iota((rows_dev, 128), 1)
            hot_ref[:, at] = onehot(start_ref[...] == p)
        expand_by(t, hot_ref[...])
        return carry

    lax.fori_loop(0, jnp.minimum(steps, READY), expand, 0)
    lax.fori_loop(READY, steps, expand_more, 0)
    for b in range(rows_dev // 128):
        at = slice(b * 128, (b + 1) * 128)
        named = acc_ref[2 * K : 2 * K + 1, at] > 0.5
        x_ref[b * K : (b + 1) * K, :] = jnp.where(
            named, (acc_ref[0:K, at] + acc_ref[K : 2 * K, at]) * (1.0 / SCALE), FAR
        )
    have = near_ref[...]
    got = [x_ref[pl.ds(k, 8, stride=K), :] for k in range(K)]
    mins = [
        jnp.minimum(have[k * 8 : (k + 1) * 8, :], got[K - 1 - k])
        for k in range(K)
    ]
    best = merge_low(mins)
    for k in range(K):
        x_ref[k * 8 : (k + 1) * 8, :] = best[k]
    for b in range(rows_dev // 128):
        out_ref[:, b * 128 : (b + 1) * 128] = x_ref[pl.ds(b, K, stride=8), :]


def merge(back, best, pos, row, info, q, start, hit):
    rows_dev = start.shape[0]
    vmem = pl.BlockSpec(memory_space=pltpu.VMEM)
    return pl.pallas_call(
        merge_kernel,
        in_specs=[vmem] * 8,
        out_specs=vmem,
        out_shape=jax.ShapeDtypeStruct((K, rows_dev), F32),
        scratch_shapes=[
            pltpu.VMEM((pos.shape[1], 256), BF16),
            pltpu.VMEM((K * PITCH, 128), F32),
            pltpu.VMEM((rows_dev // 128 * K, 128), F32),
            pltpu.VMEM((2 * K + K // 2, rows_dev), F32),
            pltpu.VMEM((rows_dev, STEP), BF16),
        ],
        compiler_params=pltpu.CompilerParams(vmem_limit_bytes=20 << 20),
        name="merge",
    )(back, best, pos, row, info, q, start, hit)


def per_device(embeddings, candidates, fresh_flags, current):
    chips = lax.axis_size("rows")
    back, best, pos, row, info, q, start, hit = one_round(
        candidates, fresh_flags, embeddings, current.T, chips
    )
    back = back.reshape(2, chips, 2, 128)
    return merge(back, best, pos.reshape(1, -1), row, info, q, start, hit).T


def solution(mesh):
    spec = P(("rows", "sub"), None)
    return jax.shard_map(
        per_device, mesh=mesh, in_specs=(spec,) * 4, out_specs=spec, check_vma=False
    )
```

```python
import functools

import jax
import jax.numpy as jnp
from jax import lax
from jax.experimental import pallas as pl
from jax.experimental.pallas import tpu as pltpu
from jax.sharding import PartitionSpec as P

BLOCK = 128
CAP = 16
K = 32
FAR = 1.0e9
F32, BF16, I32 = jnp.float32, jnp.bfloat16, jnp.int32
NT = (((1,), (1,)), ((), ()))
NN = (((1,), (0,)), ((), ()))
PITCH = 40
NY, NZ, NX = 4, 8, 4
PLANE = NY * NX
AWAY = (0, 4, 3, 5, 2, 6, 1, 7)
STEP = 384
READY = 3
SCALE = 28672.0
TOP = 65535.0
MESH = pl.DeviceIdType.MESH


def dot(a, b, dims):
    return lax.dot_general(a, b, dims, preferred_element_type=F32)


def sort_pairs(n):
    pairs = []
    p = 1
    while p < n:
        k = p
        while k >= 1:
            for j in range(k % p, n - k, 2 * k):
                for i in range(min(k, n - j - k)):
                    if (i + j) // (2 * p) == (i + j + k) // (2 * p):
                        pairs.append((i + j, i + j + k))
            k //= 2
        p *= 2
    return pairs


SORT = sort_pairs(K)


def exchange(v, i, j):
    v[i], v[j] = jnp.minimum(v[i], v[j]), jnp.maximum(v[i], v[j])


def sort_list(values):
    v = list(values)
    for i, j in SORT:
        exchange(v, i, j)
    return v


def merge_low(mins):
    v = list(mins)
    d = K // 2
    while d >= 1:
        for i in range(K):
            if i & d == 0:
                exchange(v, i, i + d)
        d //= 2
    return v


def merge_lists(a, b):
    return merge_low([jnp.minimum(a[i], b[K - 1 - i]) for i in range(K)])


def split2(x):
    hi = x.astype(BF16)
    mid = (x - hi.astype(F32)).astype(BF16)
    return hi, mid


def iota(shape, dim):
    return lax.broadcasted_iota(I32, shape, dim)


def onehot(mask):
    return jnp.where(mask, 1.0, 0.0).astype(BF16)


def place():
    chip = lax.axis_index("rows")
    return lax.div(chip, NZ * NX), lax.rem(lax.div(chip, NX), NZ), lax.rem(chip, NX), lax.axis_index("sub")


def wrap(v, n):
    return jnp.where(v >= n, v - n, v)


def chip_at(y, z, x):
    return (wrap(y, NY) * NZ + wrap(z, NZ)) * NX + wrap(x, NX)


def column_peers(here):
    y, z, x, side = here
    return [(dz, {"rows": chip_at(y, z + dz, x), "sub": side}) for dz in AWAY[1:]]


def plane_peers(here, cores=2):
    y, z, x, side = here
    return [
        (dy, dx, h, {"rows": chip_at(y + dy, z, x + dx), "sub": 1 - side if h else side})
        for dy in range(NY)
        for dx in range(NX)
        for h in range(cores)
        if dy + dx + h > 0
    ]


def greet(here):
    y, z, x, side = here
    sem = pltpu.get_barrier_semaphore()
    peers = [p[-1] for p in column_peers(here)] + [p[-1] for p in plane_peers(here, 1)]
    peers.append({"rows": chip_at(y, z, x), "sub": 1 - side})
    for device in peers:
        pl.semaphore_signal(sem, inc=1, device_id=device, device_id_type=MESH)
    return lambda: pl.semaphore_wait(sem, len(peers))


def drain(ref, sem):
    pltpu.make_async_copy(ref, ref, sem).wait()


def remote(src, dst, send, recv, device):
    return pltpu.make_async_remote_copy(
        src_ref=src, dst_ref=dst, send_sem=send, recv_sem=recv, device_id=device, device_id_type=MESH
    )


def far_rank(dz):
    return AWAY.index(dz % NZ)


def plane_rank(dy, dx):
    return (dy % NY) * NX + dx % NX


def slots_of(c_ref, w_ref, s_ref, span_bits):
    blocks, n = c_ref.shape
    chips = w_ref.shape[0]
    owners = iota((chips, n), 0)
    before = onehot(iota((n, n), 0) < iota((n, n), 1))
    ranks = iota((CAP, n), 0)
    run = jnp.zeros((chips, 1), F32)
    acc = jnp.zeros((chips, 2 * CAP), F32)
    for b in range(blocks):
        c = c_ref[b : b + 1, :]
        chip = lax.shift_right_logical(c, span_bits)
        owner = (chip & 28) * 4 + lax.shift_right_logical(chip, 5) * 4 + (chip & 3)
        row1 = (c & ((1 << span_bits) - 1)) + 1
        mine = owner == owners
        mine_b = onehot(mine)
        pre = dot(mine_b, before, NN) + run
        rank = jnp.sum(jnp.where(mine, pre, 0.0), axis=0, keepdims=True).astype(I32)
        run = run + jnp.sum(jnp.where(mine, 1.0, 0.0), axis=1, keepdims=True)
        s_ref[b : b + 1, :] = owner * CAP + rank
        sel = ranks == rank
        hi = jnp.where(sel, lax.shift_right_logical(row1, 4).astype(F32), 0.0).astype(BF16)
        lo = jnp.where(sel, (row1 & 15).astype(F32), 0.0).astype(BF16)
        acc = acc + dot(mine_b, jnp.concatenate([hi, lo], axis=0), NT)
    wanted = (acc[:, :CAP] * 16.0 + acc[:, CAP:]).astype(I32) - 1
    w_ref[...] = jnp.concatenate([wanted] + [jnp.full((chips, CAP), -1, I32)] * (128 // CAP - 1), axis=1)


def plan_way_back(a, pos_ref, row_ref, start_ref, info_ref, key_ref, lv_ref, col_ref, acc_ref, end_ref):
    rows_dev = start_ref.shape[0]
    nrow = a.shape[0]
    slots = nrow * 128
    live = (a >= 0) & (a < rows_dev)
    sid = iota((nrow, 128), 0) * 128 + iota((nrow, 128), 1)
    key = jnp.where(live, a * slots + sid, (1 << 30) + sid)
    key_ref[...] = key
    lv_ref[...] = jnp.where(live, a, rows_dev)
    for h in range(nrow // 8):
        col_ref[:, h * 8 : (h + 1) * 8] = key[h * 8 : (h + 1) * 8, :].T
    acc_ref[...] = jnp.zeros_like(acc_ref)
    lane = iota((128, nrow), 1)

    def outer(c, carry):
        col = jnp.sum(jnp.where(lane == c, col_ref[...], 0), axis=1, keepdims=True)
        colb = jnp.broadcast_to(col, (128, 128))

        def inner(e, carry):
            less = jnp.where(colb < key_ref[pl.ds(e, 1), :], 1.0, 0.0)
            part = jnp.sum(less.reshape(16, 8, 128), axis=0)
            at = pl.ds(pl.multiple_of(e * 8, 8), 8)
            acc_ref[at, :] = acc_ref[at, :] + part
            return carry

        return lax.fori_loop(0, nrow, inner, carry)

    lax.fori_loop(0, nrow, outer, 0)
    for e in range(nrow):
        pos_ref[e : e + 1, :] = jnp.sum(acc_ref[e * 8 : (e + 1) * 8, :], axis=0, keepdims=True).astype(I32)

    def start_of(g, most):
        v = g * 128 + iota((128, 128), 0)
        low = jnp.zeros((128, 128), F32)
        own = jnp.zeros((128, 128), F32)
        for e in range(nrow):
            lv = lv_ref[e : e + 1, :]
            low = low + jnp.where(lv < v, 1.0, 0.0)
            own = own + jnp.where(lv == v, 1.0, 0.0)
        start = jnp.sum(low, axis=1, keepdims=True)
        count = jnp.sum(own, axis=1, keepdims=True)
        at = pl.ds(pl.multiple_of(g * 128, 128), 128)
        end_ref[at, :] = jnp.broadcast_to((start + count).astype(I32), (128, 128))
        start_ref[at, :] = jnp.broadcast_to(jnp.where(count > 0, start, -1.0).astype(I32), (128, 128))
        return jnp.maximum(most, count)

    most = lax.fori_loop(0, rows_dev // 128, start_of, jnp.zeros((128, 1), F32))
    total = jnp.sum(jnp.where(live, 1.0, 0.0), axis=(0, 1), keepdims=True).astype(I32)
    most = jnp.max(most, axis=0, keepdims=True).astype(I32)
    info_ref[...] = jnp.where(iota((8, 128), 0) == 0, total, most).astype(F32)
    row_ref[...] = jnp.full(row_ref.shape, rows_dev, I32)

    def row_of(c, carry):
        p = c * 128 + iota((8, 128), 1)
        acc = jnp.zeros((8, 128), F32)
        for g in range(rows_dev // 8):
            acc = acc + jnp.where(end_ref[g * 8 : (g + 1) * 8, :] <= p, 1.0, 0.0)
        row = jnp.sum(acc, axis=0, keepdims=True).astype(I32)
        row_ref[pl.ds(c, 1), :] = jnp.where(p[0:1, :] < total, row, rows_dev)
        return carry

    lax.fori_loop(0, nrow, row_of, 0)


def near(fwd_ref, cur_ref, out_ref, s_ref):
    for b in range(cur_ref.shape[1] // 128):
        s_ref[b * K : (b + 1) * K, :] = cur_ref[:, b * 128 : (b + 1) * 128]
    best = sort_list([s_ref[pl.ds(k, 8, stride=K), :] for k in range(K)])

    def body(g, best):
        more = [fwd_ref[pl.ds(g * K + t, 8, stride=128), :] for t in range(K)]
        return tuple(merge_lists(list(best), sort_list(more)))

    best = lax.fori_loop(0, 128 // K, body, tuple(best))
    for k in range(K):
        out_ref[k * 8 : (k + 1) * 8, :] = best[k]


def round_kernel(
    cand_hbm, flag_hbm, emb_hbm, cur_hbm,
    back_ref, near_ref, pos_ref, row_ref, info_ref, q_ref, start_ref, hit_ref,
    c_ref, flag_ref, cur_ref, slot_ref,
    rows_ref, served_ref, pulled_ref, w_ref, d_ref, e_ref, fin_ref,
    key_ref, lv_ref, col_ref, acc_ref, end_ref,
    cand_ref, z_ref, f_ref, a_ref, fwd_ref, t_ref, hot_ref, pay_ref, w2_ref, d2_ref, s_ref,
    in_sem, half_send, half_recv, col_send, col_recv, plane_send, plane_recv, tell_send, tell_recv,
    out_send, out_recv, own_sem, col_send2, col_recv2, plane_send2, plane_recv2,
):
    here = place()
    y, z, x, side = here
    rows_dev = emb_hbm.shape[0]
    span = rows_ref.shape[0]
    chips = pulled_ref.shape[0]
    half_at = pl.multiple_of(side * rows_dev, rows_dev)
    my_half = rows_ref.at[pl.ds(half_at, rows_dev)]
    brought = [
        pltpu.make_async_copy(src, dst, in_sem.at[i])
        for i, (src, dst) in enumerate(
            [(cand_hbm, c_ref), (emb_hbm, my_half), (flag_hbm, flag_ref), (cur_hbm, cur_ref)]
        )
    ]
    for copy in brought:
        copy.start()
    wait_for_peers = greet(here)
    brought[0].wait()
    slots_of(c_ref, w_ref, slot_ref, span.bit_length() - 1)
    wait_for_peers()

    for dz, device in column_peers(here):
        src = w_ref.at[pl.ds(pl.multiple_of(wrap(z + dz, NZ) * PLANE, PLANE), PLANE)]
        dst = d_ref.at[pl.ds(far_rank(-dz) * PLANE, PLANE)]
        remote(src, dst, col_send, col_recv, device).start()
    other = {"rows": chip_at(y, z, x), "sub": 1 - side}
    half = remote(emb_hbm, my_half, half_send, half_recv, other)
    half.start()
    own = pl.ds(pl.multiple_of(z * PLANE, PLANE), PLANE)
    d_ref[far_rank(0) * PLANE : (far_rank(0) + 1) * PLANE, :] = w_ref[own, :]
    column = pl.ds(0, (NZ - 1) * PLANE)
    drain(d_ref.at[column], col_recv)
    for dy, dx, _, device in plane_peers(here, 1):
        i = plane_rank(dy, dx)
        cell = wrap(y + dy, NY) * NX + wrap(x + dx, NX)
        e_ref[i * NZ : (i + 1) * NZ, :] = d_ref[pl.ds(cell, NZ, stride=PLANE), :]
        dst = fin_ref.at[pl.ds(plane_rank(-dy, -dx) * NZ, NZ)]
        remote(e_ref.at[pl.ds(i * NZ, NZ)], dst, plane_send, plane_recv, device).start()
    fin_ref[0:NZ, :] = d_ref[pl.ds(y * NX + x, NZ, stride=PLANE), :]
    plane = pl.ds(0, (PLANE - 1) * NZ)
    for copy in brought[1:]:
        copy.wait()
    half.wait()
    drain(fin_ref.at[plane], plane_recv)
    tell = remote(fin_ref.at[pl.ds(0, chips)], fin_ref.at[pl.ds(chips, chips)], tell_send, tell_recv, other)
    tell.start()

    spread = iota((128, 128), 1) == (iota((128, 128), 0) & (CAP - 1))
    ids = iota((128, span), 1)
    me = (y * NX + x) * NZ + z

    def serve(c, carry):
        asked = fin_ref[pl.ds(pl.multiple_of(c * NZ, NZ), NZ), :]
        wide = jnp.concatenate([jnp.broadcast_to(asked[j : j + 1, :], (CAP, 128)) for j in range(NZ)], axis=0)
        col = jnp.sum(jnp.where(spread, wide, 0), axis=1, keepdims=True)
        got = dot(onehot(col == ids), rows_ref[...], NN).astype(BF16)
        for j in range(NZ):
            served_ref[c * NZ + j] = got[j * CAP : (j + 1) * CAP, :]
        y_to = wrap(y + lax.div(c, NX), NY)
        x_to = wrap(x + lax.rem(c, NX), NX)

        def send(j):
            device = {"rows": (y_to * NZ + wrap(z + AWAY[j], NZ)) * NX + x_to, "sub": side}
            remote(served_ref.at[c * NZ + j], pulled_ref.at[me], out_send, out_recv.at[c], device).start()

        @pl.when(c > 0)
        def _():
            send(0)

        for j in range(1, NZ):
            send(j)
        return carry

    lax.fori_loop(0, PLANE, serve, 0)
    stay = pltpu.make_async_copy(served_ref.at[0], pulled_ref.at[me], own_sem)
    stay.start()

    tell.wait()
    turned = [fin_ref[h * chips : (h + 1) * chips, :].T[0:CAP, :] for h in range(2)]
    plan_way_back(
        jnp.concatenate(turned, axis=0) - side * rows_dev,
        pos_ref, row_ref, start_ref, info_ref, key_ref, lv_ref, col_ref, acc_ref, end_ref,
    )

    def ready(t, carry):
        p = iota((128, 128), 0) + t * 128
        for e in range(pos_ref.shape[0]):
            q_ref[pl.ds(pl.multiple_of(t * 128, 128), 128), e * 128 : (e + 1) * 128] = onehot(pos_ref[e : e + 1, :] == p)
        return carry

    lax.fori_loop(0, READY * STEP // 128, ready, 0)
    for t in range(READY):
        for i in range(STEP // 128):
            p = iota((rows_dev, 128), 1) + (t * STEP + i * 128)
            hit_ref[t, :, i * 128 : (i + 1) * 128] = onehot(start_ref[...] == p)

    slots = slot_ref[...]
    column_id = lax.shift_right_logical(slots, 4) & (PLANE - 1)
    in_column = lax.shift_right_logical(slots, 8) * CAP + (slots & (CAP - 1))
    column_cols = column_id.T
    in_cols = in_column.T
    blocks = slot_ref.shape[0]
    size = NZ * CAP
    cells = iota((128, 2 * size), 1)

    def source(c):
        y_from = wrap(y + NY - lax.div(c, NX), NY)
        return y_from * NX + wrap(x + NX - lax.rem(c, NX), NX)

    def arrived(c, count):
        drain(pulled_ref.at[pl.ds(0, count)], out_recv.at[c])

    def column_rows(c):
        return pulled_ref[pl.ds(source(c) * NZ, NZ)].reshape(size, -1)

    def picked(b, c, rows):
        here, there = source(c), source(c + 1)
        col, at = column_cols[:, b : b + 1], in_cols[:, b : b + 1]
        at = jnp.where(col == here, at, jnp.where(col == there, at + size, -1))
        return dot(onehot(at == cells), rows, NN)

    def two_columns(c):
        return jnp.concatenate([column_rows(c), column_rows(c + 1)], axis=0)

    stay.wait()
    arrived(0, NZ - 1)
    arrived(1, NZ)
    rows = two_columns(0)
    for b in range(blocks):
        cand_ref[b * 128 : (b + 1) * 128, :] = picked(b, 0, rows)

    def more_rows(k, carry):
        arrived(2 * k, NZ)
        arrived(2 * k + 1, NZ)
        rows = two_columns(2 * k)
        for b in range(blocks):
            at = slice(b * 128, (b + 1) * 128)
            cand_ref[at, :] = cand_ref[at, :] + picked(b, 2 * k, rows)
        return carry

    lax.fori_loop(1, PLANE // 2 - 1, more_rows, 0)
    last = PLANE - 2
    arrived(last, NZ)
    arrived(last + 1, NZ)
    rows = two_columns(last)

    flags = flag_ref[...]
    flag_cols = flags.T
    eye = iota((256, 256), 0) == iota((256, 256), 1)
    off_diag = iota((128, 128), 0) != iota((128, 128), 1)
    for b in range(blocks):
        at = slice(b * 128, (b + 1) * 128)
        z_ref[0:128, :] = rows_ref[pl.ds(half_at + b * 128, 128), :]
        z_ref[128:256, :] = (cand_ref[at, :] + picked(b, last, rows)).astype(BF16)
        both = z_ref[...]
        gram = dot(both, both, NT)
        diag = jnp.where(eye, gram, 0.0)
        n_col = jnp.sum(diag, axis=1, keepdims=True)
        n_row = jnp.sum(diag, axis=0, keepdims=True)
        dist = n_col + n_row - 2.0 * gram
        f_ref[at, :] = dist[0:128, 128:256]
        fwd_ref[at, :] = dist[128:256, 0:128]
        fresh = (flag_cols[:, b : b + 1] + flags[b : b + 1, :]) > 0
        a_ref[at, :] = jnp.where(fresh & off_diag, dist[128:256, 128:256], FAR)

    def take(ref, g):
        return [ref[pl.ds(g * K + t, 8, stride=128), :] for t in range(K)]

    best = sort_list(take(f_ref, 0))

    def more(ref, lo, best):
        def body(g, best):
            return tuple(merge_lists(list(best), sort_list(take(ref, g))))

        return lax.fori_loop(lo, 128 // K, body, tuple(best))

    best = more(f_ref, 1, best)
    best = more(a_ref, 0, best)

    for k in range(K):
        t_ref[k * 8 : (k + 1) * 8, :] = jnp.floor(jnp.clip(best[k] * SCALE + 0.5, 0.0, TOP))
    octet = lax.shift_right_logical(iota((128, 128), 0), 4)
    groups = iota((chips * 2, 128), 0)
    for b in range(blocks):
        at = slice(b * 128, (b + 1) * 128)
        slot = slot_ref[b : b + 1, :]
        code = t_ref[pl.ds(b, K, stride=8), :]
        hi = jnp.floor(code * (1.0 / 256.0))
        lo = code - hi * 256.0
        mine = (slot & 7) == octet
        for i, piece in enumerate((hi[:16], lo[:16], hi[16:], lo[16:])):
            pay_ref[i * 128 : (i + 1) * 128, at] = jnp.where(mine, jnp.concatenate([piece] * 8, axis=0), 0.0).astype(BF16)
        hot_ref[:, at] = onehot(lax.shift_right_logical(slot, 3) == groups)
    sums = dot(hot_ref[...], pay_ref[...], NT)
    low = (sums[:, 0:128] * 256.0 + sums[:, 128:256]).astype(I32)
    high = (sums[:, 256:384] * 256.0 + sums[:, 384:512]).astype(I32)
    words = low + lax.shift_left(high, 16)
    for n in range(chips):
        w2_ref[n] = words[2 * n : 2 * n + 2, :]
    for dz, device in column_peers(here):
        src = w2_ref.at[pl.ds(wrap(z + dz, NZ) * PLANE, PLANE)]
        remote(src, d2_ref.at[far_rank(-dz)], col_send2, col_recv2, device).start()
    stay = pltpu.make_async_copy(w2_ref.at[pl.ds(z * PLANE, PLANE)], d2_ref.at[far_rank(0)], own_sem)
    stay.start()
    near(fwd_ref, cur_ref, near_ref, s_ref)
    stay.wait()
    drain(d2_ref.at[pl.ds(1, NZ - 1)], col_recv2)
    for dy, dx, h, device in plane_peers(here):
        cell = wrap(y + dy, NY) * NX + wrap(x + dx, NX)
        dst = back_ref.at[h, plane_rank(-dy, -dx)]
        remote(d2_ref.at[:, cell], dst, plane_send2.at[h], plane_recv2.at[h], device).start()
    stay = pltpu.make_async_copy(d2_ref.at[:, y * NX + x], back_ref.at[0, 0], own_sem)
    stay.start()
    drain(d_ref.at[column], col_send)
    drain(fin_ref.at[plane], plane_send)
    drain(served_ref.at[pl.ds(0, chips - 1)], out_send)
    drain(d2_ref.at[pl.ds(1, NZ - 1)], col_send2)
    stay.wait()
    drain(back_ref.at[0, pl.ds(1, PLANE - 1)], plane_recv2.at[0])
    drain(back_ref.at[1], plane_recv2.at[1])
    drain(back_ref.at[0, pl.ds(1, PLANE - 1)], plane_send2.at[0])
    drain(back_ref.at[1], plane_send2.at[1])


def one_round(candidates, flags, embeddings, current, chips):
    rows_dev, width = embeddings.shape
    nrow = 2 * CAP
    vmem = pl.BlockSpec(memory_space=pltpu.VMEM)
    hbm = pl.BlockSpec(memory_space=pltpu.HBM)
    grid = pltpu.VMEM((chips, 128), I32)
    block = pltpu.VMEM((rows_dev, 128), F32)
    dma = pltpu.SemaphoreType.DMA
    return pl.pallas_call(
        round_kernel,
        in_specs=[hbm] * 4,
        out_specs=[vmem] * 8,
        out_shape=(
            jax.ShapeDtypeStruct((2, PLANE, NZ, 2, 128), I32),
            jax.ShapeDtypeStruct((K * 8, 128), F32),
            jax.ShapeDtypeStruct((nrow, 128), I32),
            jax.ShapeDtypeStruct((PITCH, 128), I32),
            jax.ShapeDtypeStruct((8, 128), F32),
            jax.ShapeDtypeStruct((READY * STEP, nrow * 128), BF16),
            jax.ShapeDtypeStruct((rows_dev, 128), I32),
            jax.ShapeDtypeStruct((READY, rows_dev, STEP), BF16),
        ),
        scratch_shapes=[
            pltpu.VMEM(candidates.shape, I32),
            pltpu.VMEM(candidates.shape, I32),
            pltpu.VMEM(current.shape, F32),
            pltpu.VMEM(candidates.shape, I32),
            pltpu.VMEM((2 * rows_dev, width), BF16),
            pltpu.VMEM((chips, CAP, width), BF16),
            pltpu.VMEM((chips, CAP, width), BF16),
            grid, grid, grid,
            pltpu.VMEM((2 * chips, 128), I32),
            pltpu.VMEM((nrow, 128), I32),
            pltpu.VMEM((nrow, 128), I32),
            pltpu.VMEM((128, nrow), I32),
            pltpu.VMEM((nrow * 8, 128), F32),
            pltpu.VMEM((rows_dev, 128), I32),
            pltpu.VMEM((rows_dev, width), F32),
            pltpu.VMEM((256, width), BF16),
            block, block, block,
            pltpu.VMEM((K * 8, 128), F32),
            pltpu.VMEM((chips * 2, rows_dev), BF16),
            pltpu.VMEM((512, rows_dev), BF16),
            pltpu.VMEM((chips, 2, 128), I32),
            pltpu.VMEM((NZ, PLANE, 2, 128), I32),
            pltpu.VMEM((rows_dev // 128 * K, 128), F32),
            dma((4,)), dma, dma, dma, dma, dma, dma, dma, dma,
            dma, dma((PLANE,)), dma, dma, dma, dma((2,)), dma((2,)),
        ],
        compiler_params=pltpu.CompilerParams(
            collective_id=0, has_side_effects=True, vmem_limit_bytes=34 << 20
        ),
        name="one_round",
    )(*[pltpu.with_memory_space_constraint(v, pltpu.HBM) for v in (candidates, flags, embeddings, current)])


def merge_kernel(
    back_ref, near_ref, pos_ref, row_ref, info_ref, q_ref, start_ref, hit_ref,
    out_ref, pay_ref, s_ref, x_ref, acc_ref, hot_ref,
):
    rows_dev = out_ref.shape[1]
    chips = back_ref.shape[1]
    lanes = iota((chips, 128), 1)
    group = lax.shift_right_logical(lanes, 5)
    first = (lanes & 16) == 0
    total = jnp.max(info_ref[0:1, :]).astype(I32)
    most = jnp.max(info_ref[1:2, :]).astype(I32)
    for h in range(2):
        for rr in range(2):
            words = back_ref[h, :, rr, :]
            low = (words & 65535).astype(F32)
            high = lax.shift_right_logical(words, 16).astype(F32)
            even = jnp.where(first, low, pltpu.roll(high, 16, 1))
            odd = jnp.where(first, pltpu.roll(low, 112, 1), high)
            for q in range(8):
                n = (h * CAP + rr * 8 + q) * chips
                hi, mid = split2(jnp.where(group == q // 2, odd if q & 1 else even, 0.0))
                pay_ref[n : n + chips, 0:128] = hi
                pay_ref[n : n + chips, 128:256] = mid
    steps = (total + STEP - 1) // STEP
    width = pay_ref.shape[0]

    def place_rows(t, hot):
        got = dot(hot, pay_ref[...], NN)
        for i in range(STEP // 128):
            at = slice(i * 128, (i + 1) * 128)
            turned = (got[at, 0:128] + got[at, 128:256]).T
            vals = turned[0:32] + turned[32:64] + turned[64:96] + turned[96:128]
            s_ref[pl.ds(t * (STEP // 128) + i, K, stride=PITCH), :] = vals

    def gather(t, carry):
        place_rows(t, q_ref[pl.ds(pl.multiple_of(t * STEP, STEP), STEP), :])
        return carry

    def gather_more(t, carry):
        place_rows(t, onehot(pos_ref[...] == t * STEP + iota((STEP, width), 0)))
        return carry

    lax.fori_loop(0, jnp.minimum(steps, READY), gather, 0)
    lax.fori_loop(READY, steps, gather_more, 0)
    lane = iota((8, 128), 1)
    groups = (total + 1023) // 1024

    def ahead(ref, at, s):
        here = ref[pl.ds(at, 8), :]
        after = ref[pl.ds(at + 1, 8), :]
        return after if s == 128 else pltpu.roll(jnp.where(lane >= s, here, after), 128 - s, 1)

    for e in range(8):

        @pl.when(most > 1 << e)
        def _():
            def step(g, carry):
                at = pl.multiple_of(g * 8, 8)
                same = row_ref[pl.ds(at, 8), :] == ahead(row_ref, at, 1 << e)
                mins = []
                for k in range(K):
                    later = ahead(s_ref, (K - 1 - k) * PITCH + at, 1 << e)
                    mins.append(jnp.minimum(s_ref[pl.ds(k * PITCH + at, 8), :], jnp.where(same, later, FAR)))
                best = merge_low(mins)
                for k in range(K):
                    s_ref[pl.ds(k * PITCH + at, 8), :] = best[k]
                return carry

            lax.fori_loop(0, groups, step, 0)

    acc_ref[...] = jnp.zeros_like(acc_ref)

    def expand_by(t, hot):
        cells = [s_ref[pl.ds(t * (STEP // 128) + i, K, stride=PITCH), :] for i in range(STEP // 128)]
        vals = jnp.concatenate(cells, axis=1)
        live = t * STEP + iota((K, STEP), 1) < total
        hi, mid = split2(jnp.where(live, vals, 0.0))
        ones = jnp.ones((K // 2, STEP), BF16)
        acc_ref[...] = acc_ref[...] + dot(jnp.concatenate([hi, mid, ones], axis=0), hot, NT)

    def expand(t, carry):
        expand_by(t, hit_ref[t])
        return carry

    def expand_more(t, carry):
        for i in range(STEP // 128):
            at = slice(i * 128, (i + 1) * 128)
            p = t * STEP + i * 128 + iota((rows_dev, 128), 1)
            hot_ref[:, at] = onehot(start_ref[...] == p)
        expand_by(t, hot_ref[...])
        return carry

    lax.fori_loop(0, jnp.minimum(steps, READY), expand, 0)
    lax.fori_loop(READY, steps, expand_more, 0)
    for b in range(rows_dev // 128):
        at = slice(b * 128, (b + 1) * 128)
        named = acc_ref[2 * K : 2 * K + 1, at] > 0.5
        x_ref[b * K : (b + 1) * K, :] = jnp.where(
            named, (acc_ref[0:K, at] + acc_ref[K : 2 * K, at]) * (1.0 / SCALE), FAR
        )
    have = near_ref[...]
    got = [x_ref[pl.ds(k, 8, stride=K), :] for k in range(K)]
    mins = [
        jnp.minimum(have[k * 8 : (k + 1) * 8, :], got[K - 1 - k])
        for k in range(K)
    ]
    best = merge_low(mins)
    for k in range(K):
        x_ref[k * 8 : (k + 1) * 8, :] = best[k]
    for b in range(rows_dev // 128):
        out_ref[:, b * 128 : (b + 1) * 128] = x_ref[pl.ds(b, K, stride=8), :]


def merge(back, best, pos, row, info, q, start, hit):
    rows_dev = start.shape[0]
    vmem = pl.BlockSpec(memory_space=pltpu.VMEM)
    return pl.pallas_call(
        merge_kernel,
        in_specs=[vmem] * 8,
        out_specs=vmem,
        out_shape=jax.ShapeDtypeStruct((K, rows_dev), F32),
        scratch_shapes=[
            pltpu.VMEM((pos.shape[1], 256), BF16),
            pltpu.VMEM((K * PITCH, 128), F32),
            pltpu.VMEM((rows_dev // 128 * K, 128), F32),
            pltpu.VMEM((2 * K + K // 2, rows_dev), F32),
            pltpu.VMEM((rows_dev, STEP), BF16),
        ],
        compiler_params=pltpu.CompilerParams(vmem_limit_bytes=20 << 20),
        name="merge",
    )(back, best, pos, row, info, q, start, hit)


def per_device(embeddings, candidates, fresh_flags, current):
    chips = lax.axis_size("rows")
    back, best, pos, row, info, q, start, hit = one_round(
        candidates, fresh_flags, embeddings, current.T, chips
    )
    back = back.reshape(2, chips, 2, 128)
    return merge(back, best, pos.reshape(1, -1), row, info, q, start, hit).T


def solution(mesh):
    spec = P(("rows", "sub"), None)
    return jax.shard_map(
        per_device, mesh=mesh, in_specs=(spec,) * 4, out_specs=spec, check_vma=False
    )
```

```python
import functools

import jax
import jax.numpy as jnp
from jax import lax
from jax.experimental import pallas as pl
from jax.experimental.pallas import tpu as pltpu
from jax.sharding import PartitionSpec as P

BLOCK = 128
CAP = 16
K = 32
FAR = 1.0e9
F32, BF16, I32 = jnp.float32, jnp.bfloat16, jnp.int32
NT = (((1,), (1,)), ((), ()))
NN = (((1,), (0,)), ((), ()))
PITCH = 40
NY, NZ, NX = 4, 8, 4
PLANE = NY * NX
AWAY = (0, 4, 3, 5, 2, 6, 1, 7)
STEP = 384
READY = 3
SCALE = 28672.0
TOP = 65535.0
MESH = pl.DeviceIdType.MESH


def dot(a, b, dims):
    return lax.dot_general(a, b, dims, preferred_element_type=F32)


def sort_pairs(n):
    pairs = []
    p = 1
    while p < n:
        k = p
        while k >= 1:
            for j in range(k % p, n - k, 2 * k):
                for i in range(min(k, n - j - k)):
                    if (i + j) // (2 * p) == (i + j + k) // (2 * p):
                        pairs.append((i + j, i + j + k))
            k //= 2
        p *= 2
    return pairs


SORT = sort_pairs(K)


def exchange(v, i, j):
    v[i], v[j] = jnp.minimum(v[i], v[j]), jnp.maximum(v[i], v[j])


def sort_list(values):
    v = list(values)
    for i, j in SORT:
        exchange(v, i, j)
    return v


def merge_low(mins):
    v = list(mins)
    d = K // 2
    while d >= 1:
        for i in range(K):
            if i & d == 0:
                exchange(v, i, i + d)
        d //= 2
    return v


def merge_lists(a, b):
    return merge_low([jnp.minimum(a[i], b[K - 1 - i]) for i in range(K)])


def split2(x):
    hi = x.astype(BF16)
    mid = (x - hi.astype(F32)).astype(BF16)
    return hi, mid


def iota(shape, dim):
    return lax.broadcasted_iota(I32, shape, dim)


def onehot(mask):
    return jnp.where(mask, 1.0, 0.0).astype(BF16)


def place():
    chip = lax.axis_index("rows")
    return lax.div(chip, NZ * NX), lax.rem(lax.div(chip, NX), NZ), lax.rem(chip, NX), lax.axis_index("sub")


def wrap(v, n):
    return jnp.where(v >= n, v - n, v)


def chip_at(y, z, x):
    return (wrap(y, NY) * NZ + wrap(z, NZ)) * NX + wrap(x, NX)


def column_peers(here):
    y, z, x, side = here
    return [(dz, {"rows": chip_at(y, z + dz, x), "sub": side}) for dz in AWAY[1:]]


def plane_peers(here, cores=2):
    y, z, x, side = here
    return [
        (dy, dx, h, {"rows": chip_at(y + dy, z, x + dx), "sub": 1 - side if h else side})
        for dy in range(NY)
        for dx in range(NX)
        for h in range(cores)
        if dy + dx + h > 0
    ]


def greet(here):
    y, z, x, side = here
    sem = pltpu.get_barrier_semaphore()
    peers = [p[-1] for p in column_peers(here)] + [p[-1] for p in plane_peers(here, 1)]
    peers.append({"rows": chip_at(y, z, x), "sub": 1 - side})
    for device in peers:
        pl.semaphore_signal(sem, inc=1, device_id=device, device_id_type=MESH)
    return lambda: pl.semaphore_wait(sem, len(peers))


def drain(ref, sem):
    pltpu.make_async_copy(ref, ref, sem).wait()


def remote(src, dst, send, recv, device):
    return pltpu.make_async_remote_copy(
        src_ref=src, dst_ref=dst, send_sem=send, recv_sem=recv, device_id=device, device_id_type=MESH
    )


def far_rank(dz):
    return AWAY.index(dz % NZ)


def plane_rank(dy, dx):
    return (dy % NY) * NX + dx % NX


def slots_of(c_ref, w_ref, s_ref, span_bits):
    blocks, n = c_ref.shape
    chips = w_ref.shape[0]
    owners = iota((chips, n), 0)
    before = onehot(iota((n, n), 0) < iota((n, n), 1))
    ranks = iota((CAP, n), 0)
    run = jnp.zeros((chips, 1), F32)
    acc = jnp.zeros((chips, 2 * CAP), F32)
    for b in range(blocks):
        c = c_ref[b : b + 1, :]
        chip = lax.shift_right_logical(c, span_bits)
        owner = (chip & 28) * 4 + lax.shift_right_logical(chip, 5) * 4 + (chip & 3)
        row1 = (c & ((1 << span_bits) - 1)) + 1
        mine = owner == owners
        mine_b = onehot(mine)
        pre = dot(mine_b, before, NN) + run
        rank = jnp.sum(jnp.where(mine, pre, 0.0), axis=0, keepdims=True).astype(I32)
        run = run + jnp.sum(jnp.where(mine, 1.0, 0.0), axis=1, keepdims=True)
        s_ref[b : b + 1, :] = owner * CAP + rank
        sel = ranks == rank
        hi = jnp.where(sel, lax.shift_right_logical(row1, 4).astype(F32), 0.0).astype(BF16)
        lo = jnp.where(sel, (row1 & 15).astype(F32), 0.0).astype(BF16)
        acc = acc + dot(mine_b, jnp.concatenate([hi, lo], axis=0), NT)
    wanted = (acc[:, :CAP] * 16.0 + acc[:, CAP:]).astype(I32) - 1
    w_ref[...] = jnp.concatenate([wanted] + [jnp.full((chips, CAP), -1, I32)] * (128 // CAP - 1), axis=1)


def plan_way_back(a, pos_ref, row_ref, start_ref, info_ref, key_ref, lv_ref, col_ref, acc_ref, end_ref):
    rows_dev = start_ref.shape[0]
    nrow = a.shape[0]
    slots = nrow * 128
    live = (a >= 0) & (a < rows_dev)
    sid = iota((nrow, 128), 0) * 128 + iota((nrow, 128), 1)
    key = jnp.where(live, a * slots + sid, (1 << 30) + sid)
    key_ref[...] = key
    lv_ref[...] = jnp.where(live, a, rows_dev)
    for h in range(nrow // 8):
        col_ref[:, h * 8 : (h + 1) * 8] = key[h * 8 : (h + 1) * 8, :].T
    acc_ref[...] = jnp.zeros_like(acc_ref)
    lane = iota((128, nrow), 1)

    def outer(c, carry):
        col = jnp.sum(jnp.where(lane == c, col_ref[...], 0), axis=1, keepdims=True)
        colb = jnp.broadcast_to(col, (128, 128))

        def inner(e, carry):
            less = jnp.where(colb < key_ref[pl.ds(e, 1), :], 1.0, 0.0)
            part = jnp.sum(less.reshape(16, 8, 128), axis=0)
            at = pl.ds(pl.multiple_of(e * 8, 8), 8)
            acc_ref[at, :] = acc_ref[at, :] + part
            return carry

        return lax.fori_loop(0, nrow, inner, carry)

    lax.fori_loop(0, nrow, outer, 0)
    for e in range(nrow):
        pos_ref[e : e + 1, :] = jnp.sum(acc_ref[e * 8 : (e + 1) * 8, :], axis=0, keepdims=True).astype(I32)

    def start_of(g, most):
        v = g * 128 + iota((128, 128), 0)
        low = jnp.zeros((128, 128), F32)
        own = jnp.zeros((128, 128), F32)
        for e in range(nrow):
            lv = lv_ref[e : e + 1, :]
            low = low + jnp.where(lv < v, 1.0, 0.0)
            own = own + jnp.where(lv == v, 1.0, 0.0)
        start = jnp.sum(low, axis=1, keepdims=True)
        count = jnp.sum(own, axis=1, keepdims=True)
        at = pl.ds(pl.multiple_of(g * 128, 128), 128)
        end_ref[at, :] = jnp.broadcast_to((start + count).astype(I32), (128, 128))
        start_ref[at, :] = jnp.broadcast_to(jnp.where(count > 0, start, -1.0).astype(I32), (128, 128))
        return jnp.maximum(most, count)

    most = lax.fori_loop(0, rows_dev // 128, start_of, jnp.zeros((128, 1), F32))
    total = jnp.sum(jnp.where(live, 1.0, 0.0), axis=(0, 1), keepdims=True).astype(I32)
    most = jnp.max(most, axis=0, keepdims=True).astype(I32)
    info_ref[...] = jnp.where(iota((8, 128), 0) == 0, total, most).astype(F32)
    row_ref[...] = jnp.full(row_ref.shape, rows_dev, I32)

    def row_of(c, carry):
        p = c * 128 + iota((8, 128), 1)
        acc = jnp.zeros((8, 128), F32)
        for g in range(rows_dev // 8):
            acc = acc + jnp.where(end_ref[g * 8 : (g + 1) * 8, :] <= p, 1.0, 0.0)
        row = jnp.sum(acc, axis=0, keepdims=True).astype(I32)
        row_ref[pl.ds(c, 1), :] = jnp.where(p[0:1, :] < total, row, rows_dev)
        return carry

    lax.fori_loop(0, nrow, row_of, 0)


def near(fwd_ref, cur_ref, out_ref, s_ref):
    for b in range(cur_ref.shape[1] // 128):
        s_ref[b * K : (b + 1) * K, :] = cur_ref[:, b * 128 : (b + 1) * 128]
    best = sort_list([s_ref[pl.ds(k, 8, stride=K), :] for k in range(K)])

    def body(g, best):
        more = [fwd_ref[pl.ds(g * K + t, 8, stride=128), :] for t in range(K)]
        return tuple(merge_lists(list(best), sort_list(more)))

    best = lax.fori_loop(0, 128 // K, body, tuple(best))
    for k in range(K):
        out_ref[k * 8 : (k + 1) * 8, :] = best[k]


def round_kernel(
    cand_hbm, flag_hbm, emb_hbm, cur_hbm,
    back_ref, near_ref, pos_ref, row_ref, info_ref, q_ref, start_ref, hit_ref,
    c_ref, flag_ref, cur_ref, slot_ref,
    rows_ref, served_ref, pulled_ref, w_ref, d_ref, e_ref, fin_ref,
    key_ref, lv_ref, col_ref, acc_ref, end_ref,
    cand_ref, z_ref, f_ref, a_ref, fwd_ref, t_ref, hot_ref, pay_ref, w2_ref, d2_ref, s_ref,
    in_sem, half_send, half_recv, col_send, col_recv, plane_send, plane_recv, tell_send, tell_recv,
    out_send, out_recv, own_sem, col_send2, col_recv2, plane_send2, plane_recv2,
):
    here = place()
    y, z, x, side = here
    rows_dev = emb_hbm.shape[0]
    span = rows_ref.shape[0]
    chips = pulled_ref.shape[0]
    half_at = pl.multiple_of(side * rows_dev, rows_dev)
    my_half = rows_ref.at[pl.ds(half_at, rows_dev)]
    brought = [
        pltpu.make_async_copy(src, dst, in_sem.at[i])
        for i, (src, dst) in enumerate(
            [(cand_hbm, c_ref), (emb_hbm, my_half), (flag_hbm, flag_ref), (cur_hbm, cur_ref)]
        )
    ]
    for copy in brought:
        copy.start()
    wait_for_peers = greet(here)
    brought[0].wait()
    slots_of(c_ref, w_ref, slot_ref, span.bit_length() - 1)
    wait_for_peers()
    other = {"rows": chip_at(y, z, x), "sub": 1 - side}
    half = remote(emb_hbm, my_half, half_send, half_recv, other)
    half.start()

    for dz, device in column_peers(here):
        src = w_ref.at[pl.ds(pl.multiple_of(wrap(z + dz, NZ) * PLANE, PLANE), PLANE)]
        dst = d_ref.at[pl.ds(far_rank(-dz) * PLANE, PLANE)]
        remote(src, dst, col_send, col_recv, device).start()
    own = pl.ds(pl.multiple_of(z * PLANE, PLANE), PLANE)
    d_ref[far_rank(0) * PLANE : (far_rank(0) + 1) * PLANE, :] = w_ref[own, :]
    column = pl.ds(0, (NZ - 1) * PLANE)
    drain(d_ref.at[column], col_recv)
    for dy, dx, _, device in plane_peers(here, 1):
        i = plane_rank(dy, dx)
        cell = wrap(y + dy, NY) * NX + wrap(x + dx, NX)
        e_ref[i * NZ : (i + 1) * NZ, :] = d_ref[pl.ds(cell, NZ, stride=PLANE), :]
        dst = fin_ref.at[pl.ds(plane_rank(-dy, -dx) * NZ, NZ)]
        remote(e_ref.at[pl.ds(i * NZ, NZ)], dst, plane_send, plane_recv, device).start()
    fin_ref[0:NZ, :] = d_ref[pl.ds(y * NX + x, NZ, stride=PLANE), :]
    plane = pl.ds(0, (PLANE - 1) * NZ)
    for copy in brought[1:]:
        copy.wait()
    half.wait()

    spread = iota((128, 128), 1) == (iota((128, 128), 0) & (CAP - 1))
    ids = iota((128, span), 1)
    me = (y * NX + x) * NZ + z

    def serve(c, carry):
        asked = fin_ref[0:NZ, :] if isinstance(c, int) else fin_ref[pl.ds(pl.multiple_of(c * NZ, NZ), NZ), :]
        wide = jnp.concatenate([jnp.broadcast_to(asked[j : j + 1, :], (CAP, 128)) for j in range(NZ)], axis=0)
        col = jnp.sum(jnp.where(spread, wide, 0), axis=1, keepdims=True)
        got = dot(onehot(col == ids), rows_ref[...], NN).astype(BF16)
        for j in range(NZ):
            served_ref[c * NZ + j] = got[j * CAP : (j + 1) * CAP, :]
        y_to = wrap(y + c // NX, NY)
        x_to = wrap(x + c % NX, NX)

        def send(j):
            device = {"rows": (y_to * NZ + wrap(z + AWAY[j], NZ)) * NX + x_to, "sub": side}
            remote(served_ref.at[c * NZ + j], pulled_ref.at[me], out_send, out_recv.at[c], device).start()

        if isinstance(c, int):
            assert c == 0
        else:
            send(0)
        for j in range(1, NZ):
            send(j)
        return carry

    serve(0, 0)
    drain(fin_ref.at[plane], plane_recv)
    tell = remote(fin_ref.at[pl.ds(0, chips)], fin_ref.at[pl.ds(chips, chips)], tell_send, tell_recv, other)
    tell.start()

    lax.fori_loop(1, PLANE, serve, 0)
    stay = pltpu.make_async_copy(served_ref.at[0], pulled_ref.at[me], own_sem)
    stay.start()

    tell.wait()
    turned = [fin_ref[h * chips : (h + 1) * chips, :].T[0:CAP, :] for h in range(2)]
    plan_way_back(
        jnp.concatenate(turned, axis=0) - side * rows_dev,
        pos_ref, row_ref, start_ref, info_ref, key_ref, lv_ref, col_ref, acc_ref, end_ref,
    )

    def ready(t, carry):
        p = iota((128, 128), 0) + t * 128
        for e in range(pos_ref.shape[0]):
            q_ref[pl.ds(pl.multiple_of(t * 128, 128), 128), e * 128 : (e + 1) * 128] = onehot(pos_ref[e : e + 1, :] == p)
        return carry

    lax.fori_loop(0, READY * STEP // 128, ready, 0)
    for i in range(READY * STEP // 128):
        hit_ref[:, i * 128 : (i + 1) * 128] = onehot(start_ref[...] == iota((rows_dev, 128), 1) + i * 128)

    slots = slot_ref[...]
    column_id = lax.shift_right_logical(slots, 4) & (PLANE - 1)
    in_column = lax.shift_right_logical(slots, 8) * CAP + (slots & (CAP - 1))
    column_cols = column_id.T
    in_cols = in_column.T
    blocks = slot_ref.shape[0]
    size = NZ * CAP
    cells = iota((128, 2 * size), 1)

    def source(c):
        y_from = wrap(y + NY - lax.div(c, NX), NY)
        return y_from * NX + wrap(x + NX - lax.rem(c, NX), NX)

    def arrived(c, count):
        drain(pulled_ref.at[pl.ds(0, count)], out_recv.at[c])

    def column_rows(c):
        return pulled_ref[pl.ds(source(c) * NZ, NZ)].reshape(size, -1)

    def picked(b, c, rows):
        here, there = source(c), source(c + 1)
        col, at = column_cols[:, b : b + 1], in_cols[:, b : b + 1]
        at = jnp.where(col == here, at, jnp.where(col == there, at + size, -1))
        return dot(onehot(at == cells), rows, NN)

    def two_columns(c):
        return jnp.concatenate([column_rows(c), column_rows(c + 1)], axis=0)

    stay.wait()
    arrived(0, NZ - 1)
    arrived(1, NZ)
    rows = two_columns(0)
    for b in range(blocks):
        cand_ref[b * 128 : (b + 1) * 128, :] = picked(b, 0, rows)

    def more_rows(k, carry):
        arrived(2 * k, NZ)
        arrived(2 * k + 1, NZ)
        rows = two_columns(2 * k)
        for b in range(blocks):
            at = slice(b * 128, (b + 1) * 128)
            cand_ref[at, :] = cand_ref[at, :] + picked(b, 2 * k, rows)
        return carry

    lax.fori_loop(1, PLANE // 2 - 1, more_rows, 0)
    last = PLANE - 2
    arrived(last, NZ)
    arrived(last + 1, NZ)
    rows = two_columns(last)

    flags = flag_ref[...]
    flag_cols = flags.T
    eye = iota((256, 256), 0) == iota((256, 256), 1)
    off_diag = iota((128, 128), 0) != iota((128, 128), 1)
    for b in range(blocks):
        at = slice(b * 128, (b + 1) * 128)
        z_ref[0:128, :] = rows_ref[pl.ds(half_at + b * 128, 128), :]
        z_ref[128:256, :] = (cand_ref[at, :] + picked(b, last, rows)).astype(BF16)
        both = z_ref[...]
        gram = dot(both, both, NT)
        diag = jnp.where(eye, gram, 0.0)
        n_col = jnp.sum(diag, axis=1, keepdims=True)
        n_row = jnp.sum(diag, axis=0, keepdims=True)
        dist = n_col + n_row - 2.0 * gram
        f_ref[at, :] = dist[0:128, 128:256]
        fwd_ref[at, :] = dist[128:256, 0:128]
        fresh = (flag_cols[:, b : b + 1] + flags[b : b + 1, :]) > 0
        a_ref[at, :] = jnp.where(fresh & off_diag, dist[128:256, 128:256], FAR)

    def take(ref, g):
        return [ref[pl.ds(g * K + t, 8, stride=128), :] for t in range(K)]

    best = sort_list(take(f_ref, 0))

    def more(ref, lo, best):
        def body(g, best):
            return tuple(merge_lists(list(best), sort_list(take(ref, g))))

        return lax.fori_loop(lo, 128 // K, body, tuple(best))

    best = more(f_ref, 1, best)
    best = more(a_ref, 0, best)

    for k in range(K):
        t_ref[k * 8 : (k + 1) * 8, :] = jnp.floor(jnp.clip(best[k] * SCALE + 0.5, 0.0, TOP))
    octet = lax.shift_right_logical(iota((128, 128), 0), 4)
    groups = iota((chips * 2, 128), 0)
    for b in range(blocks):
        at = slice(b * 128, (b + 1) * 128)
        slot = slot_ref[b : b + 1, :]
        code = t_ref[pl.ds(b, K, stride=8), :]
        hi = jnp.floor(code * (1.0 / 256.0))
        lo = code - hi * 256.0
        mine = (slot & 7) == octet
        for i, piece in enumerate((hi[:16], lo[:16], hi[16:], lo[16:])):
            pay_ref[i * 128 : (i + 1) * 128, at] = jnp.where(mine, jnp.concatenate([piece] * 8, axis=0), 0.0).astype(BF16)
        hot_ref[:, at] = onehot(lax.shift_right_logical(slot, 3) == groups)
    sums = dot(hot_ref[...], pay_ref[...], NT)
    low = (sums[:, 0:128] * 256.0 + sums[:, 128:256]).astype(I32)
    high = (sums[:, 256:384] * 256.0 + sums[:, 384:512]).astype(I32)
    words = low + lax.shift_left(high, 16)
    for n in range(chips):
        w2_ref[n] = words[2 * n : 2 * n + 2, :]
    for dz, device in column_peers(here):
        src = w2_ref.at[pl.ds(wrap(z + dz, NZ) * PLANE, PLANE)]
        remote(src, d2_ref.at[far_rank(-dz)], col_send2, col_recv2, device).start()
    stay = pltpu.make_async_copy(w2_ref.at[pl.ds(z * PLANE, PLANE)], d2_ref.at[far_rank(0)], own_sem)
    stay.start()
    near(fwd_ref, cur_ref, near_ref, s_ref)
    stay.wait()
    drain(d2_ref.at[pl.ds(1, NZ - 1)], col_recv2)
    for dy, dx, h, device in plane_peers(here):
        cell = wrap(y + dy, NY) * NX + wrap(x + dx, NX)
        dst = back_ref.at[h, plane_rank(-dy, -dx)]
        remote(d2_ref.at[:, cell], dst, plane_send2.at[h], plane_recv2.at[h], device).start()
    stay = pltpu.make_async_copy(d2_ref.at[:, y * NX + x], back_ref.at[0, 0], own_sem)
    stay.start()
    drain(d_ref.at[column], col_send)
    drain(fin_ref.at[plane], plane_send)
    drain(served_ref.at[pl.ds(0, chips - 1)], out_send)
    drain(d2_ref.at[pl.ds(1, NZ - 1)], col_send2)
    stay.wait()
    drain(back_ref.at[0, pl.ds(1, PLANE - 1)], plane_recv2.at[0])
    drain(back_ref.at[1], plane_recv2.at[1])
    drain(back_ref.at[0, pl.ds(1, PLANE - 1)], plane_send2.at[0])
    drain(back_ref.at[1], plane_send2.at[1])


def one_round(candidates, flags, embeddings, current, chips):
    rows_dev, width = embeddings.shape
    nrow = 2 * CAP
    vmem = pl.BlockSpec(memory_space=pltpu.VMEM)
    hbm = pl.BlockSpec(memory_space=pltpu.HBM)
    grid = pltpu.VMEM((chips, 128), I32)
    block = pltpu.VMEM((rows_dev, 128), F32)
    dma = pltpu.SemaphoreType.DMA
    return pl.pallas_call(
        round_kernel,
        in_specs=[hbm] * 4,
        out_specs=[vmem] * 8,
        out_shape=(
            jax.ShapeDtypeStruct((2, PLANE, NZ, 2, 128), I32),
            jax.ShapeDtypeStruct((K * 8, 128), F32),
            jax.ShapeDtypeStruct((nrow, 128), I32),
            jax.ShapeDtypeStruct((PITCH, 128), I32),
            jax.ShapeDtypeStruct((8, 128), F32),
            jax.ShapeDtypeStruct((READY * STEP, nrow * 128), BF16),
            jax.ShapeDtypeStruct((rows_dev, 128), I32),
            jax.ShapeDtypeStruct((rows_dev, READY * STEP), BF16),
        ),
        scratch_shapes=[
            pltpu.VMEM(candidates.shape, I32),
            pltpu.VMEM(candidates.shape, I32),
            pltpu.VMEM(current.shape, F32),
            pltpu.VMEM(candidates.shape, I32),
            pltpu.VMEM((2 * rows_dev, width), BF16),
            pltpu.VMEM((chips, CAP, width), BF16),
            pltpu.VMEM((chips, CAP, width), BF16),
            grid, grid, grid,
            pltpu.VMEM((2 * chips, 128), I32),
            pltpu.VMEM((nrow, 128), I32),
            pltpu.VMEM((nrow, 128), I32),
            pltpu.VMEM((128, nrow), I32),
            pltpu.VMEM((nrow * 8, 128), F32),
            pltpu.VMEM((rows_dev, 128), I32),
            pltpu.VMEM((rows_dev, width), F32),
            pltpu.VMEM((256, width), BF16),
            block, block, block,
            pltpu.VMEM((K * 8, 128), F32),
            pltpu.VMEM((chips * 2, rows_dev), BF16),
            pltpu.VMEM((512, rows_dev), BF16),
            pltpu.VMEM((chips, 2, 128), I32),
            pltpu.VMEM((NZ, PLANE, 2, 128), I32),
            pltpu.VMEM((rows_dev // 128 * K, 128), F32),
            dma((4,)), dma, dma, dma, dma, dma, dma, dma, dma,
            dma, dma((PLANE,)), dma, dma, dma, dma((2,)), dma((2,)),
        ],
        compiler_params=pltpu.CompilerParams(
            collective_id=0, has_side_effects=True, vmem_limit_bytes=34 << 20
        ),
        name="one_round",
    )(*[pltpu.with_memory_space_constraint(v, pltpu.HBM) for v in (candidates, flags, embeddings, current)])


def merge_kernel(
    back_ref, near_ref, pos_ref, row_ref, info_ref, q_ref, start_ref, hit_ref,
    out_ref, pay_ref, s_ref, x_ref, acc_ref, hot_ref,
):
    rows_dev = out_ref.shape[1]
    chips = back_ref.shape[1]
    lanes = iota((chips, 128), 1)
    group = lax.shift_right_logical(lanes, 5)
    first = (lanes & 16) == 0
    keep = [onehot(group == u) for u in range(4)]
    total = jnp.max(info_ref[0:1, :]).astype(I32)
    most = jnp.max(info_ref[1:2, :]).astype(I32)
    for h in range(2):
        for rr in range(2):
            words = back_ref[h, :, rr, :]
            low = (words & 65535).astype(F32)
            high = lax.shift_right_logical(words, 16).astype(F32)
            even = jnp.where(first, low, pltpu.roll(high, 16, 1))
            odd = jnp.where(first, pltpu.roll(low, 112, 1), high)
            pieces = [split2(even), split2(odd)]
            for q in range(8):
                n = (h * CAP + rr * 8 + q) * chips
                hi, mid = pieces[q & 1]
                pay_ref[n : n + chips, 0:128] = hi * keep[q // 2]
                pay_ref[n : n + chips, 128:256] = mid * keep[q // 2]
    steps = (total + STEP - 1) // STEP
    width = pay_ref.shape[0]

    def place_rows(base, got):
        for i in range(got.shape[0] // 128):
            at = slice(i * 128, (i + 1) * 128)
            turned = (got[at, 0:128] + got[at, 128:256]).T
            vals = turned[0:32] + turned[32:64] + turned[64:96] + turned[96:128]
            s_ref[pl.ds(base + i, K, stride=PITCH), :] = vals

    def gather_more(t, carry):
        hot = onehot(pos_ref[...] == t * STEP + iota((STEP, width), 0))
        place_rows(t * (STEP // 128), dot(hot, pay_ref[...], NN))
        return carry

    place_rows(0, dot(q_ref[...], pay_ref[...], NN))
    lax.fori_loop(READY, steps, gather_more, 0)
    lane = iota((8, 128), 1)
    groups = (total + 1023) // 1024

    def ahead(ref, at, s):
        here = ref[pl.ds(at, 8), :]
        after = ref[pl.ds(at + 1, 8), :]
        return after if s == 128 else pltpu.roll(jnp.where(lane >= s, here, after), 128 - s, 1)

    for e in range(8):

        @pl.when(most > 1 << e)
        def _():
            def step(g, carry):
                at = pl.multiple_of(g * 8, 8)
                same = row_ref[pl.ds(at, 8), :] == ahead(row_ref, at, 1 << e)
                mins = []
                for k in range(K):
                    later = ahead(s_ref, (K - 1 - k) * PITCH + at, 1 << e)
                    mins.append(jnp.minimum(s_ref[pl.ds(k * PITCH + at, 8), :], jnp.where(same, later, FAR)))
                best = merge_low(mins)
                for k in range(K):
                    s_ref[pl.ds(k * PITCH + at, 8), :] = best[k]
                return carry

            lax.fori_loop(0, groups, step, 0)

    def listed(base, n):
        vals = jnp.concatenate([s_ref[pl.ds(base + i, K, stride=PITCH), :] for i in range(n)], axis=1)
        live = base * 128 + iota((K, n * 128), 1) < total
        hi, mid = split2(jnp.where(live, vals, 0.0))
        return jnp.concatenate([hi, mid, jnp.ones((K // 2, n * 128), BF16)], axis=0)

    acc_ref[...] = dot(listed(0, READY * STEP // 128), hit_ref[...], NT)

    def expand_more(t, carry):
        for i in range(STEP // 128):
            at = slice(i * 128, (i + 1) * 128)
            p = t * STEP + i * 128 + iota((rows_dev, 128), 1)
            hot_ref[:, at] = onehot(start_ref[...] == p)
        acc_ref[...] = acc_ref[...] + dot(listed(t * (STEP // 128), STEP // 128), hot_ref[...], NT)
        return carry

    lax.fori_loop(READY, steps, expand_more, 0)
    for b in range(rows_dev // 128):
        at = slice(b * 128, (b + 1) * 128)
        named = acc_ref[2 * K : 2 * K + 1, at] > 0.5
        x_ref[b * K : (b + 1) * K, :] = jnp.where(
            named, (acc_ref[0:K, at] + acc_ref[K : 2 * K, at]) * (1.0 / SCALE), FAR
        )
    have = near_ref[...]
    got = [x_ref[pl.ds(k, 8, stride=K), :] for k in range(K)]
    mins = [
        jnp.minimum(have[k * 8 : (k + 1) * 8, :], got[K - 1 - k])
        for k in range(K)
    ]
    best = merge_low(mins)
    for k in range(K):
        x_ref[k * 8 : (k + 1) * 8, :] = best[k]
    for b in range(rows_dev // 128):
        out_ref[:, b * 128 : (b + 1) * 128] = x_ref[pl.ds(b, K, stride=8), :]


def merge(back, best, pos, row, info, q, start, hit):
    rows_dev = start.shape[0]
    vmem = pl.BlockSpec(memory_space=pltpu.VMEM)
    return pl.pallas_call(
        merge_kernel,
        in_specs=[vmem] * 8,
        out_specs=vmem,
        out_shape=jax.ShapeDtypeStruct((K, rows_dev), F32),
        scratch_shapes=[
            pltpu.VMEM((pos.shape[1], 256), BF16),
            pltpu.VMEM((K * PITCH, 128), F32),
            pltpu.VMEM((rows_dev // 128 * K, 128), F32),
            pltpu.VMEM((2 * K + K // 2, rows_dev), F32),
            pltpu.VMEM((rows_dev, STEP), BF16),
        ],
        compiler_params=pltpu.CompilerParams(vmem_limit_bytes=20 << 20),
        name="merge",
    )(back, best, pos, row, info, q, start, hit)


def per_device(embeddings, candidates, fresh_flags, current):
    chips = lax.axis_size("rows")
    back, best, pos, row, info, q, start, hit = one_round(
        candidates, fresh_flags, embeddings, current.T, chips
    )
    back = back.reshape(2, chips, 2, 128)
    return merge(back, best, pos.reshape(1, -1), row, info, q, start, hit).T


def solution(mesh):
    spec = P(("rows", "sub"), None)
    return jax.shard_map(
        per_device, mesh=mesh, in_specs=(spec,) * 4, out_specs=spec, check_vma=False
    )
```

```python
import functools

import jax
import jax.numpy as jnp
from jax import lax
from jax.experimental import pallas as pl
from jax.experimental.pallas import tpu as pltpu
from jax.sharding import PartitionSpec as P

BLOCK = 128
CAP = 16
K = 32
FAR = 1.0e9
F32, BF16, I32 = jnp.float32, jnp.bfloat16, jnp.int32
NT = (((1,), (1,)), ((), ()))
NN = (((1,), (0,)), ((), ()))
PITCH = 40
NY, NZ, NX = 4, 8, 4
PLANE = NY * NX
AWAY = (0, 4, 3, 5, 2, 6, 1, 7)
STEP = 384
READY = 3
SCALE = 28672.0
TOP = 65535.0
MESH = pl.DeviceIdType.MESH


def dot(a, b, dims):
    return lax.dot_general(a, b, dims, preferred_element_type=F32)


def sort_pairs(n):
    pairs = []
    p = 1
    while p < n:
        k = p
        while k >= 1:
            for j in range(k % p, n - k, 2 * k):
                for i in range(min(k, n - j - k)):
                    if (i + j) // (2 * p) == (i + j + k) // (2 * p):
                        pairs.append((i + j, i + j + k))
            k //= 2
        p *= 2
    return pairs


SORT = sort_pairs(K)


def exchange(v, i, j):
    v[i], v[j] = jnp.minimum(v[i], v[j]), jnp.maximum(v[i], v[j])


def sort_list(values):
    v = list(values)
    for i, j in SORT:
        exchange(v, i, j)
    return v


def merge_low(mins):
    v = list(mins)
    d = K // 2
    while d >= 1:
        for i in range(K):
            if i & d == 0:
                exchange(v, i, i + d)
        d //= 2
    return v


def merge_lists(a, b):
    return merge_low([jnp.minimum(a[i], b[K - 1 - i]) for i in range(K)])


def split2(x):
    hi = x.astype(BF16)
    mid = (x - hi.astype(F32)).astype(BF16)
    return hi, mid


def iota(shape, dim):
    return lax.broadcasted_iota(I32, shape, dim)


def onehot(mask):
    return jnp.where(mask, 1.0, 0.0).astype(BF16)


def place():
    chip = lax.axis_index("rows")
    return lax.div(chip, NZ * NX), lax.rem(lax.div(chip, NX), NZ), lax.rem(chip, NX), lax.axis_index("sub")


def wrap(v, n):
    return jnp.where(v >= n, v - n, v)


def chip_at(y, z, x):
    return (wrap(y, NY) * NZ + wrap(z, NZ)) * NX + wrap(x, NX)


def column_peers(here):
    y, z, x, side = here
    return [(dz, {"rows": chip_at(y, z + dz, x), "sub": side}) for dz in AWAY[1:]]


def plane_peers(here, cores=2):
    y, z, x, side = here
    return [
        (dy, dx, h, {"rows": chip_at(y + dy, z, x + dx), "sub": 1 - side if h else side})
        for dy in range(NY)
        for dx in range(NX)
        for h in range(cores)
        if dy + dx + h > 0
    ]


def greet(here):
    y, z, x, side = here
    sem = pltpu.get_barrier_semaphore()
    peers = [p[-1] for p in column_peers(here)] + [p[-1] for p in plane_peers(here, 1)]
    peers.append({"rows": chip_at(y, z, x), "sub": 1 - side})
    for device in peers:
        pl.semaphore_signal(sem, inc=1, device_id=device, device_id_type=MESH)
    return lambda: pl.semaphore_wait(sem, len(peers))


def drain(ref, sem):
    pltpu.make_async_copy(ref, ref, sem).wait()


def remote(src, dst, send, recv, device):
    return pltpu.make_async_remote_copy(
        src_ref=src, dst_ref=dst, send_sem=send, recv_sem=recv, device_id=device, device_id_type=MESH
    )


def far_rank(dz):
    return AWAY.index(dz % NZ)


def plane_rank(dy, dx):
    return (dy % NY) * NX + dx % NX


def slots_of(c_ref, w_ref, s_ref, span_bits):
    blocks, n = c_ref.shape
    chips = w_ref.shape[0]
    owners = iota((chips, n), 0)
    before = onehot(iota((n, n), 0) < iota((n, n), 1))
    ranks = iota((CAP, n), 0)
    run = jnp.zeros((chips, 1), F32)
    acc = jnp.zeros((chips, 2 * CAP), F32)
    for b in range(blocks):
        c = c_ref[b : b + 1, :]
        chip = lax.shift_right_logical(c, span_bits)
        owner = (chip & 28) * 4 + lax.shift_right_logical(chip, 5) * 4 + (chip & 3)
        row1 = (c & ((1 << span_bits) - 1)) + 1
        mine = owner == owners
        mine_b = onehot(mine)
        pre = dot(mine_b, before, NN) + run
        rank = jnp.sum(jnp.where(mine, pre, 0.0), axis=0, keepdims=True).astype(I32)
        run = run + jnp.sum(jnp.where(mine, 1.0, 0.0), axis=1, keepdims=True)
        s_ref[b : b + 1, :] = owner * CAP + rank
        sel = ranks == rank
        hi = jnp.where(sel, lax.shift_right_logical(row1, 4).astype(F32), 0.0).astype(BF16)
        lo = jnp.where(sel, (row1 & 15).astype(F32), 0.0).astype(BF16)
        acc = acc + dot(mine_b, jnp.concatenate([hi, lo], axis=0), NT)
    wanted = (acc[:, :CAP] * 16.0 + acc[:, CAP:]).astype(I32) - 1
    w_ref[...] = jnp.concatenate([wanted] + [jnp.full((chips, CAP), -1, I32)] * (128 // CAP - 1), axis=1)


def plan_way_back(a, pos_ref, row_ref, start_ref, info_ref, key_ref, lv_ref, col_ref, acc_ref, end_ref):
    rows_dev = start_ref.shape[0]
    nrow = a.shape[0]
    slots = nrow * 128
    live = (a >= 0) & (a < rows_dev)
    sid = iota((nrow, 128), 0) * 128 + iota((nrow, 128), 1)
    key = jnp.where(live, a * slots + sid, (1 << 30) + sid)
    key_ref[...] = key
    lv_ref[...] = jnp.where(live, a, rows_dev)
    for h in range(nrow // 8):
        col_ref[:, h * 8 : (h + 1) * 8] = key[h * 8 : (h + 1) * 8, :].T
    acc_ref[...] = jnp.zeros_like(acc_ref)
    lane = iota((128, nrow), 1)

    def outer(c, carry):
        col = jnp.sum(jnp.where(lane == c, col_ref[...], 0), axis=1, keepdims=True)
        colb = jnp.broadcast_to(col, (128, 128))

        def inner(e, carry):
            less = jnp.where(colb < key_ref[pl.ds(e, 1), :], 1.0, 0.0)
            part = jnp.sum(less.reshape(16, 8, 128), axis=0)
            at = pl.ds(pl.multiple_of(e * 8, 8), 8)
            acc_ref[at, :] = acc_ref[at, :] + part
            return carry

        return lax.fori_loop(0, nrow, inner, carry)

    lax.fori_loop(0, nrow, outer, 0)
    for e in range(nrow):
        pos_ref[e : e + 1, :] = jnp.sum(acc_ref[e * 8 : (e + 1) * 8, :], axis=0, keepdims=True).astype(I32)

    def start_of(g, most):
        v = g * 128 + iota((128, 128), 0)
        low = jnp.zeros((128, 128), F32)
        own = jnp.zeros((128, 128), F32)
        for e in range(nrow):
            lv = lv_ref[e : e + 1, :]
            low = low + jnp.where(lv < v, 1.0, 0.0)
            own = own + jnp.where(lv == v, 1.0, 0.0)
        start = jnp.sum(low, axis=1, keepdims=True)
        count = jnp.sum(own, axis=1, keepdims=True)
        at = pl.ds(pl.multiple_of(g * 128, 128), 128)
        end_ref[at, :] = jnp.broadcast_to((start + count).astype(I32), (128, 128))
        start_ref[at, :] = jnp.broadcast_to(jnp.where(count > 0, start, -1.0).astype(I32), (128, 128))
        return jnp.maximum(most, count)

    most = lax.fori_loop(0, rows_dev // 128, start_of, jnp.zeros((128, 1), F32))
    total = jnp.sum(jnp.where(live, 1.0, 0.0), axis=(0, 1), keepdims=True).astype(I32)
    most = jnp.max(most, axis=0, keepdims=True).astype(I32)
    info_ref[...] = jnp.where(iota((8, 128), 0) == 0, total, most).astype(F32)
    row_ref[...] = jnp.full(row_ref.shape, rows_dev, I32)

    def row_of(c, carry):
        p = c * 128 + iota((8, 128), 1)
        acc = jnp.zeros((8, 128), F32)
        for g in range(rows_dev // 8):
            acc = acc + jnp.where(end_ref[g * 8 : (g + 1) * 8, :] <= p, 1.0, 0.0)
        row = jnp.sum(acc, axis=0, keepdims=True).astype(I32)
        row_ref[pl.ds(c, 1), :] = jnp.where(p[0:1, :] < total, row, rows_dev)
        return carry

    lax.fori_loop(0, nrow, row_of, 0)


def near(fwd_ref, cur_ref, out_ref, s_ref):
    for b in range(cur_ref.shape[1] // 128):
        s_ref[b * K : (b + 1) * K, :] = cur_ref[:, b * 128 : (b + 1) * 128]
    best = sort_list([s_ref[pl.ds(k, 8, stride=K), :] for k in range(K)])

    def body(g, best):
        more = [fwd_ref[pl.ds(g * K + t, 8, stride=128), :] for t in range(K)]
        return tuple(merge_lists(list(best), sort_list(more)))

    best = lax.fori_loop(0, 128 // K, body, tuple(best))
    for k in range(K):
        out_ref[k * 8 : (k + 1) * 8, :] = best[k]


def slot_row(n, u):
    return n // 4 * CAP + n // 2 % 2 * 8 + 2 * u + n % 2


def round_kernel(
    cand_hbm, flag_hbm, emb_hbm, cur_hbm,
    back_ref, near_ref, pos_ref, row_ref, info_ref, q_ref, start_ref, hit_ref, quad_ref,
    c_ref, flag_ref, cur_ref, slot_ref,
    rows_ref, served_ref, pulled_ref, w_ref, d_ref, e_ref, fin_ref,
    key_ref, lv_ref, col_ref, acc_ref, end_ref,
    cand_ref, z_ref, f_ref, a_ref, fwd_ref, t_ref, hot_ref, pay_ref, w2_ref, d2_ref, s_ref,
    in_sem, half_send, half_recv, col_send, col_recv, plane_send, plane_recv, tell_send, tell_recv,
    out_send, out_recv, own_sem, col_send2, col_recv2, plane_send2, plane_recv2,
):
    here = place()
    y, z, x, side = here
    rows_dev = emb_hbm.shape[0]
    span = rows_ref.shape[0]
    chips = pulled_ref.shape[0]
    half_at = pl.multiple_of(side * rows_dev, rows_dev)
    my_half = rows_ref.at[pl.ds(half_at, rows_dev)]
    brought = [
        pltpu.make_async_copy(src, dst, in_sem.at[i])
        for i, (src, dst) in enumerate(
            [(cand_hbm, c_ref), (emb_hbm, my_half), (flag_hbm, flag_ref), (cur_hbm, cur_ref)]
        )
    ]
    for copy in brought:
        copy.start()
    wait_for_peers = greet(here)
    brought[0].wait()
    slots_of(c_ref, w_ref, slot_ref, span.bit_length() - 1)
    wait_for_peers()
    other = {"rows": chip_at(y, z, x), "sub": 1 - side}
    half = remote(emb_hbm, my_half, half_send, half_recv, other)
    half.start()

    for dz, device in column_peers(here):
        src = w_ref.at[pl.ds(pl.multiple_of(wrap(z + dz, NZ) * PLANE, PLANE), PLANE)]
        dst = d_ref.at[pl.ds(far_rank(-dz) * PLANE, PLANE)]
        remote(src, dst, col_send, col_recv, device).start()
    own = pl.ds(pl.multiple_of(z * PLANE, PLANE), PLANE)
    d_ref[far_rank(0) * PLANE : (far_rank(0) + 1) * PLANE, :] = w_ref[own, :]
    column = pl.ds(0, (NZ - 1) * PLANE)
    drain(d_ref.at[column], col_recv)
    for dy, dx, _, device in plane_peers(here, 1):
        i = plane_rank(dy, dx)
        cell = wrap(y + dy, NY) * NX + wrap(x + dx, NX)
        e_ref[i * NZ : (i + 1) * NZ, :] = d_ref[pl.ds(cell, NZ, stride=PLANE), :]
        dst = fin_ref.at[pl.ds(plane_rank(-dy, -dx) * NZ, NZ)]
        remote(e_ref.at[pl.ds(i * NZ, NZ)], dst, plane_send, plane_recv, device).start()
    fin_ref[0:NZ, :] = d_ref[pl.ds(y * NX + x, NZ, stride=PLANE), :]
    plane = pl.ds(0, (PLANE - 1) * NZ)
    for copy in brought[1:]:
        copy.wait()
    half.wait()

    spread = iota((128, 128), 1) == (iota((128, 128), 0) & (CAP - 1))
    ids = iota((128, span), 1)
    me = (y * NX + x) * NZ + z

    def serve(c, carry):
        asked = fin_ref[0:NZ, :] if isinstance(c, int) else fin_ref[pl.ds(pl.multiple_of(c * NZ, NZ), NZ), :]
        wide = jnp.concatenate([jnp.broadcast_to(asked[j : j + 1, :], (CAP, 128)) for j in range(NZ)], axis=0)
        col = jnp.sum(jnp.where(spread, wide, 0), axis=1, keepdims=True)
        got = dot(onehot(col == ids), rows_ref[...], NN).astype(BF16)
        for j in range(NZ):
            served_ref[c * NZ + j] = got[j * CAP : (j + 1) * CAP, :]
        y_to = wrap(y + c // NX, NY)
        x_to = wrap(x + c % NX, NX)

        def send(j):
            device = {"rows": (y_to * NZ + wrap(z + AWAY[j], NZ)) * NX + x_to, "sub": side}
            remote(served_ref.at[c * NZ + j], pulled_ref.at[me], out_send, out_recv.at[c], device).start()

        if isinstance(c, int):
            assert c == 0
        else:
            send(0)
        for j in range(1, NZ):
            send(j)
        return carry

    serve(0, 0)
    drain(fin_ref.at[plane], plane_recv)
    tell = remote(fin_ref.at[pl.ds(0, chips)], fin_ref.at[pl.ds(chips, chips)], tell_send, tell_recv, other)
    tell.start()

    lax.fori_loop(1, PLANE, serve, 0)
    stay = pltpu.make_async_copy(served_ref.at[0], pulled_ref.at[me], own_sem)
    stay.start()

    tell.wait()
    turned = [fin_ref[h * chips : (h + 1) * chips, :].T[0:CAP, :] for h in range(2)]
    plan_way_back(
        jnp.concatenate(turned, axis=0) - side * rows_dev,
        pos_ref, row_ref, start_ref, info_ref, key_ref, lv_ref, col_ref, acc_ref, end_ref,
    )

    def ready(t, carry):
        p = iota((128, 128), 0) + t * 128
        at = pl.ds(pl.multiple_of(t * 128, 128), 128)
        quad = jnp.zeros((128, 128), F32)
        for n in range(8):
            found = jnp.zeros((128, 128), F32)
            for u in range(4):
                e = slot_row(n, u)
                hit = jnp.where(pos_ref[e : e + 1, :] == p, 1.0, 0.0)
                found = found + hit
                quad = quad + hit * float(u)
            q_ref[at, n * 128 : (n + 1) * 128] = found.astype(BF16)
        quad_ref[pl.ds(t, 1), :] = jnp.sum(quad.T, axis=0, keepdims=True)
        return carry

    lax.fori_loop(0, READY * STEP // 128, ready, 0)
    for i in range(READY * STEP // 128):
        hit_ref[:, i * 128 : (i + 1) * 128] = onehot(start_ref[...] == iota((rows_dev, 128), 1) + i * 128)

    slots = slot_ref[...]
    column_id = lax.shift_right_logical(slots, 4) & (PLANE - 1)
    in_column = lax.shift_right_logical(slots, 8) * CAP + (slots & (CAP - 1))
    column_cols = column_id.T
    in_cols = in_column.T
    blocks = slot_ref.shape[0]
    size = NZ * CAP
    cells = iota((128, 2 * size), 1)

    def source(c):
        y_from = wrap(y + NY - lax.div(c, NX), NY)
        return y_from * NX + wrap(x + NX - lax.rem(c, NX), NX)

    def arrived(c, count):
        drain(pulled_ref.at[pl.ds(0, count)], out_recv.at[c])

    def column_rows(c):
        return pulled_ref[pl.ds(source(c) * NZ, NZ)].reshape(size, -1)

    def picked(b, c, rows):
        here, there = source(c), source(c + 1)
        col, at = column_cols[:, b : b + 1], in_cols[:, b : b + 1]
        at = jnp.where(col == here, at, jnp.where(col == there, at + size, -1))
        return dot(onehot(at == cells), rows, NN)

    def two_columns(c):
        return jnp.concatenate([column_rows(c), column_rows(c + 1)], axis=0)

    stay.wait()
    arrived(0, NZ - 1)
    arrived(1, NZ)
    rows = two_columns(0)
    for b in range(blocks):
        cand_ref[b * 128 : (b + 1) * 128, :] = picked(b, 0, rows)

    def more_rows(k, carry):
        arrived(2 * k, NZ)
        arrived(2 * k + 1, NZ)
        rows = two_columns(2 * k)
        for b in range(blocks):
            at = slice(b * 128, (b + 1) * 128)
            cand_ref[at, :] = cand_ref[at, :] + picked(b, 2 * k, rows)
        return carry

    lax.fori_loop(1, PLANE // 2 - 1, more_rows, 0)
    last = PLANE - 2
    arrived(last, NZ)
    arrived(last + 1, NZ)
    rows = two_columns(last)

    flags = flag_ref[...]
    flag_cols = flags.T
    eye = iota((256, 256), 0) == iota((256, 256), 1)
    off_diag = iota((128, 128), 0) != iota((128, 128), 1)
    for b in range(blocks):
        at = slice(b * 128, (b + 1) * 128)
        z_ref[0:128, :] = rows_ref[pl.ds(half_at + b * 128, 128), :]
        z_ref[128:256, :] = (cand_ref[at, :] + picked(b, last, rows)).astype(BF16)
        both = z_ref[...]
        gram = dot(both, both, NT)
        diag = jnp.where(eye, gram, 0.0)
        n_col = jnp.sum(diag, axis=1, keepdims=True)
        n_row = jnp.sum(diag, axis=0, keepdims=True)
        dist = n_col + n_row - 2.0 * gram
        f_ref[at, :] = dist[0:128, 128:256]
        fwd_ref[at, :] = dist[128:256, 0:128]
        fresh = (flag_cols[:, b : b + 1] + flags[b : b + 1, :]) > 0
        a_ref[at, :] = jnp.where(fresh & off_diag, dist[128:256, 128:256], FAR)

    def take(ref, g):
        return [ref[pl.ds(g * K + t, 8, stride=128), :] for t in range(K)]

    best = sort_list(take(f_ref, 0))

    def more(ref, lo, best):
        def body(g, best):
            return tuple(merge_lists(list(best), sort_list(take(ref, g))))

        return lax.fori_loop(lo, 128 // K, body, tuple(best))

    best = more(f_ref, 1, best)
    best = more(a_ref, 0, best)

    for k in range(K):
        t_ref[k * 8 : (k + 1) * 8, :] = jnp.floor(jnp.clip(best[k] * SCALE + 0.5, 0.0, TOP))
    octet = lax.shift_right_logical(iota((128, 128), 0), 4)
    groups = iota((chips * 2, 128), 0)
    for b in range(blocks):
        at = slice(b * 128, (b + 1) * 128)
        slot = slot_ref[b : b + 1, :]
        code = t_ref[pl.ds(b, K, stride=8), :]
        hi = jnp.floor(code * (1.0 / 256.0))
        lo = code - hi * 256.0
        mine = (slot & 7) == octet
        for i, piece in enumerate((hi[:16], lo[:16], hi[16:], lo[16:])):
            pay_ref[i * 128 : (i + 1) * 128, at] = jnp.where(mine, jnp.concatenate([piece] * 8, axis=0), 0.0).astype(BF16)
        hot_ref[:, at] = onehot(lax.shift_right_logical(slot, 3) == groups)
    sums = dot(hot_ref[...], pay_ref[...], NT)
    low = (sums[:, 0:128] * 256.0 + sums[:, 128:256]).astype(I32)
    high = (sums[:, 256:384] * 256.0 + sums[:, 384:512]).astype(I32)
    words = low + lax.shift_left(high, 16)
    for n in range(chips):
        w2_ref[n] = words[2 * n : 2 * n + 2, :]
    for dz, device in column_peers(here):
        src = w2_ref.at[pl.ds(wrap(z + dz, NZ) * PLANE, PLANE)]
        remote(src, d2_ref.at[far_rank(-dz)], col_send2, col_recv2, device).start()
    stay = pltpu.make_async_copy(w2_ref.at[pl.ds(z * PLANE, PLANE)], d2_ref.at[far_rank(0)], own_sem)
    stay.start()
    near(fwd_ref, cur_ref, near_ref, s_ref)
    stay.wait()
    drain(d2_ref.at[pl.ds(1, NZ - 1)], col_recv2)
    for dy, dx, h, device in plane_peers(here):
        cell = wrap(y + dy, NY) * NX + wrap(x + dx, NX)
        dst = back_ref.at[h, plane_rank(-dy, -dx)]
        remote(d2_ref.at[:, cell], dst, plane_send2.at[h], plane_recv2.at[h], device).start()
    stay = pltpu.make_async_copy(d2_ref.at[:, y * NX + x], back_ref.at[0, 0], own_sem)
    stay.start()
    drain(d_ref.at[column], col_send)
    drain(fin_ref.at[plane], plane_send)
    drain(served_ref.at[pl.ds(0, chips - 1)], out_send)
    drain(d2_ref.at[pl.ds(1, NZ - 1)], col_send2)
    stay.wait()
    drain(back_ref.at[0, pl.ds(1, PLANE - 1)], plane_recv2.at[0])
    drain(back_ref.at[1], plane_recv2.at[1])
    drain(back_ref.at[0, pl.ds(1, PLANE - 1)], plane_send2.at[0])
    drain(back_ref.at[1], plane_send2.at[1])


def one_round(candidates, flags, embeddings, current, chips):
    rows_dev, width = embeddings.shape
    nrow = 2 * CAP
    vmem = pl.BlockSpec(memory_space=pltpu.VMEM)
    hbm = pl.BlockSpec(memory_space=pltpu.HBM)
    grid = pltpu.VMEM((chips, 128), I32)
    block = pltpu.VMEM((rows_dev, 128), F32)
    dma = pltpu.SemaphoreType.DMA
    return pl.pallas_call(
        round_kernel,
        in_specs=[hbm] * 4,
        out_specs=[vmem] * 9,
        out_shape=(
            jax.ShapeDtypeStruct((2, PLANE, NZ, 2, 128), I32),
            jax.ShapeDtypeStruct((K * 8, 128), F32),
            jax.ShapeDtypeStruct((nrow, 128), I32),
            jax.ShapeDtypeStruct((PITCH, 128), I32),
            jax.ShapeDtypeStruct((8, 128), F32),
            jax.ShapeDtypeStruct((READY * STEP, nrow * 32), BF16),
            jax.ShapeDtypeStruct((rows_dev, 128), I32),
            jax.ShapeDtypeStruct((rows_dev, READY * STEP), BF16),
            jax.ShapeDtypeStruct((16, 128), F32),
        ),
        scratch_shapes=[
            pltpu.VMEM(candidates.shape, I32),
            pltpu.VMEM(candidates.shape, I32),
            pltpu.VMEM(current.shape, F32),
            pltpu.VMEM(candidates.shape, I32),
            pltpu.VMEM((2 * rows_dev, width), BF16),
            pltpu.VMEM((chips, CAP, width), BF16),
            pltpu.VMEM((chips, CAP, width), BF16),
            grid, grid, grid,
            pltpu.VMEM((2 * chips, 128), I32),
            pltpu.VMEM((nrow, 128), I32),
            pltpu.VMEM((nrow, 128), I32),
            pltpu.VMEM((128, nrow), I32),
            pltpu.VMEM((nrow * 8, 128), F32),
            pltpu.VMEM((rows_dev, 128), I32),
            pltpu.VMEM((rows_dev, width), F32),
            pltpu.VMEM((256, width), BF16),
            block, block, block,
            pltpu.VMEM((K * 8, 128), F32),
            pltpu.VMEM((chips * 2, rows_dev), BF16),
            pltpu.VMEM((512, rows_dev), BF16),
            pltpu.VMEM((chips, 2, 128), I32),
            pltpu.VMEM((NZ, PLANE, 2, 128), I32),
            pltpu.VMEM((rows_dev // 128 * K, 128), F32),
            dma((4,)), dma, dma, dma, dma, dma, dma, dma, dma,
            dma, dma((PLANE,)), dma, dma, dma, dma((2,)), dma((2,)),
        ],
        compiler_params=pltpu.CompilerParams(
            collective_id=0, has_side_effects=True, vmem_limit_bytes=34 << 20
        ),
        name="one_round",
    )(*[pltpu.with_memory_space_constraint(v, pltpu.HBM) for v in (candidates, flags, embeddings, current)])


def merge_kernel(
    back_ref, near_ref, pos_ref, row_ref, info_ref, q_ref, start_ref, hit_ref, quad_ref,
    out_ref, pay_ref, s_ref, x_ref, acc_ref, hot_ref,
):
    rows_dev = out_ref.shape[1]
    chips = back_ref.shape[1]
    lanes = iota((chips, 128), 1)
    first = (lanes & 16) == 0
    total = jnp.max(info_ref[0:1, :]).astype(I32)
    most = jnp.max(info_ref[1:2, :]).astype(I32)
    for h in range(2):
        for rr in range(2):
            words = back_ref[h, :, rr, :]
            low = (words & 65535).astype(F32)
            high = lax.shift_right_logical(words, 16).astype(F32)
            even = jnp.where(first, low, pltpu.roll(high, 16, 1))
            odd = jnp.where(first, pltpu.roll(low, 112, 1), high)
            for parity, codes in enumerate((even, odd)):
                n = (h * 4 + rr * 2 + parity) * chips
                hi, mid = split2(codes)
                pay_ref[n : n + chips, 0:128] = hi
                pay_ref[n : n + chips, 128:256] = mid
    steps = (total + STEP - 1) // STEP

    def place_rows(at, turned, quad):
        parts = [turned[u * K : (u + 1) * K] for u in range(4)]
        if quad is not None:
            parts = [jnp.where(quad == float(u), part, 0.0) for u, part in enumerate(parts)]
        s_ref[pl.ds(at, K, stride=PITCH), :] = parts[0] + parts[1] + parts[2] + parts[3]

    def gather_more(t, carry):
        p = t * STEP + iota((STEP, 128), 0)
        quarter = lax.shift_right_logical(iota(pay_ref.shape, 1) & 127, 5)
        got = jnp.zeros((STEP, 256), F32)
        for u in range(4):
            rows = [slot_row(n, u) * 128 for n in range(8)]
            hot = jnp.concatenate([onehot(pos_ref[:, e : e + 128] == p) for e in rows], axis=1)
            pay = jnp.where(quarter == u, pay_ref[...].astype(F32), 0.0).astype(BF16)
            got = got + dot(hot, pay, NN)
        for i in range(STEP // 128):
            at = slice(i * 128, (i + 1) * 128)
            place_rows(t * (STEP // 128) + i, (got[at, 0:128] + got[at, 128:256]).T, None)
        return carry

    got = dot(q_ref[...], pay_ref[...], NN)
    for i in range(READY * STEP // 128):
        at = slice(i * 128, (i + 1) * 128)
        place_rows(i, (got[at, 0:128] + got[at, 128:256]).T, quad_ref[i : i + 1, :])
    lax.fori_loop(READY, steps, gather_more, 0)
    lane = iota((8, 128), 1)
    groups = (total + 1023) // 1024

    def ahead(ref, at, s):
        here = ref[pl.ds(at, 8), :]
        after = ref[pl.ds(at + 1, 8), :]
        return after if s == 128 else pltpu.roll(jnp.where(lane >= s, here, after), 128 - s, 1)

    for e in range(8):

        @pl.when(most > 1 << e)
        def _():
            def step(g, carry):
                at = pl.multiple_of(g * 8, 8)
                same = row_ref[pl.ds(at, 8), :] == ahead(row_ref, at, 1 << e)
                mins = []
                for k in range(K):
                    later = ahead(s_ref, (K - 1 - k) * PITCH + at, 1 << e)
                    mins.append(jnp.minimum(s_ref[pl.ds(k * PITCH + at, 8), :], jnp.where(same, later, FAR)))
                best = merge_low(mins)
                for k in range(K):
                    s_ref[pl.ds(k * PITCH + at, 8), :] = best[k]
                return carry

            lax.fori_loop(0, groups, step, 0)

    def listed(base, n):
        vals = jnp.concatenate([s_ref[pl.ds(base + i, K, stride=PITCH), :] for i in range(n)], axis=1)
        live = base * 128 + iota((K, n * 128), 1) < total
        hi, mid = split2(jnp.where(live, vals, 0.0))
        return jnp.concatenate([hi, mid, jnp.ones((K // 2, n * 128), BF16)], axis=0)

    acc_ref[...] = dot(listed(0, READY * STEP // 128), hit_ref[...], NT)

    def expand_more(t, carry):
        for i in range(STEP // 128):
            at = slice(i * 128, (i + 1) * 128)
            p = t * STEP + i * 128 + iota((rows_dev, 128), 1)
            hot_ref[:, at] = onehot(start_ref[...] == p)
        acc_ref[...] = acc_ref[...] + dot(listed(t * (STEP // 128), STEP // 128), hot_ref[...], NT)
        return carry

    lax.fori_loop(READY, steps, expand_more, 0)
    for b in range(rows_dev // 128):
        at = slice(b * 128, (b + 1) * 128)
        named = acc_ref[2 * K : 2 * K + 1, at] > 0.5
        x_ref[b * K : (b + 1) * K, :] = jnp.where(
            named, (acc_ref[0:K, at] + acc_ref[K : 2 * K, at]) * (1.0 / SCALE), FAR
        )
    have = near_ref[...]
    got = [x_ref[pl.ds(k, 8, stride=K), :] for k in range(K)]
    mins = [
        jnp.minimum(have[k * 8 : (k + 1) * 8, :], got[K - 1 - k])
        for k in range(K)
    ]
    best = merge_low(mins)
    for k in range(K):
        x_ref[k * 8 : (k + 1) * 8, :] = best[k]
    for b in range(rows_dev // 128):
        out_ref[:, b * 128 : (b + 1) * 128] = x_ref[pl.ds(b, K, stride=8), :]


def merge(back, best, pos, row, info, q, start, hit, quad):
    rows_dev = start.shape[0]
    vmem = pl.BlockSpec(memory_space=pltpu.VMEM)
    return pl.pallas_call(
        merge_kernel,
        in_specs=[vmem] * 9,
        out_specs=vmem,
        out_shape=jax.ShapeDtypeStruct((K, rows_dev), F32),
        scratch_shapes=[
            pltpu.VMEM((pos.shape[1] // 4, 256), BF16),
            pltpu.VMEM((K * PITCH, 128), F32),
            pltpu.VMEM((rows_dev // 128 * K, 128), F32),
            pltpu.VMEM((2 * K + K // 2, rows_dev), F32),
            pltpu.VMEM((rows_dev, STEP), BF16),
        ],
        compiler_params=pltpu.CompilerParams(vmem_limit_bytes=20 << 20),
        name="merge",
    )(back, best, pos, row, info, q, start, hit, quad)


def per_device(embeddings, candidates, fresh_flags, current):
    chips = lax.axis_size("rows")
    back, best, pos, row, info, q, start, hit, quad = one_round(
        candidates, fresh_flags, embeddings, current.T, chips
    )
    back = back.reshape(2, chips, 2, 128)
    return merge(back, best, pos.reshape(1, -1), row, info, q, start, hit, quad).T


def solution(mesh):
    spec = P(("rows", "sub"), None)
    return jax.shard_map(
        per_device, mesh=mesh, in_specs=(spec,) * 4, out_specs=spec, check_vma=False
    )
```

```python
import functools

import jax
import jax.numpy as jnp
from jax import lax
from jax.experimental import pallas as pl
from jax.experimental.pallas import tpu as pltpu
from jax.sharding import PartitionSpec as P

BLOCK = 128
CAP = 16
K = 32
FAR = 1.0e9
F32, BF16, I32 = jnp.float32, jnp.bfloat16, jnp.int32
NT = (((1,), (1,)), ((), ()))
NN = (((1,), (0,)), ((), ()))
PITCH = 40
NY, NZ, NX = 4, 8, 4
PLANE = NY * NX
AWAY = (0, 4, 3, 5, 2, 6, 1, 7)
STEP = 384
READY = 3
SCALE = 28672.0
TOP = 65535.0
MESH = pl.DeviceIdType.MESH


def dot(a, b, dims):
    return lax.dot_general(a, b, dims, preferred_element_type=F32)


def sort_pairs(n):
    pairs = []
    p = 1
    while p < n:
        k = p
        while k >= 1:
            for j in range(k % p, n - k, 2 * k):
                for i in range(min(k, n - j - k)):
                    if (i + j) // (2 * p) == (i + j + k) // (2 * p):
                        pairs.append((i + j, i + j + k))
            k //= 2
        p *= 2
    return pairs


SORT = sort_pairs(K)


def exchange(v, i, j):
    v[i], v[j] = jnp.minimum(v[i], v[j]), jnp.maximum(v[i], v[j])


def sort_list(values):
    v = list(values)
    for i, j in SORT:
        exchange(v, i, j)
    return v


def merge_low(mins):
    v = list(mins)
    d = K // 2
    while d >= 1:
        for i in range(K):
            if i & d == 0:
                exchange(v, i, i + d)
        d //= 2
    return v


def merge_lists(a, b):
    return merge_low([jnp.minimum(a[i], b[K - 1 - i]) for i in range(K)])


def split2(x):
    hi = x.astype(BF16)
    mid = (x - hi.astype(F32)).astype(BF16)
    return hi, mid


def iota(shape, dim):
    return lax.broadcasted_iota(I32, shape, dim)


def onehot(mask):
    return jnp.where(mask, 1.0, 0.0).astype(BF16)


def place():
    chip = lax.axis_index("rows")
    return lax.div(chip, NZ * NX), lax.rem(lax.div(chip, NX), NZ), lax.rem(chip, NX), lax.axis_index("sub")


def wrap(v, n):
    return jnp.where(v >= n, v - n, v)


def chip_at(y, z, x):
    return (wrap(y, NY) * NZ + wrap(z, NZ)) * NX + wrap(x, NX)


def column_peers(here):
    y, z, x, side = here
    return [(dz, {"rows": chip_at(y, z + dz, x), "sub": side}) for dz in AWAY[1:]]


def plane_peers(here, cores=2):
    y, z, x, side = here
    return [
        (dy, dx, h, {"rows": chip_at(y + dy, z, x + dx), "sub": 1 - side if h else side})
        for dy in range(NY)
        for dx in range(NX)
        for h in range(cores)
        if dy + dx + h > 0
    ]


def greet(here):
    y, z, x, side = here
    sem = pltpu.get_barrier_semaphore()
    peers = [p[-1] for p in column_peers(here)] + [p[-1] for p in plane_peers(here, 1)]
    peers.append({"rows": chip_at(y, z, x), "sub": 1 - side})
    for device in peers:
        pl.semaphore_signal(sem, inc=1, device_id=device, device_id_type=MESH)
    return lambda: pl.semaphore_wait(sem, len(peers))


def drain(ref, sem):
    pltpu.make_async_copy(ref, ref, sem).wait()


def remote(src, dst, send, recv, device):
    return pltpu.make_async_remote_copy(
        src_ref=src, dst_ref=dst, send_sem=send, recv_sem=recv, device_id=device, device_id_type=MESH
    )


def far_rank(dz):
    return AWAY.index(dz % NZ)


def plane_rank(dy, dx):
    return (dy % NY) * NX + dx % NX


def slots_of(c_ref, w_ref, s_ref, span_bits):
    blocks, n = c_ref.shape
    chips = w_ref.shape[0]
    owners = iota((chips, n), 0)
    before = onehot(iota((n, n), 0) < iota((n, n), 1))
    ranks = iota((CAP, n), 0)
    run = jnp.zeros((chips, 1), F32)
    acc = jnp.zeros((chips, 2 * CAP), F32)
    for b in range(blocks):
        c = c_ref[b : b + 1, :]
        chip = lax.shift_right_logical(c, span_bits)
        owner = (chip & 28) * 4 + lax.shift_right_logical(chip, 5) * 4 + (chip & 3)
        row1 = (c & ((1 << span_bits) - 1)) + 1
        mine = owner == owners
        mine_b = onehot(mine)
        pre = dot(mine_b, before, NN) + run
        rank = jnp.sum(jnp.where(mine, pre, 0.0), axis=0, keepdims=True).astype(I32)
        run = run + jnp.sum(jnp.where(mine, 1.0, 0.0), axis=1, keepdims=True)
        s_ref[b : b + 1, :] = owner * CAP + rank
        sel = ranks == rank
        hi = jnp.where(sel, lax.shift_right_logical(row1, 4).astype(F32), 0.0).astype(BF16)
        lo = jnp.where(sel, (row1 & 15).astype(F32), 0.0).astype(BF16)
        acc = acc + dot(mine_b, jnp.concatenate([hi, lo], axis=0), NT)
    wanted = (acc[:, :CAP] * 16.0 + acc[:, CAP:]).astype(I32) - 1
    w_ref[...] = jnp.concatenate([wanted] + [jnp.full((chips, CAP), -1, I32)] * (128 // CAP - 1), axis=1)


def plan_way_back(a, pos_ref, row_ref, start_ref, info_ref, key_ref, lv_ref, col_ref, acc_ref, end_ref):
    rows_dev = start_ref.shape[0]
    nrow = a.shape[0]
    slots = nrow * 128
    live = (a >= 0) & (a < rows_dev)
    sid = iota((nrow, 128), 0) * 128 + iota((nrow, 128), 1)
    key = jnp.where(live, a * slots + sid, (1 << 30) + sid)
    key_ref[...] = key
    lv_ref[...] = jnp.where(live, a, rows_dev)
    for h in range(nrow // 8):
        col_ref[:, h * 8 : (h + 1) * 8] = key[h * 8 : (h + 1) * 8, :].T
    acc_ref[...] = jnp.zeros_like(acc_ref)
    lane = iota((128, nrow), 1)

    def outer(c, carry):
        col = jnp.sum(jnp.where(lane == c, col_ref[...], 0), axis=1, keepdims=True)
        colb = jnp.broadcast_to(col, (128, 128))

        def inner(e, carry):
            less = jnp.where(colb < key_ref[pl.ds(e, 1), :], 1.0, 0.0)
            part = jnp.sum(less.reshape(16, 8, 128), axis=0)
            at = pl.ds(pl.multiple_of(e * 8, 8), 8)
            acc_ref[at, :] = acc_ref[at, :] + part
            return carry

        return lax.fori_loop(0, nrow, inner, carry)

    lax.fori_loop(0, nrow, outer, 0)
    for e in range(nrow):
        pos_ref[e : e + 1, :] = jnp.sum(acc_ref[e * 8 : (e + 1) * 8, :], axis=0, keepdims=True).astype(I32)

    def start_of(g, most):
        v = g * 128 + iota((128, 128), 0)
        low = jnp.zeros((128, 128), F32)
        own = jnp.zeros((128, 128), F32)
        for e in range(nrow):
            lv = lv_ref[e : e + 1, :]
            low = low + jnp.where(lv < v, 1.0, 0.0)
            own = own + jnp.where(lv == v, 1.0, 0.0)
        start = jnp.sum(low, axis=1, keepdims=True)
        count = jnp.sum(own, axis=1, keepdims=True)
        at = pl.ds(pl.multiple_of(g * 128, 128), 128)
        end_ref[at, :] = jnp.broadcast_to((start + count).astype(I32), (128, 128))
        start_ref[at, :] = jnp.broadcast_to(jnp.where(count > 0, start, -1.0).astype(I32), (128, 128))
        return jnp.maximum(most, count)

    most = lax.fori_loop(0, rows_dev // 128, start_of, jnp.zeros((128, 1), F32))
    total = jnp.sum(jnp.where(live, 1.0, 0.0), axis=(0, 1), keepdims=True).astype(I32)
    most = jnp.max(most, axis=0, keepdims=True).astype(I32)
    info_ref[...] = jnp.where(iota((8, 128), 0) == 0, total, most).astype(F32)
    row_ref[...] = jnp.full(row_ref.shape, rows_dev, I32)

    def row_of(c, carry):
        p = c * 128 + iota((8, 128), 1)
        acc = jnp.zeros((8, 128), F32)
        for g in range(rows_dev // 8):
            acc = acc + jnp.where(end_ref[g * 8 : (g + 1) * 8, :] <= p, 1.0, 0.0)
        row = jnp.sum(acc, axis=0, keepdims=True).astype(I32)
        row_ref[pl.ds(c, 1), :] = jnp.where(p[0:1, :] < total, row, rows_dev)
        return carry

    lax.fori_loop(0, nrow, row_of, 0)


def near(fwd_ref, cur_ref, out_ref, s_ref):
    for b in range(cur_ref.shape[1] // 128):
        s_ref[b * K : (b + 1) * K, :] = cur_ref[:, b * 128 : (b + 1) * 128]
    best = sort_list([s_ref[pl.ds(k, 8, stride=K), :] for k in range(K)])

    def body(g, best):
        more = [fwd_ref[pl.ds(g * K + t, 8, stride=128), :] for t in range(K)]
        return tuple(merge_lists(list(best), sort_list(more)))

    best = lax.fori_loop(0, 128 // K, body, tuple(best))
    for k in range(K):
        out_ref[k * 8 : (k + 1) * 8, :] = best[k]


def slot_row(n, u):
    return n // 4 * CAP + n // 2 % 2 * 8 + 2 * u + n % 2


def round_kernel(
    cand_hbm, flag_hbm, emb_hbm, cur_hbm,
    back_ref, near_ref, pos_ref, row_ref, info_ref, q_ref, start_ref, hit_ref, quad_ref,
    c_ref, flag_ref, cur_ref, slot_ref,
    rows_ref, served_ref, pulled_ref, w_ref, d_ref, e_ref, fin_ref,
    key_ref, lv_ref, col_ref, acc_ref, end_ref,
    cand_ref, z_ref, f_ref, a_ref, fwd_ref, t_ref, hot_ref, pay_ref, w2_ref, d2_ref, e2_ref, s_ref,
    in_sem, half_send, half_recv, col_send, col_recv, plane_send, plane_recv, tell_send, tell_recv,
    out_send, out_recv, own_sem, col_send2, col_recv2, plane_send2, plane_recv2,
):
    here = place()
    y, z, x, side = here
    rows_dev = emb_hbm.shape[0]
    span = rows_ref.shape[0]
    chips = pulled_ref.shape[0]
    half_at = pl.multiple_of(side * rows_dev, rows_dev)
    my_half = rows_ref.at[pl.ds(half_at, rows_dev)]
    brought = [
        pltpu.make_async_copy(src, dst, in_sem.at[i])
        for i, (src, dst) in enumerate(
            [(cand_hbm, c_ref), (emb_hbm, my_half), (flag_hbm, flag_ref), (cur_hbm, cur_ref)]
        )
    ]
    for copy in brought:
        copy.start()
    wait_for_peers = greet(here)
    brought[0].wait()
    slots_of(c_ref, w_ref, slot_ref, span.bit_length() - 1)
    wait_for_peers()
    other = {"rows": chip_at(y, z, x), "sub": 1 - side}
    half = remote(emb_hbm, my_half, half_send, half_recv, other)
    half.start()

    for dz, device in column_peers(here):
        src = w_ref.at[pl.ds(pl.multiple_of(wrap(z + dz, NZ) * PLANE, PLANE), PLANE)]
        dst = d_ref.at[pl.ds(far_rank(-dz) * PLANE, PLANE)]
        remote(src, dst, col_send, col_recv, device).start()
    own = pl.ds(pl.multiple_of(z * PLANE, PLANE), PLANE)
    d_ref[far_rank(0) * PLANE : (far_rank(0) + 1) * PLANE, :] = w_ref[own, :]
    column = pl.ds(0, (NZ - 1) * PLANE)
    drain(d_ref.at[column], col_recv)
    for dy, dx, _, device in plane_peers(here, 1):
        i = plane_rank(dy, dx)
        cell = wrap(y + dy, NY) * NX + wrap(x + dx, NX)
        e_ref[i * NZ : (i + 1) * NZ, :] = d_ref[pl.ds(cell, NZ, stride=PLANE), :]
        dst = fin_ref.at[pl.ds(plane_rank(-dy, -dx) * NZ, NZ)]
        remote(e_ref.at[pl.ds(i * NZ, NZ)], dst, plane_send, plane_recv, device).start()
    fin_ref[0:NZ, :] = d_ref[pl.ds(y * NX + x, NZ, stride=PLANE), :]
    plane = pl.ds(0, (PLANE - 1) * NZ)
    for copy in brought[1:]:
        copy.wait()
    half.wait()

    spread = iota((128, 128), 1) == (iota((128, 128), 0) & (CAP - 1))
    ids = iota((128, span), 1)
    me = (y * NX + x) * NZ + z

    def serve(c, carry):
        asked = fin_ref[0:NZ, :] if isinstance(c, int) else fin_ref[pl.ds(pl.multiple_of(c * NZ, NZ), NZ), :]
        wide = jnp.concatenate([jnp.broadcast_to(asked[j : j + 1, :], (CAP, 128)) for j in range(NZ)], axis=0)
        col = jnp.sum(jnp.where(spread, wide, 0), axis=1, keepdims=True)
        got = dot(onehot(col == ids), rows_ref[...], NN).astype(BF16)
        for j in range(NZ):
            served_ref[c * NZ + j] = got[j * CAP : (j + 1) * CAP, :]
        y_to = wrap(y + c // NX, NY)
        x_to = wrap(x + c % NX, NX)

        def send(j):
            device = {"rows": (y_to * NZ + wrap(z + AWAY[j], NZ)) * NX + x_to, "sub": side}
            remote(served_ref.at[c * NZ + j], pulled_ref.at[me], out_send, out_recv.at[c], device).start()

        if isinstance(c, int):
            assert c == 0
        else:
            send(0)
        for j in range(1, NZ):
            send(j)
        return carry

    serve(0, 0)
    drain(fin_ref.at[plane], plane_recv)
    tell = remote(fin_ref.at[pl.ds(0, chips)], fin_ref.at[pl.ds(chips, chips)], tell_send, tell_recv, other)
    tell.start()

    lax.fori_loop(1, PLANE, serve, 0)
    stay = pltpu.make_async_copy(served_ref.at[0], pulled_ref.at[me], own_sem)
    stay.start()

    tell.wait()
    turned = [fin_ref[h * chips : (h + 1) * chips, :].T[0:CAP, :] for h in range(2)]
    plan_way_back(
        jnp.concatenate(turned, axis=0) - side * rows_dev,
        pos_ref, row_ref, start_ref, info_ref, key_ref, lv_ref, col_ref, acc_ref, end_ref,
    )

    def ready(t, carry):
        p = iota((128, 128), 0) + t * 128
        at = pl.ds(pl.multiple_of(t * 128, 128), 128)
        quad = jnp.zeros((128, 128), F32)
        for n in range(8):
            found = jnp.zeros((128, 128), F32)
            for u in range(4):
                e = slot_row(n, u)
                hit = jnp.where(pos_ref[e : e + 1, :] == p, 1.0, 0.0)
                found = found + hit
                quad = quad + hit * float(u)
            q_ref[at, n * 128 : (n + 1) * 128] = found.astype(BF16)
        quad_ref[pl.ds(t, 1), :] = jnp.sum(quad.T, axis=0, keepdims=True)
        return carry

    lax.fori_loop(0, READY * STEP // 128, ready, 0)
    for i in range(READY * STEP // 128):
        hit_ref[:, i * 128 : (i + 1) * 128] = onehot(start_ref[...] == iota((rows_dev, 128), 1) + i * 128)

    slots = slot_ref[...]
    column_id = lax.shift_right_logical(slots, 4) & (PLANE - 1)
    in_column = lax.shift_right_logical(slots, 8) * CAP + (slots & (CAP - 1))
    column_cols = column_id.T
    in_cols = in_column.T
    blocks = slot_ref.shape[0]
    size = NZ * CAP
    cells = iota((128, 2 * size), 1)

    def source(c):
        y_from = wrap(y + NY - lax.div(c, NX), NY)
        return y_from * NX + wrap(x + NX - lax.rem(c, NX), NX)

    def arrived(c, count):
        drain(pulled_ref.at[pl.ds(0, count)], out_recv.at[c])

    def column_rows(c):
        return pulled_ref[pl.ds(source(c) * NZ, NZ)].reshape(size, -1)

    def picked(b, c, rows):
        here, there = source(c), source(c + 1)
        col, at = column_cols[:, b : b + 1], in_cols[:, b : b + 1]
        at = jnp.where(col == here, at, jnp.where(col == there, at + size, -1))
        return dot(onehot(at == cells), rows, NN)

    def two_columns(c):
        return jnp.concatenate([column_rows(c), column_rows(c + 1)], axis=0)

    stay.wait()
    arrived(0, NZ - 1)
    arrived(1, NZ)
    rows = two_columns(0)
    for b in range(blocks):
        cand_ref[b * 128 : (b + 1) * 128, :] = picked(b, 0, rows)

    def more_rows(k, carry):
        arrived(2 * k, NZ)
        arrived(2 * k + 1, NZ)
        rows = two_columns(2 * k)
        for b in range(blocks):
            at = slice(b * 128, (b + 1) * 128)
            cand_ref[at, :] = cand_ref[at, :] + picked(b, 2 * k, rows)
        return carry

    lax.fori_loop(1, PLANE // 2 - 1, more_rows, 0)
    last = PLANE - 2
    arrived(last, NZ)
    arrived(last + 1, NZ)
    rows = two_columns(last)

    flags = flag_ref[...]
    flag_cols = flags.T
    eye = iota((256, 256), 0) == iota((256, 256), 1)
    off_diag = iota((128, 128), 0) != iota((128, 128), 1)
    for b in range(blocks):
        at = slice(b * 128, (b + 1) * 128)
        z_ref[0:128, :] = rows_ref[pl.ds(half_at + b * 128, 128), :]
        z_ref[128:256, :] = (cand_ref[at, :] + picked(b, last, rows)).astype(BF16)
        both = z_ref[...]
        gram = dot(both, both, NT)
        diag = jnp.where(eye, gram, 0.0)
        n_col = jnp.sum(diag, axis=1, keepdims=True)
        n_row = jnp.sum(diag, axis=0, keepdims=True)
        dist = n_col + n_row - 2.0 * gram
        f_ref[at, :] = dist[0:128, 128:256]
        fwd_ref[at, :] = dist[128:256, 0:128]
        fresh = (flag_cols[:, b : b + 1] + flags[b : b + 1, :]) > 0
        a_ref[at, :] = jnp.where(fresh & off_diag, dist[128:256, 128:256], FAR)

    def take(ref, g):
        return [ref[pl.ds(g * K + t, 8, stride=128), :] for t in range(K)]

    best = sort_list(take(f_ref, 0))

    def more(ref, lo, best):
        def body(g, best):
            return tuple(merge_lists(list(best), sort_list(take(ref, g))))

        return lax.fori_loop(lo, 128 // K, body, tuple(best))

    best = more(f_ref, 1, best)
    best = more(a_ref, 0, best)

    for k in range(K):
        t_ref[k * 8 : (k + 1) * 8, :] = jnp.floor(jnp.clip(best[k] * SCALE + 0.5, 0.0, TOP))
    octet = lax.shift_right_logical(iota((128, 128), 0), 4)
    groups = iota((chips * 2, 128), 0)
    for b in range(blocks):
        at = slice(b * 128, (b + 1) * 128)
        slot = slot_ref[b : b + 1, :]
        code = t_ref[pl.ds(b, K, stride=8), :]
        hi = jnp.floor(code * (1.0 / 256.0))
        lo = code - hi * 256.0
        mine = (slot & 7) == octet
        for i, piece in enumerate((hi[:16], lo[:16], hi[16:], lo[16:])):
            pay_ref[i * 128 : (i + 1) * 128, at] = jnp.where(mine, jnp.concatenate([piece] * 8, axis=0), 0.0).astype(BF16)
        hot_ref[:, at] = onehot(lax.shift_right_logical(slot, 3) == groups)
    sums = dot(hot_ref[...], pay_ref[...], NT)
    low = (sums[:, 0:128] * 256.0 + sums[:, 128:256]).astype(I32)
    high = (sums[:, 256:384] * 256.0 + sums[:, 384:512]).astype(I32)
    words = low + lax.shift_left(high, 16)
    for n in range(chips):
        w2_ref[n] = words[2 * n : 2 * n + 2, :]
    for dz, device in column_peers(here):
        src = w2_ref.at[pl.ds(wrap(z + dz, NZ) * PLANE, PLANE)]
        remote(src, d2_ref.at[far_rank(-dz)], col_send2, col_recv2, device).start()
    stay = pltpu.make_async_copy(w2_ref.at[pl.ds(z * PLANE, PLANE)], d2_ref.at[far_rank(0)], own_sem)
    stay.start()
    near(fwd_ref, cur_ref, near_ref, s_ref)
    stay.wait()
    drain(d2_ref.at[pl.ds(1, NZ - 1)], col_recv2)
    for k in range(NZ):
        e2_ref[:, k] = d2_ref[k]
    for dy, dx, h, device in plane_peers(here):
        cell = wrap(y + dy, NY) * NX + wrap(x + dx, NX)
        dst = back_ref.at[h, plane_rank(-dy, -dx)]
        remote(e2_ref.at[cell], dst, plane_send2.at[h], plane_recv2.at[h], device).start()
    stay = pltpu.make_async_copy(e2_ref.at[y * NX + x], back_ref.at[0, 0], own_sem)
    stay.start()
    drain(d_ref.at[column], col_send)
    drain(fin_ref.at[plane], plane_send)
    drain(served_ref.at[pl.ds(0, chips - 1)], out_send)
    drain(d2_ref.at[pl.ds(1, NZ - 1)], col_send2)
    stay.wait()
    drain(back_ref.at[0, pl.ds(1, PLANE - 1)], plane_recv2.at[0])
    drain(back_ref.at[1], plane_recv2.at[1])
    drain(back_ref.at[0, pl.ds(1, PLANE - 1)], plane_send2.at[0])
    drain(back_ref.at[1], plane_send2.at[1])


def one_round(candidates, flags, embeddings, current, chips):
    rows_dev, width = embeddings.shape
    nrow = 2 * CAP
    vmem = pl.BlockSpec(memory_space=pltpu.VMEM)
    hbm = pl.BlockSpec(memory_space=pltpu.HBM)
    grid = pltpu.VMEM((chips, 128), I32)
    block = pltpu.VMEM((rows_dev, 128), F32)
    dma = pltpu.SemaphoreType.DMA
    return pl.pallas_call(
        round_kernel,
        in_specs=[hbm] * 4,
        out_specs=[vmem] * 9,
        out_shape=(
            jax.ShapeDtypeStruct((2, PLANE, NZ, 2, 128), I32),
            jax.ShapeDtypeStruct((K * 8, 128), F32),
            jax.ShapeDtypeStruct((nrow, 128), I32),
            jax.ShapeDtypeStruct((PITCH, 128), I32),
            jax.ShapeDtypeStruct((8, 128), F32),
            jax.ShapeDtypeStruct((READY * STEP, nrow * 32), BF16),
            jax.ShapeDtypeStruct((rows_dev, 128), I32),
            jax.ShapeDtypeStruct((rows_dev, READY * STEP), BF16),
            jax.ShapeDtypeStruct((16, 128), F32),
        ),
        scratch_shapes=[
            pltpu.VMEM(candidates.shape, I32),
            pltpu.VMEM(candidates.shape, I32),
            pltpu.VMEM(current.shape, F32),
            pltpu.VMEM(candidates.shape, I32),
            pltpu.VMEM((2 * rows_dev, width), BF16),
            pltpu.VMEM((chips, CAP, width), BF16),
            pltpu.VMEM((chips, CAP, width), BF16),
            grid, grid, grid,
            pltpu.VMEM((2 * chips, 128), I32),
            pltpu.VMEM((nrow, 128), I32),
            pltpu.VMEM((nrow, 128), I32),
            pltpu.VMEM((128, nrow), I32),
            pltpu.VMEM((nrow * 8, 128), F32),
            pltpu.VMEM((rows_dev, 128), I32),
            pltpu.VMEM((rows_dev, width), F32),
            pltpu.VMEM((256, width), BF16),
            block, block, block,
            pltpu.VMEM((K * 8, 128), F32),
            pltpu.VMEM((chips * 2, rows_dev), BF16),
            pltpu.VMEM((512, rows_dev), BF16),
            pltpu.VMEM((chips, 2, 128), I32),
            pltpu.VMEM((NZ, PLANE, 2, 128), I32),
            pltpu.VMEM((PLANE, NZ, 2, 128), I32),
            pltpu.VMEM((rows_dev // 128 * K, 128), F32),
            dma((4,)), dma, dma, dma, dma, dma, dma, dma, dma,
            dma, dma((PLANE,)), dma, dma, dma, dma((2,)), dma((2,)),
        ],
        compiler_params=pltpu.CompilerParams(
            collective_id=0, has_side_effects=True, vmem_limit_bytes=34 << 20
        ),
        name="one_round",
    )(*[pltpu.with_memory_space_constraint(v, pltpu.HBM) for v in (candidates, flags, embeddings, current)])


def merge_kernel(
    back_ref, near_ref, pos_ref, row_ref, info_ref, q_ref, start_ref, hit_ref, quad_ref,
    out_ref, pay_ref, s_ref, x_ref, acc_ref, hot_ref,
):
    rows_dev = out_ref.shape[1]
    chips = back_ref.shape[1]
    lanes = iota((chips, 128), 1)
    first = (lanes & 16) == 0
    total = jnp.max(info_ref[0:1, :]).astype(I32)
    most = jnp.max(info_ref[1:2, :]).astype(I32)
    for h in range(2):
        for rr in range(2):
            words = back_ref[h, :, rr, :]
            low = (words & 65535).astype(F32)
            high = lax.shift_right_logical(words, 16).astype(F32)
            even = jnp.where(first, low, pltpu.roll(high, 16, 1))
            odd = jnp.where(first, pltpu.roll(low, 112, 1), high)
            for parity, codes in enumerate((even, odd)):
                n = (h * 4 + rr * 2 + parity) * chips
                hi, mid = split2(codes)
                pay_ref[n : n + chips, 0:128] = hi
                pay_ref[n : n + chips, 128:256] = mid
    steps = (total + STEP - 1) // STEP

    def place_rows(at, turned, quad):
        parts = [turned[u * K : (u + 1) * K] for u in range(4)]
        if quad is not None:
            parts = [jnp.where(quad == float(u), part, 0.0) for u, part in enumerate(parts)]
        s_ref[pl.ds(at, K, stride=PITCH), :] = parts[0] + parts[1] + parts[2] + parts[3]

    def gather_more(t, carry):
        p = t * STEP + iota((STEP, 128), 0)
        quarter = lax.shift_right_logical(iota(pay_ref.shape, 1) & 127, 5)
        got = jnp.zeros((STEP, 256), F32)
        for u in range(4):
            rows = [slot_row(n, u) * 128 for n in range(8)]
            hot = jnp.concatenate([onehot(pos_ref[:, e : e + 128] == p) for e in rows], axis=1)
            pay = jnp.where(quarter == u, pay_ref[...].astype(F32), 0.0).astype(BF16)
            got = got + dot(hot, pay, NN)
        for i in range(STEP // 128):
            at = slice(i * 128, (i + 1) * 128)
            place_rows(t * (STEP // 128) + i, (got[at, 0:128] + got[at, 128:256]).T, None)
        return carry

    got = dot(q_ref[...], pay_ref[...], NN)
    for i in range(READY * STEP // 128):
        at = slice(i * 128, (i + 1) * 128)
        place_rows(i, (got[at, 0:128] + got[at, 128:256]).T, quad_ref[i : i + 1, :])
    lax.fori_loop(READY, steps, gather_more, 0)
    lane = iota((8, 128), 1)
    groups = (total + 1023) // 1024

    def ahead(ref, at, s):
        here = ref[pl.ds(at, 8), :]
        after = ref[pl.ds(at + 1, 8), :]
        return after if s == 128 else pltpu.roll(jnp.where(lane >= s, here, after), 128 - s, 1)

    for e in range(8):

        @pl.when(most > 1 << e)
        def _():
            def step(g, carry):
                at = pl.multiple_of(g * 8, 8)
                same = row_ref[pl.ds(at, 8), :] == ahead(row_ref, at, 1 << e)
                mins = []
                for k in range(K):
                    later = ahead(s_ref, (K - 1 - k) * PITCH + at, 1 << e)
                    mins.append(jnp.minimum(s_ref[pl.ds(k * PITCH + at, 8), :], jnp.where(same, later, FAR)))
                best = merge_low(mins)
                for k in range(K):
                    s_ref[pl.ds(k * PITCH + at, 8), :] = best[k]
                return carry

            lax.fori_loop(0, groups, step, 0)

    def listed(base, n):
        vals = jnp.concatenate([s_ref[pl.ds(base + i, K, stride=PITCH), :] for i in range(n)], axis=1)
        live = base * 128 + iota((K, n * 128), 1) < total
        hi, mid = split2(jnp.where(live, vals, 0.0))
        return jnp.concatenate([hi, mid, jnp.ones((K // 2, n * 128), BF16)], axis=0)

    acc_ref[...] = dot(listed(0, READY * STEP // 128), hit_ref[...], NT)

    def expand_more(t, carry):
        for i in range(STEP // 128):
            at = slice(i * 128, (i + 1) * 128)
            p = t * STEP + i * 128 + iota((rows_dev, 128), 1)
            hot_ref[:, at] = onehot(start_ref[...] == p)
        acc_ref[...] = acc_ref[...] + dot(listed(t * (STEP // 128), STEP // 128), hot_ref[...], NT)
        return carry

    lax.fori_loop(READY, steps, expand_more, 0)
    for b in range(rows_dev // 128):
        at = slice(b * 128, (b + 1) * 128)
        named = acc_ref[2 * K : 2 * K + 1, at] > 0.5
        x_ref[b * K : (b + 1) * K, :] = jnp.where(
            named, (acc_ref[0:K, at] + acc_ref[K : 2 * K, at]) * (1.0 / SCALE), FAR
        )
    have = near_ref[...]
    got = [x_ref[pl.ds(k, 8, stride=K), :] for k in range(K)]
    mins = [
        jnp.minimum(have[k * 8 : (k + 1) * 8, :], got[K - 1 - k])
        for k in range(K)
    ]
    best = merge_low(mins)
    for k in range(K):
        x_ref[k * 8 : (k + 1) * 8, :] = best[k]
    for b in range(rows_dev // 128):
        out_ref[:, b * 128 : (b + 1) * 128] = x_ref[pl.ds(b, K, stride=8), :]


def merge(back, best, pos, row, info, q, start, hit, quad):
    rows_dev = start.shape[0]
    vmem = pl.BlockSpec(memory_space=pltpu.VMEM)
    return pl.pallas_call(
        merge_kernel,
        in_specs=[vmem] * 9,
        out_specs=vmem,
        out_shape=jax.ShapeDtypeStruct((K, rows_dev), F32),
        scratch_shapes=[
            pltpu.VMEM((pos.shape[1] // 4, 256), BF16),
            pltpu.VMEM((K * PITCH, 128), F32),
            pltpu.VMEM((rows_dev // 128 * K, 128), F32),
            pltpu.VMEM((2 * K + K // 2, rows_dev), F32),
            pltpu.VMEM((rows_dev, STEP), BF16),
        ],
        compiler_params=pltpu.CompilerParams(vmem_limit_bytes=20 << 20),
        name="merge",
    )(back, best, pos, row, info, q, start, hit, quad)


def per_device(embeddings, candidates, fresh_flags, current):
    chips = lax.axis_size("rows")
    back, best, pos, row, info, q, start, hit, quad = one_round(
        candidates, fresh_flags, embeddings, current.T, chips
    )
    back = back.reshape(2, chips, 2, 128)
    return merge(back, best, pos.reshape(1, -1), row, info, q, start, hit, quad).T


def solution(mesh):
    spec = P(("rows", "sub"), None)
    return jax.shard_map(
        per_device, mesh=mesh, in_specs=(spec,) * 4, out_specs=spec, check_vma=False
    )
```
